256 devices in a mesh: shard: 64 (over z, y, core), rep: 4 (over x).
Axes of the slice: x: 4, y: 4, z: 8, core: 2. Of those that a mesh axis runs over, the one named last changes fastest.
Arguments:
- index_states: bfloat16 [65536, 768], P('shard'), may hold values from -6 to 6
- questions: bfloat16 [2048, 768], P(('shard', 'rep')), may hold values from -6 to 6
- reader_attention_scores: float32 [2048, 32], P(('shard', 'rep')), may hold values from -6 to 6
- owners: int32 [2048, 32, 1], P(('shard', 'rep')), may hold values from 0 to 63; in each aligned block of 256 rows (0 to 255, 256 to 511, ..., all dimensions but the last counted through in order) at most 8 rows name the same one
- passage_rows: int32 [2048, 32], P(('shard', 'rep')), may hold values from 0 to 1023
- w_up: bfloat16 [768, 3072], replicated, may hold values from -0.21875 to 0.21875
- final_lowering_matrix: bfloat16 [3072, 768], replicated, may hold values from -0.109375 to 0.109375
Outputs:
- ranking_logit_derivative: float32 [2048, 32], P(('shard', 'rep'))
- grad_up_t: float32 [3072, 768], P('shard')
- grad_down: float32 [3072, 768], P('shard')
The draws below stay inside these ranges and needn't reach their ends.
Inputs may be any that keep to these rules, and one draw needn't show every extreme that they name: `owners`: among the 256 retrieved passages of one device's questions (aligned blocks of 8 questions), at most 8 have the same owner; some owner has exactly 8.
All inputs are finite; a program needn't handle non-finite values.
Results may differ from the reference program's by a relative error of at most 0.0053.
Values may be sent and summed in bfloat16 or wider, within the bound.
No kernel may reach another device: no remote copies, remote signals or barrier semaphores. Data moves between devices by JAX's collectives and lax.ppermute only.
A program may use at most 128 MiB of HBM per device.

```python
import math
import jax
import jax.numpy as jnp
import numpy as np
from jax import lax

D = 768
FF = 3072
K = 32
Q_DEV = 8
PASS_DEV = 1024
CAP = 8
QUESTIONS = 2048
PASSAGES = 65536
N_SHARD = 64
N_REP = 4


def place_ends(drawn, key, low, largest):
    longest = drawn.shape.index(max(drawn.shape))
    spots = []
    for shift in (0, 1):
        where = [jax.random.randint(jax.random.fold_in(key, axis), (), 0, length) for axis, length in enumerate(drawn.shape)]
        where[longest] = (where[longest] + shift) % drawn.shape[longest]
        spots.append(tuple(where))
    return drawn.at[spots[0]].set(low).at[spots[1]].set(largest)


def level_of(own_key, dims, split, low, top_value):
    def one(axis_at, parts):
        heights = jax.random.uniform(jax.random.fold_in(jax.random.fold_in(own_key, 6), axis_at), (parts,), jnp.float32, low / len(split), top_value / len(split))
        return jnp.repeat(jnp.exp(heights), dims[axis_at] // parts).reshape((-1,) + (1,) * (len(dims) - axis_at - 1))

    loudness = one(*split[0])
    for cut in split[1:]:
        loudness = loudness * one(*cut)
    return loudness


def assign_block(stream_key, own, number, rows, amount, top, limit, lean):
    sequence = jax.random.permutation(stream_key, amount)
    heavy_load, ordinary = shares(amount, rows * top, limit, lean, True), shares(amount, rows * top, limit, lean, False)
    places = jnp.arange(amount)

    def named(tallies, turn):
        used = int((tallies > 0).sum())
        fixed = max(1, used // 4)
        passed = fixed + (places - fixed + turn * (used - fixed)) % max(1, amount - fixed)
        return jnp.zeros((amount,), jnp.int32).at[sequence[jnp.where(places < fixed, places, passed)]].set(jnp.asarray(tallies, jnp.int32))

    tallies = jnp.where(number % 4 == 0, named(heavy_load, number // 4), named(ordinary, number - number // 4 - 1))
    mixed = jax.random.permutation(jax.random.fold_in(own, 3), amount)
    giver, sink = mixed[0:amount // 2 * 2:2], mixed[1:amount // 2 * 2:2]
    slack = jnp.minimum(tallies[giver] - 1, limit - tallies[sink]) // 2
    slack = jnp.where((giver == sequence[0]) | (sink == sequence[0]) | (tallies[sink] == 0), 0, jnp.maximum(slack, 0))
    passed = jax.random.randint(jax.random.fold_in(own, 4), (amount // 2,), 0, 1 << 20) % (slack + 1)
    tallies = tallies.at[giver].add(-passed).at[sink].add(passed)
    labels = jnp.searchsorted(jnp.cumsum(tallies), jnp.arange(rows * top), side="right").astype(jnp.int32)
    listing = labels.reshape(top, rows).T
    listing = listing[jax.random.permutation(jax.random.fold_in(own, 1), rows)]
    turn = jax.random.randint(jax.random.fold_in(own, 2), (rows, 1), 0, top)
    return jnp.take_along_axis(listing, (jnp.arange(top)[None, :] + turn) % top, axis=1)


def shares(count, total, reach, skew, full):
    portions = [(1 << 20) // math.isqrt(standing ** skew) + 1 for standing in range(1, count + 1)]
    largest = reach if full else min(reach, max(-(-total // count), total * portions[0] // sum(portions)))
    least = 1 if total - largest >= count - 1 else 0
    holding, surplus = [largest] + [least] * (count - 1), total - largest - least * (count - 1)
    while surplus > 0:
        free = [i for i in range(1, count) if holding[i] < largest] or [i for i in range(1, count) if holding[i] < reach]
        mass, budget = sum([portions[i] for i in free]), surplus
        for i in free:
            extra = min(reach - holding[i], max(1, budget * portions[i] // mass), surplus)
            holding[i] = holding[i] + extra
            surplus = surplus - extra
    return np.array(holding)


def centred(stream_key, extent, width, limit, shards=(), held_as=jnp.bfloat16):
    entries = width * jax.random.normal(stream_key, extent, jnp.float32)
    if shards:
        entries = entries * level_of(stream_key, extent, shards, -0.22, 0.18)
    return jnp.clip(entries, -limit, limit).astype(held_as)


def setup_inputs(seed: int = 0) -> dict:
    seeds = jax.random.split(jax.random.key(seed), 8)
    index_states = centred(seeds[0], (PASSAGES, D), 1.0, 6.0, ((0, 64),))
    questions = centred(seeds[1], (QUESTIONS, D), 1.0, 6.0, ((0, 256),))
    reader_attention_scores = centred(seeds[2], (QUESTIONS, K), 1.5, 6.0, ((0, 256),), jnp.float32)
    owners_keys = jax.random.split(jax.random.fold_in(seeds[3], 1), QUESTIONS * K // (Q_DEV * K))
    owners_turns = jax.random.permutation(jax.random.fold_in(seeds[3], 3), QUESTIONS * K // (Q_DEV * K))
    owners = jax.vmap(lambda own, number: assign_block(jax.random.fold_in(seeds[3], 2), own, number, Q_DEV * K, N_SHARD, 1, CAP, 2))(owners_keys, owners_turns).reshape((QUESTIONS, K, 1))
    passage_rows = place_ends(jax.random.randint(seeds[4], (QUESTIONS, K), 0, PASS_DEV), jax.random.fold_in(seeds[4], 1), 0, PASS_DEV - 1).astype(jnp.int32)
    w_up = centred(seeds[5], (D, FF), D ** -0.5, 0.21875)
    final_lowering_matrix = centred(seeds[6], (FF, D), FF ** -0.5, 0.109375)
    return dict(index_states=index_states, questions=questions, reader_attention_scores=reader_attention_scores, owners=owners, passage_rows=passage_rows, w_up=w_up, final_lowering_matrix=final_lowering_matrix)


normalizer_heat = 0.1
loss_scale = 64.0
epsilon = 1e-06
gelu_coeff = 0.7978845608028654
cubic = 0.044715

def gelu_tanh(values):
    inner = gelu_coeff * (values + cubic * values * values * values)
    return 0.5 * values * (1.0 + jnp.tanh(inner))

def gelu_slope(values):
    inner = gelu_coeff * (values + cubic * values * values * values)
    tangent = jnp.tanh(inner)
    return 0.5 * (1.0 + tangent) + 0.5 * values * (1.0 - tangent * tangent) * gelu_coeff * (1.0 + 3.0 * cubic * values * values)

def normalize_questions(questions):
    wide = questions.astype(jnp.float32)
    return (wide / jnp.sqrt(lax.optimization_barrier(jnp.sum(wide * wide, -1, keepdims=True)) + epsilon)).astype(jnp.bfloat16)

def encode_rows(states, w_up, final_lowering_matrix):
    pre_act = jnp.dot(states, w_up, preferred_element_type=jnp.float32)
    hidden = gelu_tanh(pre_act).astype(jnp.bfloat16)
    embedded = states.astype(jnp.float32) + jnp.dot(hidden, final_lowering_matrix, preferred_element_type=jnp.float32)
    norms = jnp.sqrt(lax.optimization_barrier(jnp.sum(embedded * embedded, -1, keepdims=True)) + epsilon)
    return (pre_act, hidden, embedded / norms, norms)

def score_gradient(angular_match, reader_attention_scores):
    exponentiated_logits = jnp.exp(angular_match / normalizer_heat)
    probs = exponentiated_logits / lax.optimization_barrier(jnp.sum(exponentiated_logits, -1, keepdims=True))
    target_raw = jnp.exp(reader_attention_scores)
    target = target_raw / lax.optimization_barrier(jnp.sum(target_raw, -1, keepdims=True))
    return loss_scale * (probs - target)

def embed_gradient(mixing_weights, query_rows, unit_emb, norms, angular_match):
    return (mixing_weights[:, None] * (query_rows.astype(jnp.float32) - angular_match[:, None] * unit_emb) / norms).astype(jnp.bfloat16)

def contract_rows(left, right):
    return lax.dot_general(left, right, (((0,), (0,)), ((), ())), preferred_element_type=jnp.float32)

def reference(index_states, questions, reader_attention_scores, owners, passage_rows, w_up, final_lowering_matrix):
    blocks = N_SHARD * N_REP
    per_block = QUESTIONS // blocks
    q_hat = normalize_questions(questions)
    passage_ids = (owners[:, :, 0] * PASS_DEV + passage_rows).astype(jnp.int32)

    def step(totals, inputs):
        id_block, q_block, reader_block = inputs
        states = index_states[id_block.reshape(-1)]
        pre_act, hidden, unit_emb, norms = encode_rows(states, w_up, final_lowering_matrix)
        query_rows = jnp.repeat(q_block, K, axis=0)
        angular_match = lax.optimization_barrier(jnp.sum(unit_emb * query_rows.astype(jnp.float32), -1))
        derivative_collection = score_gradient(angular_match.reshape(-1, K), reader_block)
        mixing_weights = (derivative_collection / normalizer_heat).reshape(-1)
        grad_emb = embed_gradient(mixing_weights, query_rows, unit_emb, norms, angular_match)
        grad_hidden = lax.dot_general(grad_emb, final_lowering_matrix, (((1,), (1,)), ((), ())), preferred_element_type=jnp.float32)
        grad_pre = (grad_hidden * gelu_slope(pre_act)).astype(jnp.bfloat16)
        up_total = totals[0] + contract_rows(grad_pre, states)
        down_total = totals[1] + contract_rows(hidden, grad_emb)
        return ((up_total, down_total), derivative_collection)
    empty_gradient = jnp.zeros((FF, D), jnp.float32)
    inputs = (passage_ids.reshape(blocks, per_block, K), q_hat.reshape(blocks, per_block, D), reader_attention_scores.reshape(blocks, per_block, K))
    (up_total, down_total), derivative_collection = lax.scan(step, (empty_gradient, empty_gradient), inputs)
    return (derivative_collection.reshape(QUESTIONS, K), up_total, down_total)
```

```python
import itertools

import jax
import jax.numpy as jnp
from jax import lax
from jax.experimental import pallas as pl
from jax.experimental.pallas import tpu as pltpu
from jax.sharding import PartitionSpec as P

K = 32
Q = 8
CAP = 8
NZ, NY, NC, NX = 8, 4, 2, 4
OWN = 48
CHUNK = NY * NC * OWN
HALF_R, HALF_C = 24, 384

normalizer_heat = 0.1
loss_scale = 64.0
epsilon = 1e-06
gelu_coeff = 0.7978845608028654
cubic = 0.044715

bf16, f32, i32 = jnp.bfloat16, jnp.float32, jnp.int32
AXES = ("shard", "rep")


def gray(v):
    return v ^ (v >> 1)


def low_bit(v):
    return gray(v) & 1


def high_bit(v):
    return v >> 1


def label4(v, core):
    low, high = low_bit(v), high_bit(v)
    return (low * (1 - core) + high * core) * 2 + (high * (1 - core) + low * core)


def label8(v, core):
    g = gray((v - core) & 7)
    return ((g & 1) << 2) | (g & 2) | (g >> 2)


def partner(step):
    def meet(z, y, c, x):
        if step == "c":
            return (z, y, 1 - c, x)
        axis, turn = step[0], int(step[1]) - 1
        if axis == "z":
            mine = label8(z, c)
            other = [v for v in range(NZ) if label8(v, c) == mine ^ (4 >> turn)][0]
            return (other, y, c, x)
        at = x if axis == "x" else y
        mine = label4(at, c)
        other = [v for v in range(4) if label4(v, c) == mine ^ (2 >> turn)][0]
        return (z, y, c, other) if axis == "x" else (z, other, c, x)

    pairs = []
    for at, place in enumerate(itertools.product(range(NZ), range(NY), range(NC), range(NX))):
        z, y, c, x = meet(*place)
        pairs.append((at, ((z * NY + y) * NC + c) * NX + x))
    return pairs


def swap(array, step):
    return lax.ppermute(array, AXES, partner(step))


def column(values):
    count, width = values.shape
    spread = jnp.broadcast_to(values[:, None, :], (count, width, width))
    mask = lax.broadcasted_iota(i32, spread.shape, 1) == lax.broadcasted_iota(i32, spread.shape, 2)
    return jnp.sum(jnp.where(mask, spread, 0.0).reshape(count * width, width), -1, keepdims=True)


def uncolumn(values, width):
    spread = jnp.broadcast_to(values, (values.shape[0], width)).reshape(-1, width, width)
    mask = lax.broadcasted_iota(i32, spread.shape, 1) == lax.broadcasted_iota(i32, spread.shape, 2)
    return jnp.sum(jnp.where(mask, spread, 0.0), 1)


def dot(left, right, dims):
    return lax.dot_general(left, right, ((dims[0], dims[1]), ((), ())), preferred_element_type=f32)


def route_kernel(owner_ref, row_ref, send_ref, slot_ref):
    rows = Q * K
    shards = send_ref.shape[0]
    owner = column(owner_ref[...].astype(f32))
    row = column(row_ref[...].astype(f32))
    lanes = lax.broadcasted_iota(i32, (rows, shards), 1).astype(f32)
    onehot = (lanes == owner).astype(f32)
    earlier = (
        lax.broadcasted_iota(i32, (rows, rows), 1) < lax.broadcasted_iota(i32, (rows, rows), 0)
    ).astype(bf16)
    hot = onehot.astype(bf16)
    prior = dot(earlier, hot, ((1,), (0,)))
    rank = jnp.sum(prior * onehot, -1, keepdims=True)
    high = jnp.floor(row * (1.0 / 32.0))
    low = row - 32.0 * high
    at = lax.broadcasted_iota(i32, (rows, 128), 1).astype(f32) == rank
    send_high = dot(hot, jnp.where(at, high, 0.0).astype(bf16), ((0,), (0,)))
    send_low = dot(hot, jnp.where(at, low, 0.0).astype(bf16), ((0,), (0,)))
    send_ref[:, 0, :] = (32.0 * send_high + send_low).astype(i32)
    slot_ref[...] = jnp.broadcast_to(owner * CAP + rank, slot_ref.shape).astype(i32)


def fetch_kernel(rows_ref, index_ref, out_ref):
    shards, cap, width = out_ref.shape
    want = rows_ref[...].astype(f32)
    spread = jnp.broadcast_to(want, (shards, cap, want.shape[2]))
    mask = lax.broadcasted_iota(i32, spread.shape, 1) == lax.broadcasted_iota(i32, spread.shape, 2)
    at = jnp.sum(jnp.where(mask, spread, 0.0).reshape(shards * cap, -1), -1, keepdims=True)
    here = lax.broadcasted_iota(i32, (shards * cap, index_ref.shape[0]), 1).astype(f32) == at
    got = dot(here.astype(f32).astype(bf16), index_ref[...], ((1,), (0,)))
    out_ref[...] = got.reshape(shards, cap, width).astype(bf16)


def place_pieces(place_ref, value_ref, outs, x_first):
    y, c, x = place_ref[1], place_ref[2], place_ref[3]
    for other, out_ref in enumerate(outs):
        core = c ^ other
        mine_x, mine_y = label4(x, core), label4(y, core)
        for j in range(NY):
            at_y = label4(j, core) ^ mine_y
            for piece in range(4):
                at_x = piece ^ mine_x
                at = at_x * NY + at_y if x_first else at_y * NX + at_x
                start = pl.multiple_of(j * NC * OWN + core * OWN + (piece & 1) * HALF_R, 8)
                columns = (piece >> 1) * HALF_C
                out_ref[at, 0] = value_ref[pl.ds(start, HALF_R), columns : columns + HALF_C].astype(bf16)


def forward_kernel(
    place_ref, got_ref, slot_ref, question_ref, reader_ref, up_ref, down_ref,
    derivative_ref, states_out_ref, grad_emb_ref, slope_ref, keep_ref, send_ref,
    states_ref, embedded_ref, hidden_ref, value_ref,
):
    step = pl.program_id(0)
    width = question_ref.shape[1]

    @pl.when(step == 0)
    def _():
        lanes = lax.broadcasted_iota(i32, (Q * K, got_ref.shape[0]), 1)
        onehot = (lanes == slot_ref[:, :1]).astype(f32).astype(bf16)
        states = dot(onehot, got_ref[...], ((1,), (0,)))
        embedded_ref[...] = states
        states_ref[...] = states.astype(bf16)
        states_out_ref[...] = states.astype(bf16)

    @pl.when(step < NZ)
    def _():
        pre = dot(states_ref[...], up_ref[...], ((1,), (0,)))
        square = pre * pre
        tangent = jnp.tanh(gelu_coeff * (pre + cubic * square * pre))
        gate = 0.5 * (1.0 + tangent)
        hidden = (pre * gate).astype(bf16)
        slope_ref[...] = gate + 0.5 * pre * (1.0 - tangent * tangent) * gelu_coeff * (
            1.0 + 3.0 * cubic * square
        )
        hidden_ref[step] = hidden
        embedded_ref[...] += dot(hidden, down_ref[...], ((1,), (0,)))

    @pl.when(step == NZ)
    def _():
        embedded = embedded_ref[...]
        norms = jnp.sqrt(jnp.sum(embedded * embedded, -1, keepdims=True) + epsilon)
        unit = embedded / norms
        wide = question_ref[...].astype(f32)
        q_hat = (wide / jnp.sqrt(jnp.sum(wide * wide, -1, keepdims=True) + epsilon)).astype(bf16)
        query = jnp.broadcast_to(q_hat.astype(f32)[:, None, :], (Q, K, width)).reshape(Q * K, width)
        cosine = jnp.sum(unit * query, -1, keepdims=True)

        def share(scores):
            raised = jnp.exp(scores).reshape(Q, K, 1)
            return (raised / jnp.sum(raised, 1, keepdims=True)).reshape(Q * K, 1)

        derivative = loss_scale * (share(cosine / normalizer_heat) - share(column(reader_ref[...])))
        derivative_ref[...] = uncolumn(derivative, K)
        grad_emb_ref[...] = (
            (derivative / normalizer_heat) * (query - cosine * unit) / norms
        ).astype(bf16)

    @pl.when(step >= NZ)
    def _():
        value_ref[...] = dot(hidden_ref[step - NZ], grad_emb_ref[...], ((0,), (0,)))
        place_pieces(place_ref, value_ref, (keep_ref, send_ref), True)


def backward_kernel(
    place_ref, grad_emb_ref, states_ref, slope_ref, down_ref, keep_ref, send_ref, value_ref
):
    grad_hidden = dot(grad_emb_ref[...], down_ref[...], ((1,), (1,)))
    grad_pre = (grad_hidden * slope_ref[...]).astype(bf16)
    value_ref[...] = dot(grad_pre, states_ref[...], ((0,), (0,)))
    place_pieces(place_ref, value_ref, (keep_ref, send_ref), False)


def whole(shape):
    return pl.BlockSpec(shape, lambda *_: (0,) * len(shape))


def z_block(place_ref, block, other):
    core = place_ref[2] ^ other
    return (0, label8(block, core) ^ label8(place_ref[0], core), 0, 0)


def route(owners, passage_rows, shards):
    return pl.pallas_call(
        route_kernel,
        out_shape=(
            jax.ShapeDtypeStruct((shards, 1, 128), i32),
            jax.ShapeDtypeStruct((Q * K, 128), i32),
        ),
        name="route",
    )(owners, passage_rows)


def fetch(rows_in, index_states):
    shards, width = rows_in.shape[0], index_states.shape[1]
    return pl.pallas_call(
        fetch_kernel,
        out_shape=jax.ShapeDtypeStruct((shards, CAP, width), bf16),
        compiler_params=pltpu.CompilerParams(vmem_limit_bytes=32 << 20),
        name="fetch",
    )(rows_in, index_states)


def forward(place, got, slot, questions, reader, w_up, w_down):
    width, hidden = w_up.shape
    rows = Q * K
    piece = (NX * NY, NZ, HALF_R, HALF_C)
    last = NZ - 1

    def part(other):
        return pl.BlockSpec(
            (NX * NY, 1, HALF_R, HALF_C),
            lambda t, place_ref: z_block(place_ref, jnp.maximum(t - NZ, 0), other),
        )

    return pl.pallas_call(
        forward_kernel,
        grid_spec=pltpu.PrefetchScalarGridSpec(
            num_scalar_prefetch=1,
            grid=(2 * NZ,),
            in_specs=[
                whole(got.shape),
                whole(slot.shape),
                whole(questions.shape),
                whole(reader.shape),
                pl.BlockSpec((width, CHUNK), lambda t, _: (0, jnp.minimum(t, last))),
                pl.BlockSpec((CHUNK, width), lambda t, _: (jnp.minimum(t, last), 0)),
            ],
            out_specs=[
                whole((Q, K)),
                whole((rows, width)),
                whole((rows, width)),
                pl.BlockSpec((rows, CHUNK), lambda t, _: (0, jnp.minimum(t, last))),
                part(0),
                part(1),
            ],
            scratch_shapes=[
                pltpu.VMEM((rows, width), bf16),
                pltpu.VMEM((rows, width), f32),
                pltpu.VMEM((NZ, rows, CHUNK), bf16),
                pltpu.VMEM((CHUNK, width), f32),
            ],
        ),
        out_shape=(
            jax.ShapeDtypeStruct((Q, K), f32),
            jax.ShapeDtypeStruct((rows, width), bf16),
            jax.ShapeDtypeStruct((rows, width), bf16),
            jax.ShapeDtypeStruct((rows, hidden), f32),
            jax.ShapeDtypeStruct(piece, bf16),
            jax.ShapeDtypeStruct(piece, bf16),
        ),
        compiler_params=pltpu.CompilerParams(vmem_limit_bytes=40 << 20),
        cost_estimate=pl.CostEstimate(
            flops=6 * rows * width * hidden, bytes_accessed=24 << 20, transcendentals=rows * hidden
        ),
        name="forward",
    )(place, got, slot, questions, reader, w_up, w_down)


def backward(place, grad_emb, states, slope, w_down):
    hidden, width = w_down.shape
    rows = Q * K
    piece = (NX * NY, NZ, HALF_R, HALF_C)

    def part(other):
        return pl.BlockSpec(
            (NX * NY, 1, HALF_R, HALF_C), lambda t, place_ref: z_block(place_ref, t, other)
        )

    return pl.pallas_call(
        backward_kernel,
        grid_spec=pltpu.PrefetchScalarGridSpec(
            num_scalar_prefetch=1,
            grid=(NZ,),
            in_specs=[
                whole((rows, width)),
                whole((rows, width)),
                pl.BlockSpec((rows, CHUNK), lambda t, _: (0, t)),
                pl.BlockSpec((CHUNK, width), lambda t, _: (t, 0)),
            ],
            out_specs=[part(0), part(1)],
            scratch_shapes=[pltpu.VMEM((CHUNK, width), f32)],
        ),
        out_shape=(jax.ShapeDtypeStruct(piece, bf16), jax.ShapeDtypeStruct(piece, bf16)),
        compiler_params=pltpu.CompilerParams(vmem_limit_bytes=40 << 20),
        cost_estimate=pl.CostEstimate(
            flops=4 * rows * width * hidden, bytes_accessed=16 << 20, transcendentals=0
        ),
        name="backward",
    )(place, grad_emb, states, slope, w_down)


def halves(array):
    half = array.shape[0] // 2
    return array[:half], array[half:]


def meet(keep, send, step):
    came = swap(send, step)
    keep_own, keep_next = halves(keep)
    came_own, came_next = halves(came)
    return (
        keep_own.astype(f32) + came_own.astype(f32),
        (keep_next.astype(f32) + came_next.astype(f32)).astype(bf16),
    )


def total(keep, send, step):
    return keep.astype(f32) + swap(send, step).astype(f32)


def on_device(index_states, questions, reader, owners, passage_rows, w_up, w_down):
    shards = lax.axis_size("shard")
    width = questions.shape[1]
    shard, x = lax.axis_index("shard"), lax.axis_index("rep")
    z, y, c = shard >> 3, (shard >> 1) & 3, shard & 1
    place = jnp.stack([z, y, c, x]).astype(i32)

    send_rows, slot = route(owners.reshape(Q, K), passage_rows, shards)
    rows_in = lax.all_to_all(send_rows, "shard", split_axis=0, concat_axis=0, tiled=True)
    states_out = fetch(rows_in, index_states)
    got = lax.all_to_all(states_out, "shard", split_axis=0, concat_axis=0, tiled=True)
    derivative, states, grad_emb, slope, keep_down, send_down = forward(
        place, got.reshape(shards * CAP, width), slot, questions, reader, w_up, w_down
    )
    keep_up, send_up = backward(place, grad_emb, states, slope, w_down)

    down, up = (keep_down, send_down), (keep_up, send_up)
    for step in ("c", "x1", "x2", "y1"):
        down = meet(*down, step)
    for step in ("c", "y1", "y2", "x1"):
        up = meet(*up, step)
    both = jnp.concatenate([total(*down, "y2"), total(*up, "x2")])
    both = both.reshape(2, NZ, HALF_R, HALF_C).swapaxes(0, 1)
    keep, send = halves(both)
    send = send.astype(bf16)
    for step in ("z1", "z2"):
        keep, send = meet(keep, send, step)
    mine = total(keep, send, "z3")[0]

    label = label4(x, c)
    came = swap(mine, "x2")
    first = (label & 1) == 0
    mine = jnp.concatenate([jnp.where(first, mine, came), jnp.where(first, came, mine)], 1)
    came = swap(mine, "x1")
    first = (label >> 1) == 0
    mine = jnp.concatenate([jnp.where(first, mine, came), jnp.where(first, came, mine)], 2)
    return derivative, mine[1], mine[0]


def solution(mesh):
    placed = (
        P("shard", None),
        P(("shard", "rep"), None),
        P(("shard", "rep"), None),
        P(("shard", "rep"), None, None),
        P(("shard", "rep"), None),
        P(),
        P(),
    )
    return jax.shard_map(
        on_device,
        mesh=mesh,
        in_specs=placed,
        out_specs=(P(("shard", "rep"), None), P("shard", None), P("shard", None)),
        check_vma=False,
    )
```

```python
import itertools

import jax
import jax.numpy as jnp
from jax import lax
from jax.experimental import pallas as pl
from jax.experimental.pallas import tpu as pltpu
from jax.sharding import PartitionSpec as P

K = 32
Q = 8
CAP = 8
NZ, NY, NC, NX = 8, 4, 2, 4
OWN = 48
CHUNK = NY * NC * OWN
HALF_R, HALF_C = 24, 384
WIDE = 512

normalizer_heat = 0.1
loss_scale = 64.0
epsilon = 1e-06
gelu_coeff = 0.7978845608028654
cubic = 0.044715

bf16, f32, i32 = jnp.bfloat16, jnp.float32, jnp.int32
AXES = ("shard", "rep")


def gray(v):
    return v ^ (v >> 1)


def low_bit(v):
    return gray(v) & 1


def high_bit(v):
    return v >> 1


def label4(v, core):
    low, high = low_bit(v), high_bit(v)
    return (low * (1 - core) + high * core) * 2 + (high * (1 - core) + low * core)


def label8(v, core):
    g = gray((v - core) & 7)
    return ((g & 1) << 2) | (g & 2) | (g >> 2)


def partner(step):
    def meet(z, y, c, x):
        if step == "c":
            return (z, y, 1 - c, x)
        axis, turn = step[0], int(step[1]) - 1
        if axis == "z":
            mine = label8(z, c)
            other = [v for v in range(NZ) if label8(v, c) == mine ^ (4 >> turn)][0]
            return (other, y, c, x)
        at = x if axis == "x" else y
        mine = label4(at, c)
        other = [v for v in range(4) if label4(v, c) == mine ^ (2 >> turn)][0]
        return (z, y, c, other) if axis == "x" else (z, other, c, x)

    pairs = []
    for at, place in enumerate(itertools.product(range(NZ), range(NY), range(NC), range(NX))):
        z, y, c, x = meet(*place)
        pairs.append((at, ((z * NY + y) * NC + c) * NX + x))
    return pairs


def swap(array, step):
    return lax.ppermute(array, AXES, partner(step))


def column(values):
    count, width = values.shape
    spread = jnp.broadcast_to(values[:, None, :], (count, width, width))
    mask = lax.broadcasted_iota(i32, spread.shape, 1) == lax.broadcasted_iota(i32, spread.shape, 2)
    return jnp.sum(jnp.where(mask, spread, 0.0).reshape(count * width, width), -1, keepdims=True)


def uncolumn(values, width):
    spread = jnp.broadcast_to(values, (values.shape[0], width)).reshape(-1, width, width)
    mask = lax.broadcasted_iota(i32, spread.shape, 1) == lax.broadcasted_iota(i32, spread.shape, 2)
    return jnp.sum(jnp.where(mask, spread, 0.0), 1)


def dot(left, right, dims):
    return lax.dot_general(left, right, ((dims[0], dims[1]), ((), ())), preferred_element_type=f32)


def route_kernel(owner_ref, row_ref, index_hbm, send_ref, slot_ref, index_ref, sem):
    load = pltpu.make_async_copy(index_hbm, index_ref, sem)
    load.start()
    rows = Q * K
    shards = send_ref.shape[0]
    owner = column(owner_ref[...].astype(f32))
    row = column(row_ref[...].astype(f32))
    lanes = lax.broadcasted_iota(i32, (rows, shards), 1).astype(f32)
    onehot = (lanes == owner).astype(f32)
    earlier = (
        lax.broadcasted_iota(i32, (rows, rows), 1) < lax.broadcasted_iota(i32, (rows, rows), 0)
    ).astype(bf16)
    hot = onehot.astype(bf16)
    prior = dot(earlier, hot, ((1,), (0,)))
    rank = jnp.sum(prior * onehot, -1, keepdims=True)
    high = jnp.floor(row * (1.0 / 32.0))
    low = row - 32.0 * high
    at = lax.broadcasted_iota(i32, (rows, 128), 1).astype(f32) == rank
    send_high = dot(hot, jnp.where(at, high, 0.0).astype(bf16), ((0,), (0,)))
    send_low = dot(hot, jnp.where(at, low, 0.0).astype(bf16), ((0,), (0,)))
    send_ref[:, 0, :] = (32.0 * send_high + send_low).astype(i32)
    slot_ref[...] = jnp.broadcast_to(owner * CAP + rank, slot_ref.shape).astype(i32)
    load.wait()


def fetch_kernel(rows_ref, index_ref, out_ref):
    shards, cap, width = out_ref.shape
    want = rows_ref[...].astype(f32)
    spread = jnp.broadcast_to(want, (shards, cap, want.shape[2]))
    mask = lax.broadcasted_iota(i32, spread.shape, 1) == lax.broadcasted_iota(i32, spread.shape, 2)
    at = jnp.sum(jnp.where(mask, spread, 0.0).reshape(shards * cap, -1), -1, keepdims=True)
    lanes = lax.broadcasted_iota(i32, (shards * cap, index_ref.shape[0]), 1).astype(f32)
    here = (lanes == at).astype(f32).astype(bf16)
    got = dot(here, index_ref[...], ((1,), (0,)))
    out_ref[...] = got.reshape(shards, cap, width).astype(bf16)


def place_gradient(place_ref, value_ref, outs, z, x_first):
    y, c, x = place_ref[1], place_ref[2], place_ref[3]
    for other, out_ref in enumerate(outs):
        core = c ^ other
        mine_x, mine_y = label4(x, core), label4(y, core)
        at_z = label8(z, core) ^ label8(place_ref[0], core)
        for j in range(NY):
            at_y = label4(j, core) ^ mine_y
            for piece in range(4):
                at_x = piece ^ mine_x
                at = at_x * NY + at_y if x_first else at_y * NX + at_x
                start = pl.multiple_of(j * NC * OWN + core * OWN + (piece & 1) * HALF_R, 8)
                columns = (piece >> 1) * HALF_C
                out_ref[at, at_z] = value_ref[pl.ds(start, HALF_R), columns : columns + HALF_C].astype(bf16)


def forward_kernel(
    place_ref, got_ref, slot_ref, question_ref, reader_ref, up_hbm, down_hbm,
    derivative_ref, states_ref, grad_emb_ref, slope_ref, keep_ref, send_ref,
    up_ref, down_ref, hidden_ref, value_ref, sems,
):
    width = question_ref.shape[1]
    parts = up_ref.shape[1] // WIDE
    ups, downs = [], []
    for t in range(parts):
        cut = pl.ds(t * WIDE, WIDE)
        ups.append(pltpu.make_async_copy(up_hbm.at[:, cut], up_ref.at[:, cut], sems.at[0, t]))
        downs.append(pltpu.make_async_copy(down_hbm.at[cut, :], down_ref.at[cut, :], sems.at[1, t]))
        ups[t].start()
        downs[t].start()

    lanes = lax.broadcasted_iota(i32, (Q * K, got_ref.shape[0]), 1)
    onehot = (lanes == slot_ref[:, :1]).astype(f32).astype(bf16)
    states = dot(onehot, got_ref[...], ((1,), (0,))).astype(bf16)
    states_ref[...] = states
    for t in range(parts):
        cut = slice(t * WIDE, (t + 1) * WIDE)
        ups[t].wait()
        pre = dot(states, up_ref[:, cut], ((1,), (0,)))
        square = pre * pre
        tangent = jnp.tanh(pre * (gelu_coeff + (gelu_coeff * cubic) * square))
        gate = 0.5 + 0.5 * tangent
        hidden = (pre * gate).astype(bf16)
        slope_ref[:, cut] = gate + pre * (1.0 - tangent * tangent) * (
            0.5 * gelu_coeff + (1.5 * gelu_coeff * cubic) * square
        )
        hidden_ref[:, cut] = hidden
    for copy in downs:
        copy.wait()
    embedded = states.astype(f32) + dot(hidden_ref[...], down_ref[...], ((1,), (0,)))
    norms = jnp.sqrt(jnp.sum(embedded * embedded, -1, keepdims=True) + epsilon)
    unit = embedded / norms
    wide = question_ref[...].astype(f32)
    q_hat = (wide / jnp.sqrt(jnp.sum(wide * wide, -1, keepdims=True) + epsilon)).astype(bf16)
    query = jnp.broadcast_to(q_hat.astype(f32)[:, None, :], (Q, K, width)).reshape(Q * K, width)
    cosine = jnp.sum(unit * query, -1, keepdims=True)

    def share(scores):
        raised = jnp.exp(scores).reshape(Q, K, 1)
        return (raised / jnp.sum(raised, 1, keepdims=True)).reshape(Q * K, 1)

    derivative = loss_scale * (share(cosine / normalizer_heat) - share(column(reader_ref[...])))
    derivative_ref[...] = uncolumn(derivative, K)
    grad_emb = ((derivative / normalizer_heat) * (query - cosine * unit) / norms).astype(bf16)
    grad_emb_ref[...] = grad_emb
    for z in range(NZ):
        value_ref[z % 2] = dot(hidden_ref[:, z * CHUNK : (z + 1) * CHUNK], grad_emb, ((0,), (0,)))
        place_gradient(place_ref, value_ref.at[z % 2], (keep_ref, send_ref), z, True)


def backward_kernel(
    place_ref, grad_emb_ref, states_ref, slope_ref, down_hbm,
    keep_ref, send_ref,
    down_ref, grad_pre_ref, value_ref, sems,
):
    parts = down_ref.shape[0] // WIDE
    downs = []
    for t in range(parts):
        cut = pl.ds(t * WIDE, WIDE)
        downs.append(pltpu.make_async_copy(down_hbm.at[cut, :], down_ref.at[cut, :], sems.at[t]))
        downs[t].start()
    grad_emb, states = grad_emb_ref[...], states_ref[...]
    for t in range(parts):
        cut = slice(t * WIDE, (t + 1) * WIDE)
        downs[t].wait()
        grad_hidden = dot(grad_emb, down_ref[cut, :], ((1,), (1,)))
        grad_pre_ref[:, cut] = (grad_hidden * slope_ref[:, cut]).astype(bf16)
    for z in range(NZ):
        value_ref[z % 2] = dot(grad_pre_ref[:, z * CHUNK : (z + 1) * CHUNK], states, ((0,), (0,)))
        place_gradient(place_ref, value_ref.at[z % 2], (keep_ref, send_ref), z, False)


def far(array):
    return pltpu.with_memory_space_constraint(array, pltpu.HBM)


SMEM, VMEM, HBM = (
    pl.BlockSpec(memory_space=pltpu.SMEM),
    pl.BlockSpec(memory_space=pltpu.VMEM),
    pl.BlockSpec(memory_space=pltpu.HBM),
)


def route(owners, passage_rows, index_states, shards):
    return pl.pallas_call(
        route_kernel,
        in_specs=[VMEM, VMEM, HBM],
        out_specs=[VMEM] * 3,
        out_shape=(
            jax.ShapeDtypeStruct((shards, 1, 128), i32),
            jax.ShapeDtypeStruct((Q * K, 128), i32),
            jax.ShapeDtypeStruct(index_states.shape, index_states.dtype),
        ),
        scratch_shapes=[pltpu.SemaphoreType.DMA],
        name="route",
    )(owners, passage_rows, far(index_states))


def fetch(rows_in, index_states):
    shards, width = rows_in.shape[0], index_states.shape[1]
    return pl.pallas_call(
        fetch_kernel,
        out_shape=jax.ShapeDtypeStruct((shards, CAP, width), bf16),
        compiler_params=pltpu.CompilerParams(vmem_limit_bytes=32 << 20),
        name="fetch",
    )(rows_in, index_states)


def forward(place, got, slot, questions, reader, w_up, w_down):
    width, hidden = w_up.shape
    rows = Q * K
    piece = (NX * NY, NZ, HALF_R, HALF_C)
    return pl.pallas_call(
        forward_kernel,
        in_specs=[SMEM, VMEM, VMEM, VMEM, VMEM, HBM, HBM],
        out_specs=[VMEM] * 6,
        scratch_shapes=[
            pltpu.VMEM((width, hidden), bf16),
            pltpu.VMEM((hidden, width), bf16),
            pltpu.VMEM((rows, hidden), bf16),
            pltpu.VMEM((2, CHUNK, width), f32),
            pltpu.SemaphoreType.DMA((2, hidden // WIDE)),
        ],
        out_shape=(
            jax.ShapeDtypeStruct((Q, K), f32),
            jax.ShapeDtypeStruct((rows, width), bf16),
            jax.ShapeDtypeStruct((rows, width), bf16),
            jax.ShapeDtypeStruct((rows, hidden), f32),
            jax.ShapeDtypeStruct(piece, bf16),
            jax.ShapeDtypeStruct(piece, bf16),
        ),
        compiler_params=pltpu.CompilerParams(vmem_limit_bytes=32 << 20),
        cost_estimate=pl.CostEstimate(
            flops=6 * rows * width * hidden, bytes_accessed=24 << 20, transcendentals=rows * hidden
        ),
        name="forward",
    )(place, got, slot, questions, reader, far(w_up), far(w_down))


def backward(place, grad_emb, states, slope, w_down):
    hidden, width = w_down.shape
    rows = Q * K
    piece = (NX * NY, NZ, HALF_R, HALF_C)
    return pl.pallas_call(
        backward_kernel,
        in_specs=[SMEM, VMEM, VMEM, VMEM, HBM],
        out_specs=[VMEM] * 2,
        scratch_shapes=[
            pltpu.VMEM((hidden, width), bf16),
            pltpu.VMEM((rows, hidden), bf16),
            pltpu.VMEM((2, CHUNK, width), f32),
            pltpu.SemaphoreType.DMA((hidden // WIDE,)),
        ],
        out_shape=(jax.ShapeDtypeStruct(piece, bf16), jax.ShapeDtypeStruct(piece, bf16)),
        compiler_params=pltpu.CompilerParams(vmem_limit_bytes=24 << 20),
        cost_estimate=pl.CostEstimate(
            flops=4 * rows * width * hidden, bytes_accessed=16 << 20, transcendentals=0
        ),
        name="backward",
    )(place, grad_emb, states, slope, far(w_down))


def halves(array):
    half = array.shape[0] // 2
    return array[:half], array[half:]


def meet(keep, send, step):
    came = swap(send, step)
    keep_own, keep_next = halves(keep)
    came_own, came_next = halves(came)
    return (
        keep_own.astype(f32) + came_own.astype(f32),
        (keep_next.astype(f32) + came_next.astype(f32)).astype(bf16),
    )


def total(keep, send, step):
    return keep.astype(f32) + swap(send, step).astype(f32)


def on_device(index_states, questions, reader, owners, passage_rows, w_up, w_down):
    shards = lax.axis_size("shard")
    width = questions.shape[1]
    shard, x = lax.axis_index("shard"), lax.axis_index("rep")
    z, y, c = shard >> 3, (shard >> 1) & 3, shard & 1
    place = jnp.stack([z, y, c, x]).astype(i32)

    send_rows, slot, index_near = route(owners.reshape(Q, K), passage_rows, index_states, shards)
    rows_in = lax.all_to_all(send_rows, "shard", split_axis=0, concat_axis=0, tiled=True)
    states_out = fetch(rows_in, index_near)
    got = lax.all_to_all(states_out, "shard", split_axis=0, concat_axis=0, tiled=True)
    derivative, states, grad_emb, slope, keep_down, send_down = forward(
        place, got.reshape(shards * CAP, width), slot, questions, reader, w_up, w_down
    )
    keep_up, send_up = backward(place, grad_emb, states, slope, w_down)

    down, up = (keep_down, send_down), (keep_up, send_up)
    for step in ("c", "x1", "x2", "y1"):
        down = meet(*down, step)
    for step in ("c", "y1", "y2", "x1"):
        up = meet(*up, step)
    both = jnp.concatenate([total(*down, "y2"), total(*up, "x2")])
    both = both.reshape(2, NZ, HALF_R, HALF_C).swapaxes(0, 1)
    keep, send = halves(both)
    send = send.astype(bf16)
    for step in ("z1", "z2"):
        keep, send = meet(keep, send, step)
    mine = total(keep, send, "z3")[0]

    label = label4(x, c)
    came = swap(mine, "x2")
    first = (label & 1) == 0
    mine = jnp.concatenate([jnp.where(first, mine, came), jnp.where(first, came, mine)], 1)
    came = swap(mine, "x1")
    first = (label >> 1) == 0
    mine = jnp.concatenate([jnp.where(first, mine, came), jnp.where(first, came, mine)], 2)
    return derivative, mine[1], mine[0]


def solution(mesh):
    placed = (
        P("shard", None),
        P(("shard", "rep"), None),
        P(("shard", "rep"), None),
        P(("shard", "rep"), None, None),
        P(("shard", "rep"), None),
        P(),
        P(),
    )
    return jax.shard_map(
        on_device,
        mesh=mesh,
        in_specs=placed,
        out_specs=(P(("shard", "rep"), None), P("shard", None), P("shard", None)),
        check_vma=False,
    )
```

```python
import itertools

import jax
import jax.numpy as jnp
from jax import lax
from jax.experimental import pallas as pl
from jax.experimental.pallas import tpu as pltpu
from jax.sharding import PartitionSpec as P

K = 32
Q = 8
CAP = 8
NZ, NY, NC, NX = 8, 4, 2, 4
OWN = 48
CHUNK = NY * NC * OWN
HALF_R, HALF_C = 24, 384
WIDE = 512

normalizer_heat = 0.1
loss_scale = 64.0
epsilon = 1e-06
gelu_coeff = 0.7978845608028654
cubic = 0.044715

bf16, f32, i32 = jnp.bfloat16, jnp.float32, jnp.int32
AXES = ("shard", "rep")


def gray(v):
    return v ^ (v >> 1)


def low_bit(v):
    return gray(v) & 1


def high_bit(v):
    return v >> 1


def label4(v, core):
    low, high = low_bit(v), high_bit(v)
    return (low * (1 - core) + high * core) * 2 + (high * (1 - core) + low * core)


def label8(v, core):
    v = (v - core) & 7
    top = v >> 2
    return (((v & 1) ^ top) << 2) | ((((v >> 1) & 1) ^ top) << 1) | top


def partner(step):
    def meet(z, y, c, x):
        if step == "c":
            return (z, y, 1 - c, x)
        axis, turn = step[0], int(step[1]) - 1
        if axis == "z":
            mine = label8(z, c)
            other = [v for v in range(NZ) if label8(v, c) == mine ^ (4 >> turn)][0]
            return (other, y, c, x)
        at = x if axis == "x" else y
        mine = label4(at, c)
        other = [v for v in range(4) if label4(v, c) == mine ^ (2 >> turn)][0]
        return (z, y, c, other) if axis == "x" else (z, other, c, x)

    pairs = []
    for at, place in enumerate(itertools.product(range(NZ), range(NY), range(NC), range(NX))):
        z, y, c, x = meet(*place)
        pairs.append((at, ((z * NY + y) * NC + c) * NX + x))
    return pairs


def swap(array, step):
    return lax.ppermute(array, AXES, partner(step))


def column(values):
    count, width = values.shape
    spread = jnp.broadcast_to(values[:, None, :], (count, width, width))
    mask = lax.broadcasted_iota(i32, spread.shape, 1) == lax.broadcasted_iota(i32, spread.shape, 2)
    return jnp.sum(jnp.where(mask, spread, 0.0).reshape(count * width, width), -1, keepdims=True)


def uncolumn(values, width):
    spread = jnp.broadcast_to(values, (values.shape[0], width)).reshape(-1, width, width)
    mask = lax.broadcasted_iota(i32, spread.shape, 1) == lax.broadcasted_iota(i32, spread.shape, 2)
    return jnp.sum(jnp.where(mask, spread, 0.0), 1)


def dot(left, right, dims):
    return lax.dot_general(left, right, ((dims[0], dims[1]), ((), ())), preferred_element_type=f32)


def route_kernel(owner_ref, row_ref, index_hbm, send_ref, slot_ref, index_ref, sem):
    load = pltpu.make_async_copy(index_hbm, index_ref, sem)
    load.start()
    rows = Q * K
    shards = send_ref.shape[0]
    owner = column(owner_ref[...].astype(f32))
    row = column(row_ref[...].astype(f32))
    lanes = lax.broadcasted_iota(i32, (rows, shards), 1).astype(f32)
    onehot = (lanes == owner).astype(f32)
    earlier = (
        lax.broadcasted_iota(i32, (rows, rows), 1) < lax.broadcasted_iota(i32, (rows, rows), 0)
    ).astype(bf16)
    hot = onehot.astype(bf16)
    prior = dot(earlier, hot, ((1,), (0,)))
    rank = jnp.sum(prior * onehot, -1, keepdims=True)
    high = jnp.floor(row * (1.0 / 32.0))
    low = row - 32.0 * high
    at = lax.broadcasted_iota(i32, (rows, 128), 1).astype(f32) == rank
    send_high = dot(hot, jnp.where(at, high, 0.0).astype(bf16), ((0,), (0,)))
    send_low = dot(hot, jnp.where(at, low, 0.0).astype(bf16), ((0,), (0,)))
    send_ref[:, 0, :] = (32.0 * send_high + send_low).astype(i32)
    slot_ref[...] = jnp.broadcast_to(owner * CAP + rank, slot_ref.shape).astype(i32)
    load.wait()


def fetch_kernel(rows_ref, index_ref, out_ref):
    shards, cap, width = out_ref.shape
    want = rows_ref[...].astype(f32)
    spread = jnp.broadcast_to(want, (shards, cap, want.shape[2]))
    mask = lax.broadcasted_iota(i32, spread.shape, 1) == lax.broadcasted_iota(i32, spread.shape, 2)
    at = jnp.sum(jnp.where(mask, spread, 0.0).reshape(shards * cap, -1), -1, keepdims=True)
    lanes = lax.broadcasted_iota(i32, (shards * cap, index_ref.shape[0]), 1).astype(f32)
    here = (lanes == at).astype(f32).astype(bf16)
    got = dot(here, index_ref[...], ((1,), (0,)))
    out_ref[...] = got.reshape(shards, cap, width).astype(bf16)


def place_gradient(place_ref, value_ref, outs, z, x_first):
    y, c, x = place_ref[1], place_ref[2], place_ref[3]
    for other, out_ref in enumerate(outs):
        core = c ^ other
        mine_x, mine_y = label4(x, core), label4(y, core)
        at_z = label8(z, core) ^ label8(place_ref[0], core)
        for j in range(NY):
            at_y = label4(j, core) ^ mine_y
            for piece in range(4):
                at_x = piece ^ mine_x
                at = at_x * NY + at_y if x_first else at_y * NX + at_x
                start = pl.multiple_of(j * NC * OWN + core * OWN + (piece & 1) * HALF_R, 8)
                columns = (piece >> 1) * HALF_C
                out_ref[at, at_z] = value_ref[pl.ds(start, HALF_R), columns : columns + HALF_C].astype(bf16)


def forward_kernel(
    place_ref, got_ref, slot_ref, question_ref, reader_ref, up_hbm, down_hbm,
    derivative_ref, states_ref, grad_emb_ref, slope_ref, keep_ref, send_ref,
    up_ref, down_ref, hidden_ref, value_ref, sems,
):
    width = question_ref.shape[1]
    parts = up_ref.shape[1] // WIDE
    ups, downs = [], []
    for t in range(parts):
        cut = pl.ds(t * WIDE, WIDE)
        ups.append(pltpu.make_async_copy(up_hbm.at[:, cut], up_ref.at[:, cut], sems.at[0, t]))
        downs.append(pltpu.make_async_copy(down_hbm.at[cut, :], down_ref.at[cut, :], sems.at[1, t]))
        ups[t].start()
        downs[t].start()

    lanes = lax.broadcasted_iota(i32, (Q * K, got_ref.shape[0]), 1)
    onehot = (lanes == slot_ref[:, :1]).astype(f32).astype(bf16)
    states = dot(onehot, got_ref[...], ((1,), (0,))).astype(bf16)
    states_ref[...] = states
    for t in range(parts):
        cut = slice(t * WIDE, (t + 1) * WIDE)
        ups[t].wait()
        pre = dot(states, up_ref[:, cut], ((1,), (0,)))
        square = pre * pre
        tangent = jnp.tanh(pre * (gelu_coeff + (gelu_coeff * cubic) * square))
        gate = 0.5 + 0.5 * tangent
        hidden = (pre * gate).astype(bf16)
        slope_ref[:, cut] = gate + pre * (1.0 - tangent * tangent) * (
            0.5 * gelu_coeff + (1.5 * gelu_coeff * cubic) * square
        )
        hidden_ref[:, cut] = hidden
    for copy in downs:
        copy.wait()
    embedded = states.astype(f32) + dot(hidden_ref[...], down_ref[...], ((1,), (0,)))
    norms = jnp.sqrt(jnp.sum(embedded * embedded, -1, keepdims=True) + epsilon)
    unit = embedded / norms
    wide = question_ref[...].astype(f32)
    q_hat = (wide / jnp.sqrt(jnp.sum(wide * wide, -1, keepdims=True) + epsilon)).astype(bf16)
    query = jnp.broadcast_to(q_hat.astype(f32)[:, None, :], (Q, K, width)).reshape(Q * K, width)
    cosine = jnp.sum(unit * query, -1, keepdims=True)

    def share(scores):
        raised = jnp.exp(scores).reshape(Q, K, 1)
        return (raised / jnp.sum(raised, 1, keepdims=True)).reshape(Q * K, 1)

    derivative = loss_scale * (share(cosine / normalizer_heat) - share(column(reader_ref[...])))
    derivative_ref[...] = uncolumn(derivative, K)
    grad_emb = ((derivative / normalizer_heat) * (query - cosine * unit) / norms).astype(bf16)
    grad_emb_ref[...] = grad_emb
    for z in range(NZ):
        value_ref[z % 2] = dot(hidden_ref[:, z * CHUNK : (z + 1) * CHUNK], grad_emb, ((0,), (0,)))
        place_gradient(place_ref, value_ref.at[z % 2], (keep_ref, send_ref), z, True)


def backward_kernel(
    place_ref, grad_emb_ref, states_ref, slope_ref, down_hbm,
    keep_ref, send_ref,
    down_ref, grad_pre_ref, value_ref, sems,
):
    parts = down_ref.shape[0] // WIDE
    downs = []
    for t in range(parts):
        cut = pl.ds(t * WIDE, WIDE)
        downs.append(pltpu.make_async_copy(down_hbm.at[cut, :], down_ref.at[cut, :], sems.at[t]))
        downs[t].start()
    grad_emb, states = grad_emb_ref[...], states_ref[...]
    for t in range(parts):
        cut = slice(t * WIDE, (t + 1) * WIDE)
        downs[t].wait()
        grad_hidden = dot(grad_emb, down_ref[cut, :], ((1,), (1,)))
        grad_pre_ref[:, cut] = (grad_hidden * slope_ref[:, cut]).astype(bf16)
    for z in range(NZ):
        value_ref[z % 2] = dot(grad_pre_ref[:, z * CHUNK : (z + 1) * CHUNK], states, ((0,), (0,)))
        place_gradient(place_ref, value_ref.at[z % 2], (keep_ref, send_ref), z, False)


def far(array):
    return pltpu.with_memory_space_constraint(array, pltpu.HBM)


SMEM, VMEM, HBM = (
    pl.BlockSpec(memory_space=pltpu.SMEM),
    pl.BlockSpec(memory_space=pltpu.VMEM),
    pl.BlockSpec(memory_space=pltpu.HBM),
)


def route(owners, passage_rows, index_states, shards):
    return pl.pallas_call(
        route_kernel,
        in_specs=[VMEM, VMEM, HBM],
        out_specs=[VMEM] * 3,
        out_shape=(
            jax.ShapeDtypeStruct((shards, 1, 128), i32),
            jax.ShapeDtypeStruct((Q * K, 128), i32),
            pltpu.VMEM(index_states.shape, index_states.dtype),
        ),
        scratch_shapes=[pltpu.SemaphoreType.DMA],
        name="route",
    )(owners, passage_rows, far(index_states))


def fetch(rows_in, index_states):
    shards, width = rows_in.shape[0], index_states.shape[1]
    return pl.pallas_call(
        fetch_kernel,
        out_shape=jax.ShapeDtypeStruct((shards, CAP, width), bf16),
        compiler_params=pltpu.CompilerParams(vmem_limit_bytes=32 << 20),
        name="fetch",
    )(rows_in, pltpu.with_memory_space_constraint(index_states, pltpu.VMEM))


def forward(place, got, slot, questions, reader, w_up, w_down):
    width, hidden = w_up.shape
    rows = Q * K
    piece = (NX * NY, NZ, HALF_R, HALF_C)
    return pl.pallas_call(
        forward_kernel,
        in_specs=[SMEM, VMEM, VMEM, VMEM, VMEM, HBM, HBM],
        out_specs=[VMEM] * 6,
        scratch_shapes=[
            pltpu.VMEM((width, hidden), bf16),
            pltpu.VMEM((hidden, width), bf16),
            pltpu.VMEM((rows, hidden), bf16),
            pltpu.VMEM((2, CHUNK, width), f32),
            pltpu.SemaphoreType.DMA((2, hidden // WIDE)),
        ],
        out_shape=(
            jax.ShapeDtypeStruct((Q, K), f32),
            jax.ShapeDtypeStruct((rows, width), bf16),
            jax.ShapeDtypeStruct((rows, width), bf16),
            jax.ShapeDtypeStruct((rows, hidden), f32),
            jax.ShapeDtypeStruct(piece, bf16),
            jax.ShapeDtypeStruct(piece, bf16),
        ),
        compiler_params=pltpu.CompilerParams(vmem_limit_bytes=32 << 20),
        cost_estimate=pl.CostEstimate(
            flops=6 * rows * width * hidden, bytes_accessed=24 << 20, transcendentals=rows * hidden
        ),
        name="forward",
    )(place, got, slot, questions, reader, far(w_up), far(w_down))


def backward(place, grad_emb, states, slope, w_down):
    hidden, width = w_down.shape
    rows = Q * K
    piece = (NX * NY, NZ, HALF_R, HALF_C)
    return pl.pallas_call(
        backward_kernel,
        in_specs=[SMEM, VMEM, VMEM, VMEM, HBM],
        out_specs=[VMEM] * 2,
        scratch_shapes=[
            pltpu.VMEM((hidden, width), bf16),
            pltpu.VMEM((rows, hidden), bf16),
            pltpu.VMEM((2, CHUNK, width), f32),
            pltpu.SemaphoreType.DMA((hidden // WIDE,)),
        ],
        out_shape=(jax.ShapeDtypeStruct(piece, bf16), jax.ShapeDtypeStruct(piece, bf16)),
        compiler_params=pltpu.CompilerParams(vmem_limit_bytes=24 << 20),
        cost_estimate=pl.CostEstimate(
            flops=4 * rows * width * hidden, bytes_accessed=16 << 20, transcendentals=0
        ),
        name="backward",
    )(place, grad_emb, states, slope, far(w_down))


def halves(array):
    half = array.shape[0] // 2
    return array[:half], array[half:]


def meet(keep, send, step):
    came = swap(send, step)
    keep_own, keep_next = halves(keep)
    came_own, came_next = halves(came)
    return (
        keep_own.astype(f32) + came_own.astype(f32),
        (keep_next.astype(f32) + came_next.astype(f32)).astype(bf16),
    )


def total(keep, send, step):
    return keep.astype(f32) + swap(send, step).astype(f32)


def sum_plane(keep, send, steps):
    ahead, rest = swap(send[4:], steps[0]), swap(send[:4], steps[0])
    send = (keep[4:].astype(f32) + ahead.astype(f32)).astype(bf16)
    keep = keep[:4].astype(f32) + rest.astype(f32)
    ahead, rest = swap(send[2:], steps[1]), swap(send[:2], steps[1])
    came = swap((keep[2:] + ahead.astype(f32)).astype(bf16), steps[2])
    keep = keep[:2] + rest.astype(f32) + came.astype(f32)
    return keep[:1] + swap(keep[1:].astype(bf16), steps[3]).astype(f32)


def on_device(index_states, questions, reader, owners, passage_rows, w_up, w_down):
    shards = lax.axis_size("shard")
    width = questions.shape[1]
    shard, x = lax.axis_index("shard"), lax.axis_index("rep")
    z, y, c = shard >> 3, (shard >> 1) & 3, shard & 1
    place = jnp.stack([z, y, c, x]).astype(i32)

    send_rows, slot, index_near = route(owners.reshape(Q, K), passage_rows, index_states, shards)
    rows_in = lax.all_to_all(send_rows, "shard", split_axis=0, concat_axis=0, tiled=True)
    states_out = fetch(rows_in, index_near)
    got = lax.all_to_all(states_out, "shard", split_axis=0, concat_axis=0, tiled=True)
    derivative, states, grad_emb, slope, keep_down, send_down = forward(
        place, got.reshape(shards * CAP, width), slot, questions, reader, w_up, w_down
    )
    keep_up, send_up = backward(place, grad_emb, states, slope, w_down)

    down = sum_plane(*meet(keep_down, send_down, "c"), ("x1", "x2", "y1", "y2"))
    up = sum_plane(*meet(keep_up, send_up, "c"), ("y1", "y2", "x1", "x2"))
    both = jnp.concatenate([down, up])
    both = both.reshape(2, NZ, HALF_R, HALF_C).swapaxes(0, 1)
    keep, send = halves(both)
    send = send.astype(bf16)
    for step in ("z1", "z2"):
        keep, send = meet(keep, send, step)
    mine = total(keep, send, "z3")[0]

    label = label4(x, c)
    came = swap(mine, "x2")
    first = (label & 1) == 0
    mine = jnp.concatenate([jnp.where(first, mine, came), jnp.where(first, came, mine)], 1)
    came = swap(mine, "x1")
    first = (label >> 1) == 0
    mine = jnp.concatenate([jnp.where(first, mine, came), jnp.where(first, came, mine)], 2)
    return derivative, mine[1], mine[0]


def solution(mesh):
    placed = (
        P("shard", None),
        P(("shard", "rep"), None),
        P(("shard", "rep"), None),
        P(("shard", "rep"), None, None),
        P(("shard", "rep"), None),
        P(),
        P(),
    )
    return jax.shard_map(
        on_device,
        mesh=mesh,
        in_specs=placed,
        out_specs=(P(("shard", "rep"), None), P("shard", None), P("shard", None)),
        check_vma=False,
    )
```

```python
import itertools

import jax
import jax.numpy as jnp
from jax import lax
from jax.experimental import pallas as pl
from jax.experimental.pallas import tpu as pltpu
from jax.sharding import PartitionSpec as P

K = 32
Q = 8
CAP = 8
NZ, NY, NC, NX = 8, 4, 2, 4
OWN = 48
CHUNK = NY * NC * OWN
HALF_R, HALF_C = 24, 384
WIDE = 512

normalizer_heat = 0.1
loss_scale = 64.0
epsilon = 1e-06
gelu_coeff = 0.7978845608028654
cubic = 0.044715

bf16, f32, i32 = jnp.bfloat16, jnp.float32, jnp.int32
AXES = ("shard", "rep")


def gray(v):
    return v ^ (v >> 1)


def low_bit(v):
    return gray(v) & 1


def high_bit(v):
    return v >> 1


def label4(v, core):
    low, high = low_bit(v), high_bit(v)
    return (low * (1 - core) + high * core) * 2 + (high * (1 - core) + low * core)


def label8(v, core):
    v = (v - core) & 7
    top = v >> 2
    return (((v & 1) ^ top) << 2) | ((((v >> 1) & 1) ^ top) << 1) | top


def partner(step):
    def meet(z, y, c, x):
        if step == "c":
            return (z, y, 1 - c, x)
        axis, turn = step[0], int(step[1]) - 1
        if axis == "z":
            mine = label8(z, c)
            other = [v for v in range(NZ) if label8(v, c) == mine ^ (4 >> turn)][0]
            return (other, y, c, x)
        at = x if axis == "x" else y
        mine = label4(at, c)
        other = [v for v in range(4) if label4(v, c) == mine ^ (2 >> turn)][0]
        return (z, y, c, other) if axis == "x" else (z, other, c, x)

    pairs = []
    for at, place in enumerate(itertools.product(range(NZ), range(NY), range(NC), range(NX))):
        z, y, c, x = meet(*place)
        pairs.append((at, ((z * NY + y) * NC + c) * NX + x))
    return pairs


def swap(array, step):
    return lax.ppermute(array, AXES, partner(step))


def column(values):
    count, width = values.shape
    spread = jnp.broadcast_to(values[:, None, :], (count, width, width))
    mask = lax.broadcasted_iota(i32, spread.shape, 1) == lax.broadcasted_iota(i32, spread.shape, 2)
    return jnp.sum(jnp.where(mask, spread, 0.0).reshape(count * width, width), -1, keepdims=True)


def uncolumn(values, width):
    spread = jnp.broadcast_to(values, (values.shape[0], width)).reshape(-1, width, width)
    mask = lax.broadcasted_iota(i32, spread.shape, 1) == lax.broadcasted_iota(i32, spread.shape, 2)
    return jnp.sum(jnp.where(mask, spread, 0.0), 1)


def dot(left, right, dims):
    return lax.dot_general(left, right, ((dims[0], dims[1]), ((), ())), preferred_element_type=f32)


def route_kernel(owner_ref, row_ref, index_hbm, send_ref, slot_ref, index_ref, sem):
    load = pltpu.make_async_copy(index_hbm, index_ref, sem)
    load.start()
    rows = Q * K
    shards = send_ref.shape[0]
    owner = column(owner_ref[...].astype(f32))
    row = column(row_ref[...].astype(f32))
    lanes = lax.broadcasted_iota(i32, (rows, shards), 1).astype(f32)
    onehot = (lanes == owner).astype(f32)
    earlier = (
        lax.broadcasted_iota(i32, (rows, rows), 1) < lax.broadcasted_iota(i32, (rows, rows), 0)
    ).astype(bf16)
    hot = onehot.astype(bf16)
    prior = dot(earlier, hot, ((1,), (0,)))
    rank = jnp.sum(prior * onehot, -1, keepdims=True)
    high = jnp.floor(row * (1.0 / 32.0))
    low = row - 32.0 * high
    at = lax.broadcasted_iota(i32, (rows, 128), 1).astype(f32) == rank
    send_high = dot(hot, jnp.where(at, high, 0.0).astype(bf16), ((0,), (0,)))
    send_low = dot(hot, jnp.where(at, low, 0.0).astype(bf16), ((0,), (0,)))
    send_ref[:, 0, :] = (32.0 * send_high + send_low).astype(i32)
    slot_ref[...] = jnp.broadcast_to(owner * CAP + rank, slot_ref.shape).astype(i32)
    load.wait()


def fetch_kernel(rows_ref, index_ref, out_ref):
    shards, cap, width = out_ref.shape
    want = rows_ref[...].astype(f32)
    spread = jnp.broadcast_to(want, (shards, cap, want.shape[2]))
    mask = lax.broadcasted_iota(i32, spread.shape, 1) == lax.broadcasted_iota(i32, spread.shape, 2)
    at = jnp.sum(jnp.where(mask, spread, 0.0).reshape(shards * cap, -1), -1, keepdims=True)
    lanes = lax.broadcasted_iota(i32, (shards * cap, index_ref.shape[0]), 1).astype(f32)
    here = (lanes == at).astype(f32).astype(bf16)
    got = dot(here, index_ref[...], ((1,), (0,)))
    out_ref[...] = got.reshape(shards, cap, width).astype(bf16)


def place_gradient(place_ref, value_ref, outs, z, x_first):
    y, c, x = place_ref[1], place_ref[2], place_ref[3]
    for other, out_ref in enumerate(outs):
        core = c ^ other
        mine_x, mine_y = label4(x, core), label4(y, core)
        at_z = label8(z, core) ^ label8(place_ref[0], core)
        for j in range(NY):
            at_y = label4(j, core) ^ mine_y
            for piece in range(4):
                at_x = piece ^ mine_x
                at = at_x * NY + at_y if x_first else at_y * NX + at_x
                start = pl.multiple_of(j * NC * OWN + core * OWN + (piece & 1) * HALF_R, 8)
                columns = (piece >> 1) * HALF_C
                out_ref[at, at_z] = value_ref[pl.ds(start, HALF_R), columns : columns + HALF_C].astype(bf16)


def forward_kernel(
    place_ref, got_ref, slot_ref, question_ref, reader_ref, up_hbm, down_hbm,
    derivative_ref, states_ref, grad_emb_ref, slope_ref, keep_ref, send_ref,
    up_ref, down_ref, hidden_ref, value_ref, sems,
):
    width = question_ref.shape[1]
    parts = up_ref.shape[1] // WIDE
    ups, downs = [], []
    for t in range(parts):
        cut = pl.ds(t * WIDE, WIDE)
        ups.append(pltpu.make_async_copy(up_hbm.at[:, cut], up_ref.at[:, cut], sems.at[0, t]))
        downs.append(pltpu.make_async_copy(down_hbm.at[cut, :], down_ref.at[cut, :], sems.at[1, t]))
        ups[t].start()
        downs[t].start()

    lanes = lax.broadcasted_iota(i32, (Q * K, got_ref.shape[0]), 1)
    onehot = (lanes == slot_ref[:, :1]).astype(f32).astype(bf16)
    states = dot(onehot, got_ref[...], ((1,), (0,))).astype(bf16)
    states_ref[...] = states
    for t in range(parts):
        cut = slice(t * WIDE, (t + 1) * WIDE)
        ups[t].wait()
        pre = dot(states, up_ref[:, cut], ((1,), (0,)))
        square = pre * pre
        tangent = jnp.tanh(pre * (gelu_coeff + (gelu_coeff * cubic) * square))
        gate = 0.5 + 0.5 * tangent
        hidden = (pre * gate).astype(bf16)
        slope_ref[:, cut] = gate + pre * (1.0 - tangent * tangent) * (
            0.5 * gelu_coeff + (1.5 * gelu_coeff * cubic) * square
        )
        hidden_ref[:, cut] = hidden
    for copy in downs:
        copy.wait()
    embedded = states.astype(f32) + dot(hidden_ref[...], down_ref[...], ((1,), (0,)))
    norms = jnp.sqrt(jnp.sum(embedded * embedded, -1, keepdims=True) + epsilon)
    unit = embedded / norms
    wide = question_ref[...].astype(f32)
    q_hat = (wide / jnp.sqrt(jnp.sum(wide * wide, -1, keepdims=True) + epsilon)).astype(bf16)
    query = jnp.broadcast_to(q_hat.astype(f32)[:, None, :], (Q, K, width)).reshape(Q * K, width)
    cosine = jnp.sum(unit * query, -1, keepdims=True)

    def share(scores):
        raised = jnp.exp(scores).reshape(Q, K, 1)
        return (raised / jnp.sum(raised, 1, keepdims=True)).reshape(Q * K, 1)

    derivative = loss_scale * (share(cosine / normalizer_heat) - share(column(reader_ref[...])))
    derivative_ref[...] = uncolumn(derivative, K)
    grad_emb = ((derivative / normalizer_heat) * (query - cosine * unit) / norms).astype(bf16)
    grad_emb_ref[...] = grad_emb
    for z in range(NZ):
        value_ref[z % 2] = dot(hidden_ref[:, z * CHUNK : (z + 1) * CHUNK], grad_emb, ((0,), (0,)))
        place_gradient(place_ref, value_ref.at[z % 2], (keep_ref, send_ref), z, True)


def backward_kernel(
    place_ref, grad_emb_ref, states_ref, slope_ref, down_hbm,
    keep_ref, send_ref,
    down_ref, grad_pre_ref, value_ref, sems,
):
    parts = down_ref.shape[0] // WIDE
    downs = []
    for t in range(parts):
        cut = pl.ds(t * WIDE, WIDE)
        downs.append(pltpu.make_async_copy(down_hbm.at[cut, :], down_ref.at[cut, :], sems.at[t]))
        downs[t].start()
    grad_emb, states = grad_emb_ref[...], states_ref[...]
    for t in range(parts):
        cut = slice(t * WIDE, (t + 1) * WIDE)
        downs[t].wait()
        grad_hidden = dot(grad_emb, down_ref[cut, :], ((1,), (1,)))
        grad_pre_ref[:, cut] = (grad_hidden * slope_ref[:, cut]).astype(bf16)
    for z in range(NZ):
        value_ref[z % 2] = dot(grad_pre_ref[:, z * CHUNK : (z + 1) * CHUNK], states, ((0,), (0,)))
        place_gradient(place_ref, value_ref.at[z % 2], (keep_ref, send_ref), z, False)


def far(array):
    return pltpu.with_memory_space_constraint(array, pltpu.HBM)


SMEM, VMEM, HBM = (
    pl.BlockSpec(memory_space=pltpu.SMEM),
    pl.BlockSpec(memory_space=pltpu.VMEM),
    pl.BlockSpec(memory_space=pltpu.HBM),
)


def route(owners, passage_rows, index_states, shards):
    return pl.pallas_call(
        route_kernel,
        in_specs=[VMEM, VMEM, HBM],
        out_specs=[VMEM] * 3,
        out_shape=(
            jax.ShapeDtypeStruct((shards, 1, 128), i32),
            jax.ShapeDtypeStruct((Q * K, 128), i32),
            pltpu.VMEM(index_states.shape, index_states.dtype),
        ),
        scratch_shapes=[pltpu.SemaphoreType.DMA],
        name="route",
    )(owners, passage_rows, far(index_states))


def fetch(rows_in, index_states):
    shards, width = rows_in.shape[0], index_states.shape[1]
    return pl.pallas_call(
        fetch_kernel,
        out_shape=jax.ShapeDtypeStruct((shards, CAP, width), bf16),
        compiler_params=pltpu.CompilerParams(vmem_limit_bytes=32 << 20),
        name="fetch",
    )(rows_in, pltpu.with_memory_space_constraint(index_states, pltpu.VMEM))


def forward(place, got, slot, questions, reader, w_up, w_down):
    width, hidden = w_up.shape
    rows = Q * K
    piece = (NX * NY, NZ, HALF_R, HALF_C)
    return pl.pallas_call(
        forward_kernel,
        in_specs=[SMEM, VMEM, VMEM, VMEM, VMEM, HBM, HBM],
        out_specs=[VMEM] * 6,
        scratch_shapes=[
            pltpu.VMEM((width, hidden), bf16),
            pltpu.VMEM((hidden, width), bf16),
            pltpu.VMEM((rows, hidden), bf16),
            pltpu.VMEM((2, CHUNK, width), f32),
            pltpu.SemaphoreType.DMA((2, hidden // WIDE)),
        ],
        out_shape=(
            jax.ShapeDtypeStruct((Q, K), f32),
            jax.ShapeDtypeStruct((rows, width), bf16),
            jax.ShapeDtypeStruct((rows, width), bf16),
            jax.ShapeDtypeStruct((rows, hidden), f32),
            jax.ShapeDtypeStruct(piece, bf16),
            jax.ShapeDtypeStruct(piece, bf16),
        ),
        compiler_params=pltpu.CompilerParams(vmem_limit_bytes=32 << 20),
        cost_estimate=pl.CostEstimate(
            flops=6 * rows * width * hidden, bytes_accessed=24 << 20, transcendentals=rows * hidden
        ),
        name="forward",
    )(place, got, slot, questions, reader, far(w_up), far(w_down))


def backward(place, grad_emb, states, slope, w_down):
    hidden, width = w_down.shape
    rows = Q * K
    piece = (NX * NY, NZ, HALF_R, HALF_C)
    return pl.pallas_call(
        backward_kernel,
        in_specs=[SMEM, VMEM, VMEM, VMEM, HBM],
        out_specs=[VMEM] * 2,
        scratch_shapes=[
            pltpu.VMEM((hidden, width), bf16),
            pltpu.VMEM((rows, hidden), bf16),
            pltpu.VMEM((2, CHUNK, width), f32),
            pltpu.SemaphoreType.DMA((hidden // WIDE,)),
        ],
        out_shape=(jax.ShapeDtypeStruct(piece, bf16), jax.ShapeDtypeStruct(piece, bf16)),
        compiler_params=pltpu.CompilerParams(vmem_limit_bytes=24 << 20),
        cost_estimate=pl.CostEstimate(
            flops=4 * rows * width * hidden, bytes_accessed=16 << 20, transcendentals=0
        ),
        name="backward",
    )(place, grad_emb, states, slope, far(w_down))


def halves(array):
    half = array.shape[0] // 2
    return array[:half], array[half:]


def meet(keep, send, step):
    came = swap(send, step)
    keep_own, keep_next = halves(keep)
    came_own, came_next = halves(came)
    return (
        keep_own.astype(f32) + came_own.astype(f32),
        (keep_next.astype(f32) + came_next.astype(f32)).astype(bf16),
    )


def total(keep, send, step):
    return keep.astype(f32) + swap(send, step).astype(f32)


def apart(array):
    half = array.shape[0] // 2
    return array[half:], array[:half]


def sum_plane(keep, send, steps):
    next_keep, keep, next_send, send = lax.optimization_barrier((*apart(keep), *apart(send)))
    ahead, rest = swap(next_send, steps[0]), swap(send, steps[0])
    next_send, send = apart((ahead.astype(f32) + next_keep).astype(bf16))
    next_send, send = lax.optimization_barrier((next_send, send))
    ahead, rest_two = swap(next_send, steps[1]), swap(send, steps[1])
    next_keep, keep = lax.optimization_barrier(apart(keep + rest.astype(f32)))
    came = swap((ahead.astype(f32) + next_keep).astype(bf16), steps[2])
    keep = came.astype(f32) + (keep + rest_two.astype(f32))
    return swap(keep[1:].astype(bf16), steps[3]).astype(f32) + keep[:1]


def on_device(index_states, questions, reader, owners, passage_rows, w_up, w_down):
    shards = lax.axis_size("shard")
    width = questions.shape[1]
    shard, x = lax.axis_index("shard"), lax.axis_index("rep")
    z, y, c = shard >> 3, (shard >> 1) & 3, shard & 1
    place = jnp.stack([z, y, c, x]).astype(i32)

    send_rows, slot, index_near = route(owners.reshape(Q, K), passage_rows, index_states, shards)
    rows_in = lax.all_to_all(send_rows, "shard", split_axis=0, concat_axis=0, tiled=True)
    states_out = fetch(rows_in, index_near)
    got = lax.all_to_all(states_out, "shard", split_axis=0, concat_axis=0, tiled=True)
    derivative, states, grad_emb, slope, keep_down, send_down = forward(
        place, got.reshape(shards * CAP, width), slot, questions, reader, w_up, w_down
    )
    keep_up, send_up = backward(place, grad_emb, states, slope, w_down)

    down = sum_plane(*meet(keep_down, send_down, "c"), ("x1", "x2", "y1", "y2"))
    up = sum_plane(*meet(keep_up, send_up, "c"), ("y1", "y2", "x1", "x2"))
    both = jnp.concatenate([down, up])
    both = both.reshape(2, NZ, HALF_R, HALF_C).swapaxes(0, 1)
    keep, send = halves(both)
    send = send.astype(bf16)
    for step in ("z1", "z2"):
        keep, send = meet(keep, send, step)
    mine = total(keep, send, "z3")[0]

    label = label4(x, c)
    came = swap(mine, "x2")
    first = (label & 1) == 0
    mine = jnp.concatenate([jnp.where(first, mine, came), jnp.where(first, came, mine)], 1)
    came = swap(mine, "x1")
    first = (label >> 1) == 0
    mine = jnp.concatenate([jnp.where(first, mine, came), jnp.where(first, came, mine)], 2)
    return derivative, mine[1], mine[0]


def solution(mesh):
    placed = (
        P("shard", None),
        P(("shard", "rep"), None),
        P(("shard", "rep"), None),
        P(("shard", "rep"), None, None),
        P(("shard", "rep"), None),
        P(),
        P(),
    )
    return jax.shard_map(
        on_device,
        mesh=mesh,
        in_specs=placed,
        out_specs=(P(("shard", "rep"), None), P("shard", None), P("shard", None)),
        check_vma=False,
    )
```

```python
import functools
import itertools

import jax
import jax.numpy as jnp
from jax import lax
from jax.experimental import pallas as pl
from jax.experimental.pallas import tpu as pltpu
from jax.sharding import PartitionSpec as P

K = 32
Q = 8
CAP = 8
NZ, NY, NC, NX = 8, 4, 2, 4
OWN = 48
CHUNK = NY * NC * OWN
HALF_R, HALF_C = 24, 384
WIDE = 2 * CHUNK

normalizer_heat = 0.1
loss_scale = 64.0
epsilon = 1e-06
gelu_coeff = 0.7978845608028654
cubic = 0.044715

bf16, f32, i32 = jnp.bfloat16, jnp.float32, jnp.int32
AXES = ("shard", "rep")


def gray(v):
    return v ^ (v >> 1)


def low_bit(v):
    return gray(v) & 1


def high_bit(v):
    return v >> 1


def label4(v, core):
    low, high = low_bit(v), high_bit(v)
    return (low * (1 - core) + high * core) * 2 + (high * (1 - core) + low * core)


def place4(label, core):
    first, second = label >> 1, label & 1
    low, high = first * (1 - core) + second * core, second * (1 - core) + first * core
    return high * 2 + (low ^ high)


def label8(v, core):
    v = (v - core) & 7
    top = v >> 2
    return (((v & 1) ^ top) << 2) | ((((v >> 1) & 1) ^ top) << 1) | top


def partner(step):
    def meet(z, y, c, x):
        if step == "c":
            return (z, y, 1 - c, x)
        axis, turn = step[0], int(step[1]) - 1
        if axis == "z":
            mine = label8(z, c)
            other = [v for v in range(NZ) if label8(v, c) == mine ^ (4 >> turn)][0]
            return (other, y, c, x)
        at = x if axis == "x" else y
        mine = label4(at, c)
        other = [v for v in range(4) if label4(v, c) == mine ^ (2 >> turn)][0]
        return (z, y, c, other) if axis == "x" else (z, other, c, x)

    pairs = []
    for at, place in enumerate(itertools.product(range(NZ), range(NY), range(NC), range(NX))):
        z, y, c, x = meet(*place)
        pairs.append((at, ((z * NY + y) * NC + c) * NX + x))
    return pairs


def swap(array, step):
    return lax.ppermute(array, AXES, partner(step))


def column(values):
    count, width = values.shape
    spread = jnp.broadcast_to(values[:, None, :], (count, width, width))
    mask = lax.broadcasted_iota(i32, spread.shape, 1) == lax.broadcasted_iota(i32, spread.shape, 2)
    return jnp.sum(jnp.where(mask, spread, 0.0).reshape(count * width, width), -1, keepdims=True)


def uncolumn(values, width):
    spread = jnp.broadcast_to(values, (values.shape[0], width)).reshape(-1, width, width)
    mask = lax.broadcasted_iota(i32, spread.shape, 1) == lax.broadcasted_iota(i32, spread.shape, 2)
    return jnp.sum(jnp.where(mask, spread, 0.0), 1)


def dot(left, right, dims):
    return lax.dot_general(left, right, ((dims[0], dims[1]), ((), ())), preferred_element_type=f32)


def route_kernel(owner_ref, row_ref, index_hbm, send_ref, slot_ref, index_ref, sem):
    load = pltpu.make_async_copy(index_hbm, index_ref, sem)
    load.start()
    rows = Q * K
    shards = send_ref.shape[0]
    owner = column(owner_ref[...].astype(f32))
    row = column(row_ref[...].astype(f32))
    lanes = lax.broadcasted_iota(i32, (rows, shards), 1).astype(f32)
    onehot = (lanes == owner).astype(f32)
    earlier = (
        lax.broadcasted_iota(i32, (rows, rows), 1) < lax.broadcasted_iota(i32, (rows, rows), 0)
    ).astype(bf16)
    hot = onehot.astype(bf16)
    prior = dot(earlier, hot, ((1,), (0,)))
    rank = jnp.sum(prior * onehot, -1, keepdims=True)
    high = jnp.floor(row * (1.0 / 32.0))
    low = row - 32.0 * high
    at = lax.broadcasted_iota(i32, (rows, 128), 1).astype(f32) == rank
    send_high = dot(hot, jnp.where(at, high, 0.0).astype(bf16), ((0,), (0,)))
    send_low = dot(hot, jnp.where(at, low, 0.0).astype(bf16), ((0,), (0,)))
    send_ref[:, 0, :] = (32.0 * send_high + send_low).astype(i32)
    slot_ref[...] = jnp.broadcast_to(owner * CAP + rank, slot_ref.shape).astype(i32)
    load.wait()


def fetch_kernel(rows_ref, index_ref, out_ref):
    shards, cap, width = out_ref.shape
    want = rows_ref[...].astype(f32)
    spread = jnp.broadcast_to(want, (shards, cap, want.shape[2]))
    mask = lax.broadcasted_iota(i32, spread.shape, 1) == lax.broadcasted_iota(i32, spread.shape, 2)
    at = jnp.sum(jnp.where(mask, spread, 0.0).reshape(shards * cap, -1), -1, keepdims=True)
    lanes = lax.broadcasted_iota(i32, (shards * cap, index_ref.shape[0]), 1).astype(f32)
    here = (lanes == at).astype(f32).astype(bf16)
    got = dot(here, index_ref[...], ((1,), (0,)))
    out_ref[...] = got.reshape(shards, cap, width).astype(bf16)


def turn_kernel(up_hbm, up_t_ref, up_ref, sems):
    parts = sems.shape[0]
    copies = []
    for t in range(parts):
        cut = pl.ds(t * WIDE, WIDE)
        copies.append(pltpu.make_async_copy(up_hbm.at[:, cut], up_ref.at[:, cut], sems.at[t]))
        copies[t].start()
    for t in range(parts):
        cut = slice(t * WIDE, (t + 1) * WIDE)
        copies[t].wait()
        up_t_ref[cut, :] = up_ref[:, cut].T


def share_units(units_ref, core, mine_ref, other_ref, t):
    for block in range(2 * t * NY, 2 * (t + 1) * NY):
        for own, out_ref in ((core, mine_ref), (1 - core, other_ref)):
            start = pl.multiple_of(block * NC * OWN + own * OWN, 16)
            out_ref[block * OWN : (block + 1) * OWN, :] = units_ref[pl.ds(start, OWN), :]


def forward_kernel(
    place_ref, got_ref, slot_ref, question_ref, reader_ref, up_t_hbm, down_hbm,
    derivative_ref, states_ref, grad_emb_ref, slope_ref, mine_ref, pack_ref, down_ref,
    hidden_ref, up_t_ref, sems,
):
    width = question_ref.shape[1]
    parts = hidden_ref.shape[0] // WIDE
    ups, downs = [], []
    for t in range(parts):
        cut = pl.ds(t * WIDE, WIDE)
        ups.append(pltpu.make_async_copy(up_t_hbm.at[cut, :], up_t_ref.at[cut, :], sems.at[0, t]))
        downs.append(pltpu.make_async_copy(down_hbm.at[cut, :], down_ref.at[cut, :], sems.at[1, t]))
    ups[0].start()
    ups[1].start()
    lanes = lax.broadcasted_iota(i32, (Q * K, got_ref.shape[0]), 1)
    onehot = (lanes == slot_ref[:, :1]).astype(f32).astype(bf16)
    states = dot(onehot, got_ref[...], ((1,), (0,))).astype(bf16)
    states_ref[...] = states
    for t in range(parts):
        cut = slice(t * WIDE, (t + 1) * WIDE)
        ups[t].wait()
        for copy in (ups + downs)[2 * t + 2 : 2 * t + 4]:
            copy.start()
        pre = dot(up_t_ref[cut, :], states, ((1,), (1,)))
        square = pre * pre
        tangent = jnp.tanh(pre * (gelu_coeff + (gelu_coeff * cubic) * square))
        gate = 0.5 + 0.5 * tangent
        hidden_ref[cut, :] = (pre * gate).astype(bf16)
        slope_ref[cut, :] = gate + pre * (1.0 - tangent * tangent) * (
            0.5 * gelu_coeff + (1.5 * gelu_coeff * cubic) * square
        )
        share_units(hidden_ref, place_ref[2], mine_ref, pack_ref, t)
    for copy in downs:
        copy.wait()
    embedded = states.astype(f32) + dot(hidden_ref[...], down_ref[...], ((0,), (0,)))

    norms = jnp.sqrt(jnp.sum(embedded * embedded, -1, keepdims=True) + epsilon)
    unit = embedded / norms
    wide = question_ref[...].astype(f32)
    q_hat = (wide / jnp.sqrt(jnp.sum(wide * wide, -1, keepdims=True) + epsilon)).astype(bf16)
    query = jnp.broadcast_to(q_hat.astype(f32)[:, None, :], (Q, K, width)).reshape(Q * K, width)
    cosine = jnp.sum(unit * query, -1, keepdims=True)

    def share(scores):
        raised = jnp.exp(scores).reshape(Q, K, 1)
        return (raised / jnp.sum(raised, 1, keepdims=True)).reshape(Q * K, 1)

    derivative = loss_scale * (share(cosine / normalizer_heat) - share(column(reader_ref[...])))
    derivative_ref[...] = uncolumn(derivative, K)
    grad_emb = ((derivative / normalizer_heat) * (query - cosine * unit) / norms).astype(bf16)
    grad_emb_ref[...] = grad_emb
    units = mine_ref.shape[0]
    for block, array in enumerate((grad_emb, states)):
        for part in range(width // (Q * K)):
            start = units + block * width + part * Q * K
            pack_ref[start : start + Q * K, :] = array[:, part * Q * K : (part + 1) * Q * K]


def backward_kernel(place_ref, grad_emb_ref, slope_ref, down_ref, mine_ref, other_ref, grad_pre_ref):
    grad_emb = grad_emb_ref[...]
    for t in range(down_ref.shape[0] // WIDE):
        cut = slice(t * WIDE, (t + 1) * WIDE)
        grad_hidden = dot(down_ref[cut, :], grad_emb, ((1,), (1,)))
        grad_pre_ref[cut, :] = (grad_hidden * slope_ref[cut, :]).astype(bf16)
        share_units(grad_pre_ref, place_ref[2], mine_ref, other_ref, t)


def gradient_kernel(
    x_first, right_at, place_ref, mine_ref, came_ref, right_ref, pack_ref,
    next_keep_ref, keep_ref, next_send_ref, send_ref, value_ref,
):
    z, y, core, x = place_ref[0], place_ref[1], place_ref[2], place_ref[3]
    mine_x, mine_y, mine_z = label4(x, core), label4(y, core), label8(z, core)
    right = right_ref[...]
    rows, width = right.shape
    right_came = jnp.concatenate(
        [pack_ref[right_at + part * rows : right_at + (part + 1) * rows, :] for part in range(width // rows)], 1
    )
    outs = (keep_ref, next_keep_ref, send_ref, next_send_ref)
    per = 2 * NY * OWN
    spots = []
    for at in range(NX * NY):
        at_x, at_y = (at >> 2, at & 3) if x_first else (at & 3, at >> 2)
        piece, j = at_x ^ mine_x, place4(at_y ^ mine_y, core)
        spots.append((j * OWN + (piece & 1) * HALF_R, pl.multiple_of((piece >> 1) * HALF_C, 128)))
    for t in range(NZ // 2):
        cut = slice(t * per, (t + 1) * per)
        value_ref[t % 2] = dot(mine_ref[cut, :], right, ((1,), (0,))) + dot(
            came_ref[cut, :], right_came, ((1,), (0,))
        )
        for half in range(2):
            at_z = label8(2 * t + half, core) ^ mine_z
            for at, (row, column) in enumerate(spots):
                row = pl.multiple_of(half * NY * OWN + row, 8)
                out_ref = outs[at >> 2]
                out_ref[at & 3, at_z] = value_ref[
                    t % 2, pl.ds(row, HALF_R), pl.ds(column, HALF_C)
                ].astype(out_ref.dtype)


def far(array):
    return pltpu.with_memory_space_constraint(array, pltpu.HBM)


SMEM, VMEM, HBM = (
    pl.BlockSpec(memory_space=pltpu.SMEM),
    pl.BlockSpec(memory_space=pltpu.VMEM),
    pl.BlockSpec(memory_space=pltpu.HBM),
)


def route(owners, passage_rows, index_states, shards):
    return pl.pallas_call(
        route_kernel,
        in_specs=[VMEM, VMEM, HBM],
        out_specs=[VMEM] * 3,
        out_shape=(
            jax.ShapeDtypeStruct((shards, 1, 128), i32),
            jax.ShapeDtypeStruct((Q * K, 128), i32),
            pltpu.VMEM(index_states.shape, index_states.dtype),
        ),
        scratch_shapes=[pltpu.SemaphoreType.DMA],
        name="route",
    )(owners, passage_rows, far(index_states))


def fetch(rows_in, index_states):
    shards, width = rows_in.shape[0], index_states.shape[1]
    return pl.pallas_call(
        fetch_kernel,
        out_shape=jax.ShapeDtypeStruct((shards, CAP, width), bf16),
        compiler_params=pltpu.CompilerParams(vmem_limit_bytes=32 << 20),
        name="fetch",
    )(rows_in, pltpu.with_memory_space_constraint(index_states, pltpu.VMEM))


def near(array):
    return pltpu.with_memory_space_constraint(array, pltpu.VMEM)


def turn(w_up):
    width, hidden = w_up.shape
    return pl.pallas_call(
        turn_kernel,
        in_specs=[HBM],
        out_specs=VMEM,
        scratch_shapes=[pltpu.VMEM((width, hidden), bf16), pltpu.SemaphoreType.DMA((hidden // WIDE,))],
        out_shape=jax.ShapeDtypeStruct((hidden, width), bf16),
        compiler_params=pltpu.CompilerParams(vmem_limit_bytes=24 << 20),
        cost_estimate=pl.CostEstimate(flops=0, bytes_accessed=16 << 20, transcendentals=0),
        name="turn",
    )(far(w_up))


def forward(place, got, slot, questions, reader, up_t, w_down):
    hidden, width = up_t.shape
    rows = Q * K
    return pl.pallas_call(
        forward_kernel,
        in_specs=[SMEM, VMEM, VMEM, VMEM, VMEM, HBM, HBM],
        out_specs=[VMEM] * 7,
        scratch_shapes=[
            pltpu.VMEM((hidden, rows), bf16),
            pltpu.VMEM((hidden, width), bf16),
            pltpu.SemaphoreType.DMA((2, hidden // WIDE)),
        ],
        out_shape=(
            jax.ShapeDtypeStruct((Q, K), f32),
            jax.ShapeDtypeStruct((rows, width), bf16),
            jax.ShapeDtypeStruct((rows, width), bf16),
            jax.ShapeDtypeStruct((hidden, rows), f32),
            jax.ShapeDtypeStruct((hidden // NC, rows), bf16),
            jax.ShapeDtypeStruct((hidden // NC + 2 * width, rows), bf16),
            pltpu.VMEM((hidden, width), bf16),
        ),
        compiler_params=pltpu.CompilerParams(vmem_limit_bytes=24 << 20),
        cost_estimate=pl.CostEstimate(
            flops=4 * rows * width * hidden, bytes_accessed=16 << 20, transcendentals=rows * hidden
        ),
        name="forward",
    )(place, got, slot, questions, reader, far(up_t), far(w_down))


def backward(place, grad_emb, slope, w_down):
    hidden, width = w_down.shape
    rows = Q * K
    return pl.pallas_call(
        backward_kernel,
        in_specs=[SMEM] + [VMEM] * 3,
        out_specs=[VMEM] * 2,
        scratch_shapes=[pltpu.VMEM((hidden, rows), bf16)],
        out_shape=(jax.ShapeDtypeStruct((hidden // NC, rows), bf16),) * 2,
        compiler_params=pltpu.CompilerParams(vmem_limit_bytes=24 << 20),
        cost_estimate=pl.CostEstimate(
            flops=2 * rows * width * hidden, bytes_accessed=8 << 20, transcendentals=0
        ),
        name="backward",
    )(place, grad_emb, slope, near(w_down))


def gradient(place, mine, came, right, pack, right_at, x_first, name):
    rows, width = right.shape
    piece = (4, NZ, HALF_R, HALF_C)
    return pl.pallas_call(
        functools.partial(gradient_kernel, x_first, right_at),
        in_specs=[SMEM] + [VMEM] * 4,
        out_specs=[VMEM] * 4,
        scratch_shapes=[pltpu.VMEM((2, 2 * NY * OWN, width), f32)],
        out_shape=(jax.ShapeDtypeStruct(piece, f32),) * 2 + (jax.ShapeDtypeStruct(piece, bf16),) * 2,
        compiler_params=pltpu.CompilerParams(vmem_limit_bytes=24 << 20),
        cost_estimate=pl.CostEstimate(
            flops=4 * rows * width * mine.shape[0], bytes_accessed=8 << 20, transcendentals=0
        ),
        name=name,
    )(place, mine, came, right, pack)


def halves(array):
    half = array.shape[0] // 2
    return array[:half], array[half:]


def meet(keep, send, step):
    came = swap(send, step)
    keep_own, keep_next = halves(keep)
    came_own, came_next = halves(came)
    return (
        keep_own.astype(f32) + came_own.astype(f32),
        (keep_next.astype(f32) + came_next.astype(f32)).astype(bf16),
    )


def total(keep, send, step):
    return keep.astype(f32) + swap(send, step).astype(f32)


def apart(array):
    half = array.shape[0] // 2
    return array[half:], array[:half]


def sum_plane(next_keep, keep, next_send, send, steps):
    ahead, rest = swap(next_send, steps[0]), swap(send, steps[0])
    next_send, send = apart((ahead.astype(f32) + next_keep).astype(bf16))
    next_send, send = lax.optimization_barrier((next_send, send))
    ahead, rest_two = swap(next_send, steps[1]), swap(send, steps[1])
    next_keep, keep = lax.optimization_barrier(apart(keep + rest.astype(f32)))
    came = swap((ahead.astype(f32) + next_keep).astype(bf16), steps[2])
    keep = came.astype(f32) + (keep + rest_two.astype(f32))
    return swap(keep[1:].astype(bf16), steps[3]).astype(f32) + keep[:1]


def on_device(index_states, questions, reader, owners, passage_rows, w_up, w_down):
    shards = lax.axis_size("shard")
    width = questions.shape[1]
    shard, x = lax.axis_index("shard"), lax.axis_index("rep")
    z, y, c = shard >> 3, (shard >> 1) & 3, shard & 1
    place = jnp.stack([z, y, c, x]).astype(i32)

    send_rows, slot, index_near = route(owners.reshape(Q, K), passage_rows, index_states, shards)
    send_rows, place = lax.optimization_barrier((send_rows, place))
    rows_in = lax.all_to_all(send_rows, "shard", split_axis=0, concat_axis=0, tiled=True)
    states_out = fetch(rows_in, index_near)
    got = lax.all_to_all(states_out, "shard", split_axis=0, concat_axis=0, tiled=True)
    derivative, states, grad_emb, slope, hidden, pack, down = forward(
        place, got.reshape(shards * CAP, width), slot, questions, reader, turn(w_up), w_down
    )
    pack = swap(pack, "c")
    grad_pre, other = backward(place, grad_emb, slope, down)
    other = swap(other, "c")
    units = hidden.shape[0]
    down = gradient(place, hidden, pack, grad_emb, pack, units, True, "gradient_down")
    down, other = lax.optimization_barrier((down, other))
    up = gradient(place, grad_pre, other, states, pack, units + width, False, "gradient_up")
    down = sum_plane(*down, ("x1", "x2", "y1", "y2"))
    up = sum_plane(*up, ("y1", "y2", "x1", "x2"))
    both = jnp.concatenate([down, up])
    both = both.reshape(2, NZ, HALF_R, HALF_C).swapaxes(0, 1)
    keep, send = halves(both)
    send = send.astype(bf16)
    for step in ("z1", "z2"):
        keep, send = meet(keep, send, step)
    mine = total(keep, send, "z3")[0].astype(bf16)

    label = label4(x, c)
    came = swap(mine, "x2")
    first = (label & 1) == 0
    mine = jnp.concatenate([jnp.where(first, mine, came), jnp.where(first, came, mine)], 1)
    came = swap(mine, "x1")
    first = (label >> 1) == 0
    mine = jnp.concatenate([jnp.where(first, mine, came), jnp.where(first, came, mine)], 2)
    return derivative, mine[1].astype(f32), mine[0].astype(f32)


def solution(mesh):
    placed = (
        P("shard", None),
        P(("shard", "rep"), None),
        P(("shard", "rep"), None),
        P(("shard", "rep"), None, None),
        P(("shard", "rep"), None),
        P(),
        P(),
    )
    return jax.shard_map(
        on_device,
        mesh=mesh,
        in_specs=placed,
        out_specs=(P(("shard", "rep"), None), P("shard", None), P("shard", None)),
        check_vma=False,
    )
```

```python
import functools
import itertools

import jax
import jax.numpy as jnp
from jax import lax
from jax.experimental import pallas as pl
from jax.experimental.pallas import tpu as pltpu
from jax.sharding import PartitionSpec as P

K = 32
Q = 8
CAP = 8
NZ, NY, NC, NX = 8, 4, 2, 4
OWN = 48
CHUNK = NY * NC * OWN
HALF_R, HALF_C = 24, 384
WIDE = 2 * CHUNK

normalizer_heat = 0.1
loss_scale = 64.0
epsilon = 1e-06
gelu_coeff = 0.7978845608028654
cubic = 0.044715

bf16, f32, i32 = jnp.bfloat16, jnp.float32, jnp.int32
AXES = ("shard", "rep")


def gray(v):
    return v ^ (v >> 1)


def low_bit(v):
    return gray(v) & 1


def high_bit(v):
    return v >> 1


def label4(v, core):
    low, high = low_bit(v), high_bit(v)
    return (low * (1 - core) + high * core) * 2 + (high * (1 - core) + low * core)


def place4(label, core):
    first, second = label >> 1, label & 1
    low, high = first * (1 - core) + second * core, second * (1 - core) + first * core
    return high * 2 + (low ^ high)


def label8(v, core):
    v = (v - core) & 7
    top = v >> 2
    return (((v & 1) ^ top) << 2) | ((((v >> 1) & 1) ^ top) << 1) | top


def partner(step):
    def meet(z, y, c, x):
        if step == "c":
            return (z, y, 1 - c, x)
        axis, turn = step[0], int(step[1]) - 1
        if axis == "z":
            mine = label8(z, c)
            other = [v for v in range(NZ) if label8(v, c) == mine ^ (4 >> turn)][0]
            return (other, y, c, x)
        at = x if axis == "x" else y
        mine = label4(at, c)
        other = [v for v in range(4) if label4(v, c) == mine ^ (2 >> turn)][0]
        return (z, y, c, other) if axis == "x" else (z, other, c, x)

    pairs = []
    for at, place in enumerate(itertools.product(range(NZ), range(NY), range(NC), range(NX))):
        z, y, c, x = meet(*place)
        pairs.append((at, ((z * NY + y) * NC + c) * NX + x))
    return pairs


def swap(array, step):
    return lax.ppermute(array, AXES, partner(step))


def column(values):
    count, width = values.shape
    spread = jnp.broadcast_to(values[:, None, :], (count, width, width))
    mask = lax.broadcasted_iota(i32, spread.shape, 1) == lax.broadcasted_iota(i32, spread.shape, 2)
    return jnp.sum(jnp.where(mask, spread, 0.0).reshape(count * width, width), -1, keepdims=True)


def uncolumn(values, width):
    spread = jnp.broadcast_to(values, (values.shape[0], width)).reshape(-1, width, width)
    mask = lax.broadcasted_iota(i32, spread.shape, 1) == lax.broadcasted_iota(i32, spread.shape, 2)
    return jnp.sum(jnp.where(mask, spread, 0.0), 1)


def dot(left, right, dims):
    return lax.dot_general(left, right, ((dims[0], dims[1]), ((), ())), preferred_element_type=f32)


def route_kernel(owner_ref, row_ref, index_hbm, send_ref, slot_ref, index_ref, sem):
    load = pltpu.make_async_copy(index_hbm, index_ref, sem)
    load.start()
    rows = Q * K
    shards = send_ref.shape[0]
    owner = column(owner_ref[...].astype(f32))
    row = column(row_ref[...].astype(f32))
    lanes = lax.broadcasted_iota(i32, (rows, shards), 1).astype(f32)
    onehot = (lanes == owner).astype(f32)
    earlier = (
        lax.broadcasted_iota(i32, (rows, rows), 1) < lax.broadcasted_iota(i32, (rows, rows), 0)
    ).astype(bf16)
    hot = onehot.astype(bf16)
    prior = dot(earlier, hot, ((1,), (0,)))
    rank = jnp.sum(prior * onehot, -1, keepdims=True)
    high = jnp.floor(row * (1.0 / 32.0))
    low = row - 32.0 * high
    at = lax.broadcasted_iota(i32, (rows, 128), 1).astype(f32) == rank
    send_high = dot(hot, jnp.where(at, high, 0.0).astype(bf16), ((0,), (0,)))
    send_low = dot(hot, jnp.where(at, low, 0.0).astype(bf16), ((0,), (0,)))
    send_ref[:, 0, :] = (32.0 * send_high + send_low).astype(i32)
    slot_ref[...] = jnp.broadcast_to(owner * CAP + rank, slot_ref.shape).astype(i32)
    load.wait()


def fetch_kernel(rows_ref, index_ref, out_ref):
    shards, cap, width = out_ref.shape
    want = rows_ref[...].astype(f32)
    spread = jnp.broadcast_to(want, (shards, cap, want.shape[2]))
    mask = lax.broadcasted_iota(i32, spread.shape, 1) == lax.broadcasted_iota(i32, spread.shape, 2)
    at = jnp.sum(jnp.where(mask, spread, 0.0).reshape(shards * cap, -1), -1, keepdims=True)
    lanes = lax.broadcasted_iota(i32, (shards * cap, index_ref.shape[0]), 1).astype(f32)
    here = (lanes == at).astype(f32).astype(bf16)
    got = dot(here, index_ref[...], ((1,), (0,)))
    out_ref[...] = got.reshape(shards, cap, width).astype(bf16)


def turn_kernel(up_hbm, up_t_ref, up_ref, sems):
    parts = sems.shape[0]
    copies = []
    for t in range(parts):
        cut = pl.ds(t * WIDE, WIDE)
        copies.append(pltpu.make_async_copy(up_hbm.at[:, cut], up_ref.at[:, cut], sems.at[t]))
        copies[t].start()
    for t in range(parts):
        cut = slice(t * WIDE, (t + 1) * WIDE)
        copies[t].wait()
        up_t_ref[cut, :] = up_ref[:, cut].T


def share_units(units_ref, core, mine_ref, other_ref, t):
    for block in range(2 * t * NY, 2 * (t + 1) * NY):
        for own, out_ref in ((core, mine_ref), (1 - core, other_ref)):
            start = pl.multiple_of(block * NC * OWN + own * OWN, 16)
            out_ref[block * OWN : (block + 1) * OWN, :] = units_ref[pl.ds(start, OWN), :]


def forward_kernel(
    place_ref, got_ref, slot_ref, question_ref, reader_ref, up_t_hbm, down_hbm,
    derivative_ref, states_ref, grad_emb_ref, slope_ref, mine_ref, pack_ref, down_ref,
    hidden_ref, up_t_ref, sems,
):
    width = question_ref.shape[1]
    parts = hidden_ref.shape[0] // WIDE
    ups, downs = [], []
    for t in range(parts):
        cut = pl.ds(t * WIDE, WIDE)
        ups.append(pltpu.make_async_copy(up_t_hbm.at[cut, :], up_t_ref.at[cut, :], sems.at[0, t]))
        downs.append(pltpu.make_async_copy(down_hbm.at[cut, :], down_ref.at[cut, :], sems.at[1, t]))
    ups[0].start()
    ups[1].start()
    lanes = lax.broadcasted_iota(i32, (Q * K, got_ref.shape[0]), 1)
    onehot = (lanes == slot_ref[:, :1]).astype(f32).astype(bf16)
    states = dot(onehot, got_ref[...], ((1,), (0,))).astype(bf16)
    states_ref[...] = states
    for t in range(parts):
        cut = slice(t * WIDE, (t + 1) * WIDE)
        ups[t].wait()
        for copy in (ups + downs)[2 * t + 2 : 2 * t + 4]:
            copy.start()
        pre = dot(up_t_ref[cut, :], states, ((1,), (1,)))
        square = pre * pre
        tangent = jnp.tanh(pre * (gelu_coeff + (gelu_coeff * cubic) * square))
        gate = 0.5 + 0.5 * tangent
        hidden_ref[cut, :] = (pre * gate).astype(bf16)
        slope_ref[cut, :] = gate + pre * (1.0 - tangent * tangent) * (
            0.5 * gelu_coeff + (1.5 * gelu_coeff * cubic) * square
        )
        share_units(hidden_ref, place_ref[2], mine_ref, pack_ref, t)
    for copy in downs:
        copy.wait()
    embedded = states.astype(f32) + dot(hidden_ref[...], down_ref[...], ((0,), (0,)))

    norms = jnp.sqrt(jnp.sum(embedded * embedded, -1, keepdims=True) + epsilon)
    unit = embedded / norms
    wide = question_ref[...].astype(f32)
    q_hat = (wide / jnp.sqrt(jnp.sum(wide * wide, -1, keepdims=True) + epsilon)).astype(bf16)
    query = jnp.broadcast_to(q_hat.astype(f32)[:, None, :], (Q, K, width)).reshape(Q * K, width)
    cosine = jnp.sum(unit * query, -1, keepdims=True)

    def share(scores):
        raised = jnp.exp(scores).reshape(Q, K, 1)
        return (raised / jnp.sum(raised, 1, keepdims=True)).reshape(Q * K, 1)

    derivative = loss_scale * (share(cosine / normalizer_heat) - share(column(reader_ref[...])))
    derivative_ref[...] = uncolumn(derivative, K)
    grad_emb = ((derivative / normalizer_heat) * (query - cosine * unit) / norms).astype(bf16)
    grad_emb_ref[...] = grad_emb
    units = mine_ref.shape[0]
    for block, array in enumerate((grad_emb, states)):
        for part in range(width // (Q * K)):
            start = units + block * width + part * Q * K
            pack_ref[start : start + Q * K, :] = array[:, part * Q * K : (part + 1) * Q * K]


def backward_kernel(place_ref, grad_emb_ref, slope_ref, down_ref, mine_ref, other_ref, grad_pre_ref):
    grad_emb = grad_emb_ref[...]
    for t in range(down_ref.shape[0] // WIDE):
        cut = slice(t * WIDE, (t + 1) * WIDE)
        grad_hidden = dot(down_ref[cut, :], grad_emb, ((1,), (1,)))
        grad_pre_ref[cut, :] = (grad_hidden * slope_ref[cut, :]).astype(bf16)
        share_units(grad_pre_ref, place_ref[2], mine_ref, other_ref, t)


def gradient_kernel(
    x_first, right_at, place_ref, mine_ref, came_ref, right_ref, pack_ref,
    next_keep_ref, keep_ref, next_send_ref, send_ref, value_ref,
):
    z, y, core, x = place_ref[0], place_ref[1], place_ref[2], place_ref[3]
    mine_x, mine_y, mine_z = label4(x, core), label4(y, core), label8(z, core)
    right = right_ref[...]
    rows, width = right.shape
    right_came = jnp.concatenate(
        [pack_ref[right_at + part * rows : right_at + (part + 1) * rows, :] for part in range(width // rows)], 1
    )
    outs = (keep_ref, next_keep_ref, send_ref, next_send_ref)
    per = 2 * NY * OWN
    spots = []
    for at in range(NX * NY):
        at_x, at_y = (at >> 2, at & 3) if x_first else (at & 3, at >> 2)
        piece, j = at_x ^ mine_x, place4(at_y ^ mine_y, core)
        spots.append((j * OWN + (piece & 1) * HALF_R, pl.multiple_of((piece >> 1) * HALF_C, 128)))
    for t in range(NZ // 2):
        cut = slice(t * per, (t + 1) * per)
        value_ref[t % 2] = dot(mine_ref[cut, :], right, ((1,), (0,))) + dot(
            came_ref[cut, :], right_came, ((1,), (0,))
        )
        for half in range(2):
            at_z = label8(2 * t + half, core) ^ mine_z
            for at, (row, column) in enumerate(spots):
                row = pl.multiple_of(half * NY * OWN + row, 8)
                out_ref = outs[at >> 2]
                out_ref[at & 3, at_z] = value_ref[
                    t % 2, pl.ds(row, HALF_R), pl.ds(column, HALF_C)
                ].astype(out_ref.dtype)


def far(array):
    return pltpu.with_memory_space_constraint(array, pltpu.HBM)


SMEM, VMEM, HBM = (
    pl.BlockSpec(memory_space=pltpu.SMEM),
    pl.BlockSpec(memory_space=pltpu.VMEM),
    pl.BlockSpec(memory_space=pltpu.HBM),
)


def route(owners, passage_rows, index_states, shards):
    return pl.pallas_call(
        route_kernel,
        in_specs=[VMEM, VMEM, HBM],
        out_specs=[VMEM] * 3,
        out_shape=(
            jax.ShapeDtypeStruct((shards, 1, 128), i32),
            jax.ShapeDtypeStruct((Q * K, 128), i32),
            pltpu.VMEM(index_states.shape, index_states.dtype),
        ),
        scratch_shapes=[pltpu.SemaphoreType.DMA],
        name="route",
    )(owners, passage_rows, far(index_states))


def fetch(rows_in, index_states):
    shards, width = rows_in.shape[0], index_states.shape[1]
    return pl.pallas_call(
        fetch_kernel,
        out_shape=jax.ShapeDtypeStruct((shards, CAP, width), bf16),
        compiler_params=pltpu.CompilerParams(vmem_limit_bytes=32 << 20),
        name="fetch",
    )(rows_in, pltpu.with_memory_space_constraint(index_states, pltpu.VMEM))


def near(array):
    return pltpu.with_memory_space_constraint(array, pltpu.VMEM)


def turn(w_up):
    width, hidden = w_up.shape
    return pl.pallas_call(
        turn_kernel,
        in_specs=[HBM],
        out_specs=VMEM,
        scratch_shapes=[pltpu.VMEM((width, hidden), bf16), pltpu.SemaphoreType.DMA((hidden // WIDE,))],
        out_shape=jax.ShapeDtypeStruct((hidden, width), bf16),
        compiler_params=pltpu.CompilerParams(vmem_limit_bytes=24 << 20),
        cost_estimate=pl.CostEstimate(flops=0, bytes_accessed=16 << 20, transcendentals=0),
        name="turn",
    )(far(w_up))


def forward(place, got, slot, questions, reader, up_t, w_down):
    hidden, width = up_t.shape
    rows = Q * K
    return pl.pallas_call(
        forward_kernel,
        in_specs=[SMEM, VMEM, VMEM, VMEM, VMEM, HBM, HBM],
        out_specs=[VMEM] * 7,
        scratch_shapes=[
            pltpu.VMEM((hidden, rows), bf16),
            pltpu.VMEM((hidden, width), bf16),
            pltpu.SemaphoreType.DMA((2, hidden // WIDE)),
        ],
        out_shape=(
            jax.ShapeDtypeStruct((Q, K), f32),
            jax.ShapeDtypeStruct((rows, width), bf16),
            jax.ShapeDtypeStruct((rows, width), bf16),
            jax.ShapeDtypeStruct((hidden, rows), f32),
            jax.ShapeDtypeStruct((hidden // NC, rows), bf16),
            jax.ShapeDtypeStruct((hidden // NC + 2 * width, rows), bf16),
            pltpu.VMEM((hidden, width), bf16),
        ),
        compiler_params=pltpu.CompilerParams(vmem_limit_bytes=24 << 20),
        cost_estimate=pl.CostEstimate(
            flops=4 * rows * width * hidden, bytes_accessed=16 << 20, transcendentals=rows * hidden
        ),
        name="forward",
    )(place, got, slot, questions, reader, far(up_t), far(w_down))


def backward(place, grad_emb, slope, w_down):
    hidden, width = w_down.shape
    rows = Q * K
    return pl.pallas_call(
        backward_kernel,
        in_specs=[SMEM] + [VMEM] * 3,
        out_specs=[VMEM] * 2,
        scratch_shapes=[pltpu.VMEM((hidden, rows), bf16)],
        out_shape=(jax.ShapeDtypeStruct((hidden // NC, rows), bf16),) * 2,
        compiler_params=pltpu.CompilerParams(vmem_limit_bytes=24 << 20),
        cost_estimate=pl.CostEstimate(
            flops=2 * rows * width * hidden, bytes_accessed=8 << 20, transcendentals=0
        ),
        name="backward",
    )(place, grad_emb, slope, near(w_down))


def gradient(place, mine, came, right, pack, right_at, x_first, name):
    rows, width = right.shape
    piece = (4, NZ, HALF_R, HALF_C)
    return pl.pallas_call(
        functools.partial(gradient_kernel, x_first, right_at),
        in_specs=[SMEM] + [VMEM] * 4,
        out_specs=[VMEM] * 4,
        scratch_shapes=[pltpu.VMEM((2, 2 * NY * OWN, width), f32)],
        out_shape=(jax.ShapeDtypeStruct(piece, f32),) * 2 + (jax.ShapeDtypeStruct(piece, bf16),) * 2,
        compiler_params=pltpu.CompilerParams(vmem_limit_bytes=24 << 20),
        cost_estimate=pl.CostEstimate(
            flops=4 * rows * width * mine.shape[0], bytes_accessed=8 << 20, transcendentals=0
        ),
        name=name,
    )(place, mine, came, right, pack)


def halves(array):
    half = array.shape[0] // 2
    return array[:half], array[half:]


def meet(keep, send, step):
    came = swap(send, step)
    keep_own, keep_next = halves(keep)
    came_own, came_next = halves(came)
    return (
        keep_own.astype(f32) + came_own.astype(f32),
        (keep_next.astype(f32) + came_next.astype(f32)).astype(bf16),
    )


def total(keep, send, step):
    return keep.astype(f32) + swap(send, step).astype(f32)


def apart(array):
    half = array.shape[0] // 2
    return array[half:], array[:half]


def after(array, other):
    return lax.optimization_barrier((array, other))[0]


def sum_planes(down, up):
    plans = (("x1", "x2", "y1", "y2"), ("y1", "y2", "x1", "x2"))
    both = list(zip((down, up), plans))
    first = [(swap(chain[2], plan[0]), swap(chain[3], plan[0])) for chain, plan in both]
    ahead, sends = [], []
    for ((next_keep, *_), plan), (came, _) in zip(both, first):
        next_send, send = lax.optimization_barrier(apart((came.astype(f32) + next_keep).astype(bf16)))
        ahead.append(swap(next_send, plan[1]))
        sends.append((next_send, send))
    keeps, rest = [], []
    for at, (((_, keep, *_), plan), (_, came)) in enumerate(zip(both, first)):
        came = after(came, sends[1][0])
        next_keep, keep = apart(keep + came.astype(f32))
        next_keep, keep, send = lax.optimization_barrier((next_keep, keep, sends[at][1]))
        rest.append(swap(send, plan[1]))
        keeps.append((next_keep, keep))
    sends = [(ahead[at].astype(f32) + keeps[at][0]).astype(bf16) for at in range(2)]
    third = [swap(sends[at], plan[2]) for at, (_, plan) in enumerate(both)]
    sums = []
    for at, (_, plan) in enumerate(both):
        keep = after(third[at], sends[1]).astype(f32) + (keeps[at][1] + rest[at].astype(f32))
        sums.append(swap(keep[1:].astype(bf16), plan[3]).astype(f32) + keep[:1])
    return sums


def on_device(index_states, questions, reader, owners, passage_rows, w_up, w_down):
    shards = lax.axis_size("shard")
    width = questions.shape[1]
    shard, x = lax.axis_index("shard"), lax.axis_index("rep")
    z, y, c = shard >> 3, (shard >> 1) & 3, shard & 1
    place = jnp.stack([z, y, c, x]).astype(i32)

    send_rows, slot, index_near = route(owners.reshape(Q, K), passage_rows, index_states, shards)
    send_rows, place = lax.optimization_barrier((send_rows, place))
    rows_in = lax.all_to_all(send_rows, "shard", split_axis=0, concat_axis=0, tiled=True)
    states_out = fetch(rows_in, index_near)
    got = lax.all_to_all(states_out, "shard", split_axis=0, concat_axis=0, tiled=True)
    derivative, states, grad_emb, slope, hidden, pack, down = forward(
        place, got.reshape(shards * CAP, width), slot, questions, reader, turn(w_up), w_down
    )
    pack = swap(pack, "c")
    grad_pre, other = backward(place, grad_emb, slope, down)
    other = swap(other, "c")
    units = hidden.shape[0]
    down = gradient(place, hidden, pack, grad_emb, pack, units, True, "gradient_down")
    down, other = lax.optimization_barrier((down, other))
    up = gradient(place, grad_pre, other, states, pack, units + width, False, "gradient_up")
    both = jnp.concatenate(sum_planes(down, up))
    both = both.reshape(2, NZ, HALF_R, HALF_C).swapaxes(0, 1)
    keep, send = halves(both)
    send = send.astype(bf16)
    for step in ("z1", "z2"):
        keep, send = meet(keep, send, step)
    mine = total(keep, send, "z3")[0].astype(bf16)

    label = label4(x, c)
    came = swap(mine, "x2")
    first = (label & 1) == 0
    mine = jnp.concatenate([jnp.where(first, mine, came), jnp.where(first, came, mine)], 1)
    came = swap(mine, "x1")
    first = (label >> 1) == 0
    mine = jnp.concatenate([jnp.where(first, mine, came), jnp.where(first, came, mine)], 2)
    return derivative, mine[1].astype(f32), mine[0].astype(f32)


def solution(mesh):
    placed = (
        P("shard", None),
        P(("shard", "rep"), None),
        P(("shard", "rep"), None),
        P(("shard", "rep"), None, None),
        P(("shard", "rep"), None),
        P(),
        P(),
    )
    return jax.shard_map(
        on_device,
        mesh=mesh,
        in_specs=placed,
        out_specs=(P(("shard", "rep"), None), P("shard", None), P("shard", None)),
        check_vma=False,
    )
```

```python
import functools
import itertools

import jax
import jax.numpy as jnp
from jax import lax
from jax.experimental import pallas as pl
from jax.experimental.pallas import tpu as pltpu
from jax.sharding import PartitionSpec as P

K = 32
Q = 8
CAP = 8
NZ, NY, NC, NX = 8, 4, 2, 4
OWN = 48
CHUNK = NY * NC * OWN
HALF_R, HALF_C = 24, 384
WIDE = 2 * CHUNK

normalizer_heat = 0.1
loss_scale = 64.0
epsilon = 1e-06
gelu_coeff = 0.7978845608028654
cubic = 0.044715

bf16, f32, i32 = jnp.bfloat16, jnp.float32, jnp.int32
AXES = ("shard", "rep")


def gray(v):
    return v ^ (v >> 1)


def low_bit(v):
    return gray(v) & 1


def high_bit(v):
    return v >> 1


def label4(v, core):
    low, high = low_bit(v), high_bit(v)
    return (low * (1 - core) + high * core) * 2 + (high * (1 - core) + low * core)


def place4(label, core):
    first, second = label >> 1, label & 1
    low, high = first * (1 - core) + second * core, second * (1 - core) + first * core
    return high * 2 + (low ^ high)


def label8(v, core):
    v = (v - core) & 7
    top = v >> 2
    return (((v & 1) ^ top) << 2) | ((((v >> 1) & 1) ^ top) << 1) | top


def partner(step):
    def meet(z, y, c, x):
        if step == "c":
            return (z, y, 1 - c, x)
        axis, turn = step[0], int(step[1]) - 1
        if axis == "z":
            mine = label8(z, c)
            other = [v for v in range(NZ) if label8(v, c) == mine ^ (4 >> turn)][0]
            return (other, y, c, x)
        at = x if axis == "x" else y
        mine = label4(at, c)
        other = [v for v in range(4) if label4(v, c) == mine ^ (2 >> turn)][0]
        return (z, y, c, other) if axis == "x" else (z, other, c, x)

    pairs = []
    for at, place in enumerate(itertools.product(range(NZ), range(NY), range(NC), range(NX))):
        z, y, c, x = meet(*place)
        pairs.append((at, ((z * NY + y) * NC + c) * NX + x))
    return pairs


def swap(array, step):
    return lax.ppermute(array, AXES, partner(step))


def column(values):
    count, width = values.shape
    spread = jnp.broadcast_to(values[:, None, :], (count, width, width))
    mask = lax.broadcasted_iota(i32, spread.shape, 1) == lax.broadcasted_iota(i32, spread.shape, 2)
    return jnp.sum(jnp.where(mask, spread, 0.0).reshape(count * width, width), -1, keepdims=True)


def uncolumn(values, width):
    spread = jnp.broadcast_to(values, (values.shape[0], width)).reshape(-1, width, width)
    mask = lax.broadcasted_iota(i32, spread.shape, 1) == lax.broadcasted_iota(i32, spread.shape, 2)
    return jnp.sum(jnp.where(mask, spread, 0.0), 1)


def dot(left, right, dims):
    return lax.dot_general(left, right, ((dims[0], dims[1]), ((), ())), preferred_element_type=f32)


def route_kernel(owner_ref, row_ref, index_hbm, send_ref, slot_ref, index_ref, sem):
    load = pltpu.make_async_copy(index_hbm, index_ref, sem)
    load.start()
    rows = Q * K
    shards = send_ref.shape[0]
    owner = column(owner_ref[...].astype(f32))
    row = column(row_ref[...].astype(f32))
    lanes = lax.broadcasted_iota(i32, (rows, shards), 1).astype(f32)
    onehot = (lanes == owner).astype(f32)
    earlier = (
        lax.broadcasted_iota(i32, (rows, rows), 1) < lax.broadcasted_iota(i32, (rows, rows), 0)
    ).astype(bf16)
    hot = onehot.astype(bf16)
    prior = dot(earlier, hot, ((1,), (0,)))
    rank = jnp.sum(prior * onehot, -1, keepdims=True)
    high = jnp.floor(row * (1.0 / 32.0))
    low = row - 32.0 * high
    at = lax.broadcasted_iota(i32, (rows, 128), 1).astype(f32) == rank
    send_high = dot(hot, jnp.where(at, high, 0.0).astype(bf16), ((0,), (0,)))
    send_low = dot(hot, jnp.where(at, low, 0.0).astype(bf16), ((0,), (0,)))
    send_ref[:, 0, :] = (32.0 * send_high + send_low).astype(i32)
    slot_ref[...] = jnp.broadcast_to(owner * CAP + rank, slot_ref.shape).astype(i32)
    load.wait()


def fetch_kernel(rows_ref, index_ref, out_ref):
    shards, cap, width = out_ref.shape
    want = rows_ref[...].astype(f32)
    spread = jnp.broadcast_to(want, (shards, cap, want.shape[2]))
    mask = lax.broadcasted_iota(i32, spread.shape, 1) == lax.broadcasted_iota(i32, spread.shape, 2)
    at = jnp.sum(jnp.where(mask, spread, 0.0).reshape(shards * cap, -1), -1, keepdims=True)
    lanes = lax.broadcasted_iota(i32, (shards * cap, index_ref.shape[0]), 1).astype(f32)
    here = (lanes == at).astype(f32).astype(bf16)
    got = dot(here, index_ref[...], ((1,), (0,)))
    out_ref[...] = got.reshape(shards, cap, width).astype(bf16)


def turn_kernel(up_hbm, up_t_ref, up_ref, sems):
    parts = sems.shape[0]
    copies = []
    for t in range(parts):
        cut = pl.ds(t * WIDE, WIDE)
        copies.append(pltpu.make_async_copy(up_hbm.at[:, cut], up_ref.at[:, cut], sems.at[t]))
        copies[t].start()
    for t in range(parts):
        cut = slice(t * WIDE, (t + 1) * WIDE)
        copies[t].wait()
        up_t_ref[cut, :] = up_ref[:, cut].T


def share_units(units_ref, core, mine_ref, other_ref, t):
    for block in range(2 * t * NY, 2 * (t + 1) * NY):
        for own, out_ref in ((core, mine_ref), (1 - core, other_ref)):
            start = pl.multiple_of(block * NC * OWN + own * OWN, 16)
            out_ref[block * OWN : (block + 1) * OWN, :] = units_ref[pl.ds(start, OWN), :]


def forward_kernel(
    place_ref, got_ref, slot_ref, question_ref, reader_ref, up_t_hbm, down_hbm,
    derivative_ref, states_ref, grad_emb_ref, slope_ref, mine_ref, pack_ref, down_ref,
    hidden_ref, up_t_ref, sems,
):
    width = question_ref.shape[1]
    parts = hidden_ref.shape[0] // WIDE
    ups, downs = [], []
    for t in range(parts):
        cut = pl.ds(t * WIDE, WIDE)
        ups.append(pltpu.make_async_copy(up_t_hbm.at[cut, :], up_t_ref.at[cut, :], sems.at[0, t]))
        downs.append(pltpu.make_async_copy(down_hbm.at[cut, :], down_ref.at[cut, :], sems.at[1, t]))
    ups[0].start()
    ups[1].start()
    lanes = lax.broadcasted_iota(i32, (Q * K, got_ref.shape[0]), 1)
    onehot = (lanes == slot_ref[:, :1]).astype(f32).astype(bf16)
    states = dot(onehot, got_ref[...], ((1,), (0,))).astype(bf16)
    states_ref[...] = states
    for t in range(parts):
        cut = slice(t * WIDE, (t + 1) * WIDE)
        ups[t].wait()
        for copy in (ups + downs)[2 * t + 2 : 2 * t + 4]:
            copy.start()
        pre = dot(up_t_ref[cut, :], states, ((1,), (1,)))
        square = pre * pre
        tangent = jnp.tanh(pre * (gelu_coeff + (gelu_coeff * cubic) * square))
        gate = 0.5 + 0.5 * tangent
        hidden_ref[cut, :] = (pre * gate).astype(bf16)
        slope_ref[cut, :] = gate + pre * (1.0 - tangent * tangent) * (
            0.5 * gelu_coeff + (1.5 * gelu_coeff * cubic) * square
        )
        share_units(hidden_ref, place_ref[2], mine_ref, pack_ref, t)
    for copy in downs:
        copy.wait()
    embedded = states.astype(f32) + dot(hidden_ref[...], down_ref[...], ((0,), (0,)))

    norms = jnp.sqrt(jnp.sum(embedded * embedded, -1, keepdims=True) + epsilon)
    unit = embedded / norms
    wide = question_ref[...].astype(f32)
    q_hat = (wide / jnp.sqrt(jnp.sum(wide * wide, -1, keepdims=True) + epsilon)).astype(bf16)
    query = jnp.broadcast_to(q_hat.astype(f32)[:, None, :], (Q, K, width)).reshape(Q * K, width)
    cosine = jnp.sum(unit * query, -1, keepdims=True)

    def share(scores):
        raised = jnp.exp(scores).reshape(Q, K, 1)
        return (raised / jnp.sum(raised, 1, keepdims=True)).reshape(Q * K, 1)

    derivative = loss_scale * (share(cosine / normalizer_heat) - share(column(reader_ref[...])))
    derivative_ref[...] = uncolumn(derivative, K)
    grad_emb = ((derivative / normalizer_heat) * (query - cosine * unit) / norms).astype(bf16)
    grad_emb_ref[...] = grad_emb
    units = mine_ref.shape[0]
    for block, array in enumerate((grad_emb, states)):
        for part in range(width // (Q * K)):
            start = units + block * width + part * Q * K
            pack_ref[start : start + Q * K, :] = array[:, part * Q * K : (part + 1) * Q * K]


def backward_kernel(place_ref, grad_emb_ref, slope_ref, down_ref, mine_ref, other_ref, grad_pre_ref):
    grad_emb = grad_emb_ref[...]
    for t in range(down_ref.shape[0] // WIDE):
        cut = slice(t * WIDE, (t + 1) * WIDE)
        grad_hidden = dot(down_ref[cut, :], grad_emb, ((1,), (1,)))
        grad_pre_ref[cut, :] = (grad_hidden * slope_ref[cut, :]).astype(bf16)
        share_units(grad_pre_ref, place_ref[2], mine_ref, other_ref, t)


def gradient_kernel(
    x_first, right_at, place_ref, mine_ref, came_ref, right_ref, pack_ref,
    next_keep_ref, keep_ref, next_send_ref, send_ref, value_ref,
):
    z, y, core, x = place_ref[0], place_ref[1], place_ref[2], place_ref[3]
    mine_x, mine_y, mine_z = label4(x, core), label4(y, core), label8(z, core)
    right = right_ref[...]
    rows, width = right.shape
    right_came = jnp.concatenate(
        [pack_ref[right_at + part * rows : right_at + (part + 1) * rows, :] for part in range(width // rows)], 1
    )
    outs = (keep_ref, next_keep_ref, send_ref, next_send_ref)
    per = 2 * NY * OWN
    spots = []
    for at in range(NX * NY):
        at_x, at_y = (at >> 2, at & 3) if x_first else (at & 3, at >> 2)
        piece, j = at_x ^ mine_x, place4(at_y ^ mine_y, core)
        spots.append((j * OWN + (piece & 1) * HALF_R, pl.multiple_of((piece >> 1) * HALF_C, 128)))
    for t in range(NZ // 2):
        cut = slice(t * per, (t + 1) * per)
        value_ref[t % 2] = dot(mine_ref[cut, :], right, ((1,), (0,))) + dot(
            came_ref[cut, :], right_came, ((1,), (0,))
        )
        for half in range(2):
            at_z = label8(2 * t + half, core) ^ mine_z
            for at, (row, column) in enumerate(spots):
                row = pl.multiple_of(half * NY * OWN + row, 8)
                out_ref = outs[at >> 2]
                out_ref[at & 3, at_z] = value_ref[
                    t % 2, pl.ds(row, HALF_R), pl.ds(column, HALF_C)
                ].astype(out_ref.dtype)


def far(array):
    return pltpu.with_memory_space_constraint(array, pltpu.HBM)


SMEM, VMEM, HBM = (
    pl.BlockSpec(memory_space=pltpu.SMEM),
    pl.BlockSpec(memory_space=pltpu.VMEM),
    pl.BlockSpec(memory_space=pltpu.HBM),
)


def route(owners, passage_rows, index_states, shards):
    return pl.pallas_call(
        route_kernel,
        in_specs=[VMEM, VMEM, HBM],
        out_specs=[VMEM] * 3,
        out_shape=(
            jax.ShapeDtypeStruct((shards, 1, 128), i32),
            jax.ShapeDtypeStruct((Q * K, 128), i32),
            pltpu.VMEM(index_states.shape, index_states.dtype),
        ),
        scratch_shapes=[pltpu.SemaphoreType.DMA],
        name="route",
    )(owners, passage_rows, far(index_states))


def fetch(rows_in, index_states):
    shards, width = rows_in.shape[0], index_states.shape[1]
    return pl.pallas_call(
        fetch_kernel,
        out_shape=jax.ShapeDtypeStruct((shards, CAP, width), bf16),
        compiler_params=pltpu.CompilerParams(vmem_limit_bytes=32 << 20),
        name="fetch",
    )(rows_in, pltpu.with_memory_space_constraint(index_states, pltpu.VMEM))


def near(array):
    return pltpu.with_memory_space_constraint(array, pltpu.VMEM)


def turn(w_up):
    width, hidden = w_up.shape
    return pl.pallas_call(
        turn_kernel,
        in_specs=[HBM],
        out_specs=VMEM,
        scratch_shapes=[pltpu.VMEM((width, hidden), bf16), pltpu.SemaphoreType.DMA((hidden // WIDE,))],
        out_shape=jax.ShapeDtypeStruct((hidden, width), bf16),
        compiler_params=pltpu.CompilerParams(vmem_limit_bytes=24 << 20),
        cost_estimate=pl.CostEstimate(flops=0, bytes_accessed=16 << 20, transcendentals=0),
        name="turn",
    )(far(w_up))


def forward(place, got, slot, questions, reader, up_t, w_down):
    hidden, width = up_t.shape
    rows = Q * K
    return pl.pallas_call(
        forward_kernel,
        in_specs=[SMEM, VMEM, VMEM, VMEM, VMEM, HBM, HBM],
        out_specs=[VMEM] * 7,
        scratch_shapes=[
            pltpu.VMEM((hidden, rows), bf16),
            pltpu.VMEM((hidden, width), bf16),
            pltpu.SemaphoreType.DMA((2, hidden // WIDE)),
        ],
        out_shape=(
            jax.ShapeDtypeStruct((Q, K), f32),
            jax.ShapeDtypeStruct((rows, width), bf16),
            jax.ShapeDtypeStruct((rows, width), bf16),
            jax.ShapeDtypeStruct((hidden, rows), f32),
            jax.ShapeDtypeStruct((hidden // NC, rows), bf16),
            jax.ShapeDtypeStruct((hidden // NC + 2 * width, rows), bf16),
            pltpu.VMEM((hidden, width), bf16),
        ),
        compiler_params=pltpu.CompilerParams(vmem_limit_bytes=24 << 20),
        cost_estimate=pl.CostEstimate(
            flops=4 * rows * width * hidden, bytes_accessed=16 << 20, transcendentals=rows * hidden
        ),
        name="forward",
    )(place, got, slot, questions, reader, far(up_t), far(w_down))


def backward(place, grad_emb, slope, w_down):
    hidden, width = w_down.shape
    rows = Q * K
    return pl.pallas_call(
        backward_kernel,
        in_specs=[SMEM] + [VMEM] * 3,
        out_specs=[VMEM] * 2,
        scratch_shapes=[pltpu.VMEM((hidden, rows), bf16)],
        out_shape=(jax.ShapeDtypeStruct((hidden // NC, rows), bf16),) * 2,
        compiler_params=pltpu.CompilerParams(vmem_limit_bytes=24 << 20),
        cost_estimate=pl.CostEstimate(
            flops=2 * rows * width * hidden, bytes_accessed=8 << 20, transcendentals=0
        ),
        name="backward",
    )(place, grad_emb, slope, near(w_down))


def gradient(place, mine, came, right, pack, right_at, x_first, name):
    rows, width = right.shape
    piece = (4, NZ, HALF_R, HALF_C)
    return pl.pallas_call(
        functools.partial(gradient_kernel, x_first, right_at),
        in_specs=[SMEM] + [VMEM] * 4,
        out_specs=[VMEM] * 4,
        scratch_shapes=[pltpu.VMEM((2, 2 * NY * OWN, width), f32)],
        out_shape=(jax.ShapeDtypeStruct(piece, f32),) * 2 + (jax.ShapeDtypeStruct(piece, bf16),) * 2,
        compiler_params=pltpu.CompilerParams(vmem_limit_bytes=24 << 20),
        cost_estimate=pl.CostEstimate(
            flops=4 * rows * width * mine.shape[0], bytes_accessed=8 << 20, transcendentals=0
        ),
        name=name,
    )(place, mine, came, right, pack)


def halves(array):
    half = array.shape[0] // 2
    return array[:half], array[half:]


def meet(keep, send, step):
    came = swap(send, step)
    keep_own, keep_next = halves(keep)
    came_own, came_next = halves(came)
    return (
        keep_own.astype(f32) + came_own.astype(f32),
        (keep_next.astype(f32) + came_next.astype(f32)).astype(bf16),
    )


def total(keep, send, step):
    return keep.astype(f32) + swap(send, step).astype(f32)


def apart(array):
    half = array.shape[0] // 2
    return array[half:], array[:half]


def after(array, other):
    return lax.optimization_barrier((array, other))[0]


def sum_planes(down, up):
    plans = (("x1", "x2", "y1", "y2"), ("y1", "y2", "x1", "x2"))
    both = list(zip((down, up), plans))
    first = [(swap(chain[2], plan[0]), swap(chain[3], plan[0])) for chain, plan in both]
    sends = [(came.astype(f32) + chain[0]).astype(bf16) for (chain, _), (came, _) in zip(both, first)]
    second = [swap(send, plan[1]) for send, (_, plan) in zip(sends, both)]
    keeps = [
        apart(chain[1] + after(came, sends[1]).astype(f32)) for (chain, _), (_, came) in zip(both, first)
    ]
    keeps = [lax.optimization_barrier(keep) for keep in keeps]
    parts = [apart(came) for came in second]
    sends = [(part[0].astype(f32) + keep[0]).astype(bf16) for part, keep in zip(parts, keeps)]
    third = [swap(send, plan[2]) for send, (_, plan) in zip(sends, both)]
    sums = []
    for at, (_, plan) in enumerate(both):
        keep = after(third[at], sends[1]).astype(f32) + (keeps[at][1] + parts[at][1].astype(f32))
        sums.append(swap(keep[1:].astype(bf16), plan[3]).astype(f32) + keep[:1])
    return sums


def on_device(index_states, questions, reader, owners, passage_rows, w_up, w_down):
    shards = lax.axis_size("shard")
    width = questions.shape[1]
    shard, x = lax.axis_index("shard"), lax.axis_index("rep")
    z, y, c = shard >> 3, (shard >> 1) & 3, shard & 1
    place = jnp.stack([z, y, c, x]).astype(i32)

    send_rows, slot, index_near = route(owners.reshape(Q, K), passage_rows, index_states, shards)
    send_rows, place = lax.optimization_barrier((send_rows, place))
    rows_in = lax.all_to_all(send_rows, "shard", split_axis=0, concat_axis=0, tiled=True)
    states_out = fetch(rows_in, index_near)
    got = lax.all_to_all(states_out, "shard", split_axis=0, concat_axis=0, tiled=True)
    derivative, states, grad_emb, slope, hidden, pack, down = forward(
        place, got.reshape(shards * CAP, width), slot, questions, reader, turn(w_up), w_down
    )
    pack = swap(pack, "c")
    grad_pre, other = backward(place, grad_emb, slope, down)
    other = swap(other, "c")
    units = hidden.shape[0]
    down = gradient(place, hidden, pack, grad_emb, pack, units, True, "gradient_down")
    down, other = lax.optimization_barrier((down, other))
    up = gradient(place, grad_pre, other, states, pack, units + width, False, "gradient_up")
    both = jnp.concatenate(sum_planes(down, up))
    both = both.reshape(2, NZ, HALF_R, HALF_C).swapaxes(0, 1)
    keep, send = halves(both)
    send = send.astype(bf16)
    for step in ("z1", "z2"):
        keep, send = meet(keep, send, step)
    mine = total(keep, send, "z3")[0].astype(bf16)

    label = label4(x, c)
    came = swap(mine, "x2")
    first = (label & 1) == 0
    mine = jnp.concatenate([jnp.where(first, mine, came), jnp.where(first, came, mine)], 1)
    came = swap(mine, "x1")
    first = (label >> 1) == 0
    mine = jnp.concatenate([jnp.where(first, mine, came), jnp.where(first, came, mine)], 2)
    return derivative, mine[1].astype(f32), mine[0].astype(f32)


def solution(mesh):
    placed = (
        P("shard", None),
        P(("shard", "rep"), None),
        P(("shard", "rep"), None),
        P(("shard", "rep"), None, None),
        P(("shard", "rep"), None),
        P(),
        P(),
    )
    return jax.shard_map(
        on_device,
        mesh=mesh,
        in_specs=placed,
        out_specs=(P(("shard", "rep"), None), P("shard", None), P("shard", None)),
        check_vma=False,
    )
```

```python
import functools
import itertools

import jax
import jax.numpy as jnp
from jax import lax
from jax.experimental import pallas as pl
from jax.experimental.pallas import tpu as pltpu
from jax.sharding import PartitionSpec as P

K = 32
Q = 8
CAP = 8
NZ, NY, NC, NX = 8, 4, 2, 4
OWN = 48
CHUNK = NY * NC * OWN
HALF_R, HALF_C = 24, 384
WIDE = 2 * CHUNK

normalizer_heat = 0.1
loss_scale = 64.0
epsilon = 1e-06
gelu_coeff = 0.7978845608028654
cubic = 0.044715

bf16, f32, i32 = jnp.bfloat16, jnp.float32, jnp.int32
AXES = ("shard", "rep")


def gray(v):
    return v ^ (v >> 1)


def low_bit(v):
    return gray(v) & 1


def high_bit(v):
    return v >> 1


def label4(v, core):
    low, high = low_bit(v), high_bit(v)
    return (low * (1 - core) + high * core) * 2 + (high * (1 - core) + low * core)


def place4(label, core):
    first, second = label >> 1, label & 1
    low, high = first * (1 - core) + second * core, second * (1 - core) + first * core
    return high * 2 + (low ^ high)


def label8(v, core):
    v = (v - core) & 7
    top = v >> 2
    return (((v & 1) ^ top) << 2) | ((((v >> 1) & 1) ^ top) << 1) | top


def partner(step):
    def meet(z, y, c, x):
        if step == "c":
            return (z, y, 1 - c, x)
        axis, turn = step[0], int(step[1]) - 1
        if axis == "z":
            mine = label8(z, c)
            other = [v for v in range(NZ) if label8(v, c) == mine ^ (4 >> turn)][0]
            return (other, y, c, x)
        at = x if axis == "x" else y
        mine = label4(at, c)
        other = [v for v in range(4) if label4(v, c) == mine ^ (2 >> turn)][0]
        return (z, y, c, other) if axis == "x" else (z, other, c, x)

    pairs = []
    for at, place in enumerate(itertools.product(range(NZ), range(NY), range(NC), range(NX))):
        z, y, c, x = meet(*place)
        pairs.append((at, ((z * NY + y) * NC + c) * NX + x))
    return pairs


def swap(array, step):
    return lax.ppermute(array, AXES, partner(step))


def column(values):
    count, width = values.shape
    spread = jnp.broadcast_to(values[:, None, :], (count, width, width))
    mask = lax.broadcasted_iota(i32, spread.shape, 1) == lax.broadcasted_iota(i32, spread.shape, 2)
    return jnp.sum(jnp.where(mask, spread, 0.0).reshape(count * width, width), -1, keepdims=True)


def uncolumn(values, width):
    spread = jnp.broadcast_to(values, (values.shape[0], width)).reshape(-1, width, width)
    mask = lax.broadcasted_iota(i32, spread.shape, 1) == lax.broadcasted_iota(i32, spread.shape, 2)
    return jnp.sum(jnp.where(mask, spread, 0.0), 1)


def dot(left, right, dims):
    return lax.dot_general(left, right, ((dims[0], dims[1]), ((), ())), preferred_element_type=f32)


def route_kernel(owner_ref, row_ref, index_hbm, send_ref, slot_ref, index_ref, sem):
    load = pltpu.make_async_copy(index_hbm, index_ref, sem)
    load.start()
    rows = Q * K
    shards = send_ref.shape[0]
    owner = column(owner_ref[...].astype(f32))
    row = column(row_ref[...].astype(f32))
    lanes = lax.broadcasted_iota(i32, (rows, shards), 1).astype(f32)
    onehot = (lanes == owner).astype(f32)
    earlier = (
        lax.broadcasted_iota(i32, (rows, rows), 1) < lax.broadcasted_iota(i32, (rows, rows), 0)
    ).astype(bf16)
    hot = onehot.astype(bf16)
    prior = dot(earlier, hot, ((1,), (0,)))
    rank = jnp.sum(prior * onehot, -1, keepdims=True)
    high = jnp.floor(row * (1.0 / 32.0))
    low = row - 32.0 * high
    at = lax.broadcasted_iota(i32, (rows, 128), 1).astype(f32) == rank
    send_high = dot(hot, jnp.where(at, high, 0.0).astype(bf16), ((0,), (0,)))
    send_low = dot(hot, jnp.where(at, low, 0.0).astype(bf16), ((0,), (0,)))
    send_ref[:, 0, :] = (32.0 * send_high + send_low).astype(i32)
    slot_ref[...] = jnp.broadcast_to(owner * CAP + rank, slot_ref.shape).astype(i32)
    load.wait()


def fetch_kernel(rows_ref, index_ref, out_ref):
    shards, cap, width = out_ref.shape
    want = rows_ref[...].astype(f32)
    spread = jnp.broadcast_to(want, (shards, cap, want.shape[2]))
    mask = lax.broadcasted_iota(i32, spread.shape, 1) == lax.broadcasted_iota(i32, spread.shape, 2)
    at = jnp.sum(jnp.where(mask, spread, 0.0).reshape(shards * cap, -1), -1, keepdims=True)
    lanes = lax.broadcasted_iota(i32, (shards * cap, index_ref.shape[0]), 1).astype(f32)
    here = (lanes == at).astype(f32).astype(bf16)
    got = dot(here, index_ref[...], ((1,), (0,)))
    out_ref[...] = got.reshape(shards, cap, width).astype(bf16)


def turn_kernel(up_hbm, up_t_ref, up_ref, sems):
    parts = sems.shape[0]
    copies = []
    for t in range(parts):
        cut = pl.ds(t * WIDE, WIDE)
        copies.append(pltpu.make_async_copy(up_hbm.at[:, cut], up_ref.at[:, cut], sems.at[t]))
        copies[t].start()
    for t in range(parts):
        cut = slice(t * WIDE, (t + 1) * WIDE)
        copies[t].wait()
        up_t_ref[cut, :] = up_ref[:, cut].T


def share_units(units_ref, core, mine_ref, other_ref, t):
    for block in range(2 * t * NY, 2 * (t + 1) * NY):
        for own, out_ref in ((core, mine_ref), (1 - core, other_ref)):
            start = pl.multiple_of(block * NC * OWN + own * OWN, 16)
            out_ref[block * OWN : (block + 1) * OWN, :] = units_ref[pl.ds(start, OWN), :]


def forward_kernel(
    place_ref, got_ref, slot_ref, question_ref, reader_ref, up_t_hbm, down_hbm,
    derivative_ref, states_ref, grad_emb_ref, slope_ref, mine_ref, pack_ref, down_ref,
    hidden_ref, up_t_ref, sems,
):
    width = question_ref.shape[1]
    parts = hidden_ref.shape[0] // WIDE
    ups, downs = [], []
    for t in range(parts):
        cut = pl.ds(t * WIDE, WIDE)
        ups.append(pltpu.make_async_copy(up_t_hbm.at[cut, :], up_t_ref.at[cut, :], sems.at[0, t]))
        downs.append(pltpu.make_async_copy(down_hbm.at[cut, :], down_ref.at[cut, :], sems.at[1, t]))
    ups[0].start()
    ups[1].start()
    lanes = lax.broadcasted_iota(i32, (Q * K, got_ref.shape[0]), 1)
    onehot = (lanes == slot_ref[:, :1]).astype(f32).astype(bf16)
    states = dot(onehot, got_ref[...], ((1,), (0,))).astype(bf16)
    states_ref[...] = states
    for t in range(parts):
        cut = slice(t * WIDE, (t + 1) * WIDE)
        ups[t].wait()
        for copy in (ups + downs)[2 * t + 2 : 2 * t + 4]:
            copy.start()
        pre = dot(up_t_ref[cut, :], states, ((1,), (1,)))
        square = pre * pre
        tangent = jnp.tanh(pre * (gelu_coeff + (gelu_coeff * cubic) * square))
        gate = 0.5 + 0.5 * tangent
        hidden_ref[cut, :] = (pre * gate).astype(bf16)
        slope_ref[cut, :] = gate + pre * (1.0 - tangent * tangent) * (
            0.5 * gelu_coeff + (1.5 * gelu_coeff * cubic) * square
        )
        share_units(hidden_ref, place_ref[2], mine_ref, pack_ref, t)
    for copy in downs:
        copy.wait()
    embedded = states.astype(f32) + dot(hidden_ref[...], down_ref[...], ((0,), (0,)))

    norms = jnp.sqrt(jnp.sum(embedded * embedded, -1, keepdims=True) + epsilon)
    unit = embedded / norms
    wide = question_ref[...].astype(f32)
    q_hat = (wide / jnp.sqrt(jnp.sum(wide * wide, -1, keepdims=True) + epsilon)).astype(bf16)
    query = jnp.broadcast_to(q_hat.astype(f32)[:, None, :], (Q, K, width)).reshape(Q * K, width)
    cosine = jnp.sum(unit * query, -1, keepdims=True)

    def share(scores):
        raised = jnp.exp(scores).reshape(Q, K, 1)
        return (raised / jnp.sum(raised, 1, keepdims=True)).reshape(Q * K, 1)

    derivative = loss_scale * (share(cosine / normalizer_heat) - share(column(reader_ref[...])))
    derivative_ref[...] = uncolumn(derivative, K)
    grad_emb = ((derivative / normalizer_heat) * (query - cosine * unit) / norms).astype(bf16)
    grad_emb_ref[...] = grad_emb
    units = mine_ref.shape[0]
    for block, array in enumerate((grad_emb, states)):
        for part in range(width // (Q * K)):
            start = units + block * width + part * Q * K
            pack_ref[start : start + Q * K, :] = array[:, part * Q * K : (part + 1) * Q * K]


def backward_kernel(place_ref, grad_emb_ref, slope_ref, down_ref, mine_ref, other_ref, grad_pre_ref):
    grad_emb = grad_emb_ref[...]
    for t in range(down_ref.shape[0] // WIDE):
        cut = slice(t * WIDE, (t + 1) * WIDE)
        grad_hidden = dot(down_ref[cut, :], grad_emb, ((1,), (1,)))
        grad_pre_ref[cut, :] = (grad_hidden * slope_ref[cut, :]).astype(bf16)
        share_units(grad_pre_ref, place_ref[2], mine_ref, other_ref, t)


def gradient_kernel(
    x_first, right_at, place_ref, mine_ref, came_ref, right_ref, pack_ref,
    next_keep_ref, keep_ref, next_send_ref, send_ref, value_ref,
):
    z, y, core, x = place_ref[0], place_ref[1], place_ref[2], place_ref[3]
    mine_x, mine_y, mine_z = label4(x, core), label4(y, core), label8(z, core)
    right = right_ref[...]
    rows, width = right.shape
    right_came = jnp.concatenate(
        [pack_ref[right_at + part * rows : right_at + (part + 1) * rows, :] for part in range(width // rows)], 1
    )
    outs = (keep_ref, next_keep_ref, send_ref, next_send_ref)
    per = 2 * NY * OWN
    spots = []
    for at in range(NX * NY):
        at_x, at_y = (at >> 2, at & 3) if x_first else (at & 3, at >> 2)
        piece, j = at_x ^ mine_x, place4(at_y ^ mine_y, core)
        spots.append((j * OWN + (piece & 1) * HALF_R, pl.multiple_of((piece >> 1) * HALF_C, 128)))
    for t in range(NZ // 2):
        cut = slice(t * per, (t + 1) * per)
        value_ref[t % 2] = dot(mine_ref[cut, :], right, ((1,), (0,))) + dot(
            came_ref[cut, :], right_came, ((1,), (0,))
        )
        for half in range(2):
            at_z = label8(2 * t + half, core) ^ mine_z
            for at, (row, column) in enumerate(spots):
                row = pl.multiple_of(half * NY * OWN + row, 8)
                out_ref = outs[at >> 2]
                out_ref[at & 3, at_z] = value_ref[
                    t % 2, pl.ds(row, HALF_R), pl.ds(column, HALF_C)
                ].astype(out_ref.dtype)


def far(array):
    return pltpu.with_memory_space_constraint(array, pltpu.HBM)


SMEM, VMEM, HBM = (
    pl.BlockSpec(memory_space=pltpu.SMEM),
    pl.BlockSpec(memory_space=pltpu.VMEM),
    pl.BlockSpec(memory_space=pltpu.HBM),
)


def route(owners, passage_rows, index_states, shards):
    return pl.pallas_call(
        route_kernel,
        in_specs=[VMEM, VMEM, HBM],
        out_specs=[VMEM] * 3,
        out_shape=(
            jax.ShapeDtypeStruct((shards, 1, 128), i32),
            jax.ShapeDtypeStruct((Q * K, 128), i32),
            pltpu.VMEM(index_states.shape, index_states.dtype),
        ),
        scratch_shapes=[pltpu.SemaphoreType.DMA],
        compiler_params=pltpu.CompilerParams(vmem_limit_bytes=16 << 20),
        name="route",
    )(owners, passage_rows, far(index_states))


def fetch(rows_in, index_states):
    shards, width = rows_in.shape[0], index_states.shape[1]
    return pl.pallas_call(
        fetch_kernel,
        out_shape=jax.ShapeDtypeStruct((shards, CAP, width), bf16),
        compiler_params=pltpu.CompilerParams(vmem_limit_bytes=32 << 20),
        name="fetch",
    )(rows_in, pltpu.with_memory_space_constraint(index_states, pltpu.VMEM))


def near(array):
    return pltpu.with_memory_space_constraint(array, pltpu.VMEM)


def turn(w_up):
    width, hidden = w_up.shape
    return pl.pallas_call(
        turn_kernel,
        in_specs=[HBM],
        out_specs=VMEM,
        scratch_shapes=[pltpu.VMEM((width, hidden), bf16), pltpu.SemaphoreType.DMA((hidden // WIDE,))],
        out_shape=jax.ShapeDtypeStruct((hidden, width), bf16),
        compiler_params=pltpu.CompilerParams(vmem_limit_bytes=24 << 20),
        cost_estimate=pl.CostEstimate(flops=0, bytes_accessed=16 << 20, transcendentals=0),
        name="turn",
    )(far(w_up))


def forward(place, got, slot, questions, reader, up_t, w_down):
    hidden, width = up_t.shape
    rows = Q * K
    return pl.pallas_call(
        forward_kernel,
        in_specs=[SMEM, VMEM, VMEM, VMEM, VMEM, HBM, HBM],
        out_specs=[VMEM] * 7,
        scratch_shapes=[
            pltpu.VMEM((hidden, rows), bf16),
            pltpu.VMEM((hidden, width), bf16),
            pltpu.SemaphoreType.DMA((2, hidden // WIDE)),
        ],
        out_shape=(
            jax.ShapeDtypeStruct((Q, K), f32),
            jax.ShapeDtypeStruct((rows, width), bf16),
            jax.ShapeDtypeStruct((rows, width), bf16),
            jax.ShapeDtypeStruct((hidden, rows), f32),
            jax.ShapeDtypeStruct((hidden // NC, rows), bf16),
            jax.ShapeDtypeStruct((hidden // NC + 2 * width, rows), bf16),
            pltpu.VMEM((hidden, width), bf16),
        ),
        compiler_params=pltpu.CompilerParams(vmem_limit_bytes=24 << 20),
        cost_estimate=pl.CostEstimate(
            flops=4 * rows * width * hidden, bytes_accessed=16 << 20, transcendentals=rows * hidden
        ),
        name="forward",
    )(place, got, slot, questions, reader, far(up_t), far(w_down))


def backward(place, grad_emb, slope, w_down):
    hidden, width = w_down.shape
    rows = Q * K
    return pl.pallas_call(
        backward_kernel,
        in_specs=[SMEM] + [VMEM] * 3,
        out_specs=[VMEM] * 2,
        scratch_shapes=[pltpu.VMEM((hidden, rows), bf16)],
        out_shape=(jax.ShapeDtypeStruct((hidden // NC, rows), bf16),) * 2,
        compiler_params=pltpu.CompilerParams(vmem_limit_bytes=24 << 20),
        cost_estimate=pl.CostEstimate(
            flops=2 * rows * width * hidden, bytes_accessed=8 << 20, transcendentals=0
        ),
        name="backward",
    )(place, grad_emb, slope, near(w_down))


def gradient(place, mine, came, right, pack, right_at, x_first, name):
    rows, width = right.shape
    piece = (4, NZ, HALF_R, HALF_C)
    return pl.pallas_call(
        functools.partial(gradient_kernel, x_first, right_at),
        in_specs=[SMEM] + [VMEM] * 4,
        out_specs=[VMEM] * 4,
        scratch_shapes=[pltpu.VMEM((2, 2 * NY * OWN, width), f32)],
        out_shape=(jax.ShapeDtypeStruct(piece, f32),) * 2 + (jax.ShapeDtypeStruct(piece, bf16),) * 2,
        compiler_params=pltpu.CompilerParams(vmem_limit_bytes=24 << 20),
        cost_estimate=pl.CostEstimate(
            flops=4 * rows * width * mine.shape[0], bytes_accessed=8 << 20, transcendentals=0
        ),
        name=name,
    )(place, mine, came, right, pack)


def halves(array):
    half = array.shape[0] // 2
    return array[:half], array[half:]


def meet(keep, send, step):
    came = swap(send, step)
    keep_own, keep_next = halves(keep)
    came_own, came_next = halves(came)
    return (
        keep_own.astype(f32) + came_own.astype(f32),
        (keep_next.astype(f32) + came_next.astype(f32)).astype(bf16),
    )


def total(keep, send, step):
    return keep.astype(f32) + swap(send, step).astype(f32)


def apart(array):
    half = array.shape[0] // 2
    return array[half:], array[:half]


def after(array, other):
    return lax.optimization_barrier((array, other))[0]


def sum_planes(down, up):
    plans = (("x1", "x2", "y1", "y2"), ("y1", "y2", "x1", "x2"))
    both = list(zip((down, up), plans))
    first = [(swap(chain[2], plan[0]), swap(chain[3], plan[0])) for chain, plan in both]
    sends = [(came.astype(f32) + chain[0]).astype(bf16) for (chain, _), (came, _) in zip(both, first)]
    second = [swap(send, plan[1]) for send, (_, plan) in zip(sends, both)]
    keeps = [
        apart(chain[1] + after(came, sends[1]).astype(f32)) for (chain, _), (_, came) in zip(both, first)
    ]
    keeps = [lax.optimization_barrier(keep) for keep in keeps]
    parts = [apart(came) for came in second]
    sends = [(part[0].astype(f32) + keep[0]).astype(bf16) for part, keep in zip(parts, keeps)]
    third = [swap(send, plan[2]) for send, (_, plan) in zip(sends, both)]
    sums = []
    for at, (_, plan) in enumerate(both):
        keep = after(third[at], sends[1]).astype(f32) + (keeps[at][1] + parts[at][1].astype(f32))
        sums.append(swap(keep[1:].astype(bf16), plan[3]).astype(f32) + keep[:1])
    return sums


def on_device(index_states, questions, reader, owners, passage_rows, w_up, w_down):
    shards = lax.axis_size("shard")
    width = questions.shape[1]
    shard, x = lax.axis_index("shard"), lax.axis_index("rep")
    z, y, c = shard >> 3, (shard >> 1) & 3, shard & 1
    place = jnp.stack([z, y, c, x]).astype(i32)

    send_rows, slot, index_near = route(owners.reshape(Q, K), passage_rows, index_states, shards)
    send_rows, place = lax.optimization_barrier((send_rows, place))
    rows_in = lax.all_to_all(send_rows, "shard", split_axis=0, concat_axis=0, tiled=True)
    states_out = fetch(rows_in, index_near)
    got = lax.all_to_all(states_out, "shard", split_axis=0, concat_axis=0, tiled=True)
    derivative, states, grad_emb, slope, hidden, pack, down = forward(
        place, got.reshape(shards * CAP, width), slot, questions, reader, turn(w_up), w_down
    )
    pack = swap(pack, "c")
    grad_pre, other = backward(place, grad_emb, slope, down)
    other = swap(other, "c")
    units = hidden.shape[0]
    down = gradient(place, hidden, pack, grad_emb, pack, units, True, "gradient_down")
    down, other = lax.optimization_barrier((down, other))
    up = gradient(place, grad_pre, other, states, pack, units + width, False, "gradient_up")
    both = jnp.concatenate(sum_planes(down, up))
    both = both.reshape(2, NZ, HALF_R, HALF_C).swapaxes(0, 1)
    keep, send = halves(both)
    send = send.astype(bf16)
    for step in ("z1", "z2"):
        keep, send = meet(keep, send, step)
    mine = total(keep, send, "z3")[0].astype(bf16)

    label = label4(x, c)
    came = swap(mine, "x2")
    first = (label & 1) == 0
    mine = jnp.concatenate([jnp.where(first, mine, came), jnp.where(first, came, mine)], 1)
    came = swap(mine, "x1")
    first = (label >> 1) == 0
    mine = jnp.concatenate([jnp.where(first, mine, came), jnp.where(first, came, mine)], 2)
    return derivative, mine[1].astype(f32), mine[0].astype(f32)


def solution(mesh):
    placed = (
        P("shard", None),
        P(("shard", "rep"), None),
        P(("shard", "rep"), None),
        P(("shard", "rep"), None, None),
        P(("shard", "rep"), None),
        P(),
        P(),
    )
    return jax.shard_map(
        on_device,
        mesh=mesh,
        in_specs=placed,
        out_specs=(P(("shard", "rep"), None), P("shard", None), P("shard", None)),
        check_vma=False,
    )
```

```python
import functools
import itertools

import jax
import jax.numpy as jnp
from jax import lax
from jax.experimental import pallas as pl
from jax.experimental.pallas import tpu as pltpu
from jax.sharding import PartitionSpec as P

K = 32
Q = 8
CAP = 8
NZ, NY, NC, NX = 8, 4, 2, 4
OWN = 48
CHUNK = NY * NC * OWN
HALF_R, HALF_C = 24, 384
WIDE = 2 * CHUNK

normalizer_heat = 0.1
loss_scale = 64.0
epsilon = 1e-06
gelu_coeff = 0.7978845608028654
cubic = 0.044715

bf16, f32, i32 = jnp.bfloat16, jnp.float32, jnp.int32
AXES = ("shard", "rep")


def gray(v):
    return v ^ (v >> 1)


def low_bit(v):
    return gray(v) & 1


def high_bit(v):
    return v >> 1


def label4(v, core):
    low, high = low_bit(v), high_bit(v)
    return (low * (1 - core) + high * core) * 2 + (high * (1 - core) + low * core)


def place4(label, core):
    first, second = label >> 1, label & 1
    low, high = first * (1 - core) + second * core, second * (1 - core) + first * core
    return high * 2 + (low ^ high)


def label8(v, core):
    v = (v - core) & 7
    top = v >> 2
    return (((v & 1) ^ top) << 2) | ((((v >> 1) & 1) ^ top) << 1) | top


def partner(step):
    def meet(z, y, c, x):
        if step == "c":
            return (z, y, 1 - c, x)
        axis, turn = step[0], int(step[1]) - 1
        if axis == "z":
            mine = label8(z, c)
            other = [v for v in range(NZ) if label8(v, c) == mine ^ (4 >> turn)][0]
            return (other, y, c, x)
        at = x if axis == "x" else y
        mine = label4(at, c)
        other = [v for v in range(4) if label4(v, c) == mine ^ (2 >> turn)][0]
        return (z, y, c, other) if axis == "x" else (z, other, c, x)

    pairs = []
    for at, place in enumerate(itertools.product(range(NZ), range(NY), range(NC), range(NX))):
        z, y, c, x = meet(*place)
        pairs.append((at, ((z * NY + y) * NC + c) * NX + x))
    return pairs


def swap(array, step):
    return lax.ppermute(array, AXES, partner(step))


def column(values):
    count, width = values.shape
    spread = jnp.broadcast_to(values[:, None, :], (count, width, width))
    mask = lax.broadcasted_iota(i32, spread.shape, 1) == lax.broadcasted_iota(i32, spread.shape, 2)
    return jnp.sum(jnp.where(mask, spread, 0.0).reshape(count * width, width), -1, keepdims=True)


def uncolumn(values, width):
    spread = jnp.broadcast_to(values, (values.shape[0], width)).reshape(-1, width, width)
    mask = lax.broadcasted_iota(i32, spread.shape, 1) == lax.broadcasted_iota(i32, spread.shape, 2)
    return jnp.sum(jnp.where(mask, spread, 0.0), 1)


def dot(left, right, dims):
    return lax.dot_general(left, right, ((dims[0], dims[1]), ((), ())), preferred_element_type=f32)


def route_kernel(owner_ref, row_ref, index_hbm, send_ref, slot_ref, index_ref, sem):
    load = pltpu.make_async_copy(index_hbm, index_ref, sem)
    load.start()
    rows = Q * K
    shards = send_ref.shape[0]
    owner = column(owner_ref[...].astype(f32))
    row = column(row_ref[...].astype(f32))
    lanes = lax.broadcasted_iota(i32, (rows, shards), 1).astype(f32)
    onehot = (lanes == owner).astype(f32)
    earlier = (
        lax.broadcasted_iota(i32, (rows, rows), 1) < lax.broadcasted_iota(i32, (rows, rows), 0)
    ).astype(bf16)
    hot = onehot.astype(bf16)
    prior = dot(earlier, hot, ((1,), (0,)))
    rank = jnp.sum(prior * onehot, -1, keepdims=True)
    high = jnp.floor(row * (1.0 / 32.0))
    low = row - 32.0 * high
    at = lax.broadcasted_iota(i32, (rows, 128), 1).astype(f32) == rank
    send_high = dot(hot, jnp.where(at, high, 0.0).astype(bf16), ((0,), (0,)))
    send_low = dot(hot, jnp.where(at, low, 0.0).astype(bf16), ((0,), (0,)))
    send_ref[:, 0, :] = (32.0 * send_high + send_low).astype(i32)
    slot_ref[...] = jnp.broadcast_to(owner * CAP + rank, slot_ref.shape).astype(i32)
    load.wait()


def fetch_kernel(rows_ref, index_ref, out_ref):
    shards, cap, width = out_ref.shape
    want = rows_ref[...].astype(f32)
    spread = jnp.broadcast_to(want, (shards, cap, want.shape[2]))
    mask = lax.broadcasted_iota(i32, spread.shape, 1) == lax.broadcasted_iota(i32, spread.shape, 2)
    at = jnp.sum(jnp.where(mask, spread, 0.0).reshape(shards * cap, -1), -1, keepdims=True)
    lanes = lax.broadcasted_iota(i32, (shards * cap, index_ref.shape[0]), 1).astype(f32)
    here = (lanes == at).astype(f32).astype(bf16)
    got = dot(here, index_ref[...], ((1,), (0,)))
    out_ref[...] = got.reshape(shards, cap, width).astype(bf16)


def turn_kernel(up_hbm, first_ref, rest_ref, up_ref, sems):
    parts = sems.shape[0]
    copies = []
    for t in range(parts):
        cut = pl.ds(t * WIDE, WIDE)
        copies.append(pltpu.make_async_copy(up_hbm.at[:, cut], up_ref.at[:, cut], sems.at[t]))
        copies[t].start()
    for t in range(parts):
        cut = slice(t * WIDE, (t + 1) * WIDE)
        copies[t].wait()
        if t:
            rest_ref[(t - 1) * WIDE : t * WIDE, :] = up_ref[:, cut].T
        else:
            first_ref[...] = up_ref[:, cut].T


def share_units(units_ref, core, mine_ref, other_ref, t):
    for block in range(2 * t * NY, 2 * (t + 1) * NY):
        for own, out_ref in ((core, mine_ref), (1 - core, other_ref)):
            start = pl.multiple_of(block * NC * OWN + own * OWN, 16)
            out_ref[block * OWN : (block + 1) * OWN, :] = units_ref[pl.ds(start, OWN), :]


def forward_kernel(
    place_ref, got_ref, slot_ref, question_ref, reader_ref, first_ref, rest_hbm, down_hbm,
    derivative_ref, states_ref, grad_emb_ref, slope_ref, mine_ref, pack_ref, down_ref,
    hidden_ref, rest_ref, sems,
):
    width = question_ref.shape[1]
    parts = hidden_ref.shape[0] // WIDE
    ups, downs = [], []
    for t in range(parts):
        cut = pl.ds(t * WIDE, WIDE)
        if t < parts - 1:
            ups.append(pltpu.make_async_copy(rest_hbm.at[cut, :], rest_ref.at[cut, :], sems.at[0, t]))
        downs.append(pltpu.make_async_copy(down_hbm.at[cut, :], down_ref.at[cut, :], sems.at[1, t]))
    copies = ups + downs
    copies[0].start()
    copies[1].start()
    lanes = lax.broadcasted_iota(i32, (Q * K, got_ref.shape[0]), 1)
    onehot = (lanes == slot_ref[:, :1]).astype(f32).astype(bf16)
    states = dot(onehot, got_ref[...], ((1,), (0,))).astype(bf16)
    states_ref[...] = states
    for t in range(parts):
        cut = slice(t * WIDE, (t + 1) * WIDE)
        for copy in copies[2 * t + 2 : 2 * t + 4]:
            copy.start()
        if t:
            ups[t - 1].wait()
        wide_up = rest_ref[(t - 1) * WIDE : t * WIDE, :] if t else first_ref[...]
        pre = dot(wide_up, states, ((1,), (1,)))
        square = pre * pre
        tangent = jnp.tanh(pre * (gelu_coeff + (gelu_coeff * cubic) * square))
        gate = 0.5 + 0.5 * tangent
        hidden_ref[cut, :] = (pre * gate).astype(bf16)
        slope_ref[cut, :] = gate + pre * (1.0 - tangent * tangent) * (
            0.5 * gelu_coeff + (1.5 * gelu_coeff * cubic) * square
        )
        share_units(hidden_ref, place_ref[2], mine_ref, pack_ref, t)
    for copy in downs:
        copy.wait()
    embedded = states.astype(f32) + dot(hidden_ref[...], down_ref[...], ((0,), (0,)))

    norms = jnp.sqrt(jnp.sum(embedded * embedded, -1, keepdims=True) + epsilon)
    unit = embedded / norms
    wide = question_ref[...].astype(f32)
    q_hat = (wide / jnp.sqrt(jnp.sum(wide * wide, -1, keepdims=True) + epsilon)).astype(bf16)
    query = jnp.broadcast_to(q_hat.astype(f32)[:, None, :], (Q, K, width)).reshape(Q * K, width)
    cosine = jnp.sum(unit * query, -1, keepdims=True)

    def share(scores):
        raised = jnp.exp(scores).reshape(Q, K, 1)
        return (raised / jnp.sum(raised, 1, keepdims=True)).reshape(Q * K, 1)

    derivative = loss_scale * (share(cosine / normalizer_heat) - share(column(reader_ref[...])))
    derivative_ref[...] = uncolumn(derivative, K)
    grad_emb = ((derivative / normalizer_heat) * (query - cosine * unit) / norms).astype(bf16)
    grad_emb_ref[...] = grad_emb
    units = mine_ref.shape[0]
    for block, array in enumerate((grad_emb, states)):
        for part in range(width // (Q * K)):
            start = units + block * width + part * Q * K
            pack_ref[start : start + Q * K, :] = array[:, part * Q * K : (part + 1) * Q * K]


def backward_kernel(place_ref, grad_emb_ref, slope_ref, down_ref, mine_ref, other_ref, grad_pre_ref):
    grad_emb = grad_emb_ref[...]
    for t in range(down_ref.shape[0] // WIDE):
        cut = slice(t * WIDE, (t + 1) * WIDE)
        grad_hidden = dot(down_ref[cut, :], grad_emb, ((1,), (1,)))
        grad_pre_ref[cut, :] = (grad_hidden * slope_ref[cut, :]).astype(bf16)
        share_units(grad_pre_ref, place_ref[2], mine_ref, other_ref, t)


def gradient_kernel(
    x_first, right_at, place_ref, mine_ref, came_ref, right_ref, pack_ref,
    next_keep_ref, keep_ref, next_send_ref, send_ref, value_ref,
):
    z, y, core, x = place_ref[0], place_ref[1], place_ref[2], place_ref[3]
    mine_x, mine_y, mine_z = label4(x, core), label4(y, core), label8(z, core)
    right = right_ref[...]
    rows, width = right.shape
    right_came = jnp.concatenate(
        [pack_ref[right_at + part * rows : right_at + (part + 1) * rows, :] for part in range(width // rows)], 1
    )
    outs = (keep_ref, next_keep_ref, send_ref, next_send_ref)
    per = 2 * NY * OWN
    spots = []
    for at in range(NX * NY):
        at_x, at_y = (at >> 2, at & 3) if x_first else (at & 3, at >> 2)
        piece, j = at_x ^ mine_x, place4(at_y ^ mine_y, core)
        spots.append((j * OWN + (piece & 1) * HALF_R, pl.multiple_of((piece >> 1) * HALF_C, 128)))
    for t in range(NZ // 2):
        cut = slice(t * per, (t + 1) * per)
        value_ref[t % 2] = dot(mine_ref[cut, :], right, ((1,), (0,))) + dot(
            came_ref[cut, :], right_came, ((1,), (0,))
        )
        for half in range(2):
            at_z = label8(2 * t + half, core) ^ mine_z
            for at, (row, column) in enumerate(spots):
                row = pl.multiple_of(half * NY * OWN + row, 8)
                out_ref = outs[at >> 2]
                out_ref[at & 3, at_z] = value_ref[
                    t % 2, pl.ds(row, HALF_R), pl.ds(column, HALF_C)
                ].astype(out_ref.dtype)


def far(array):
    return pltpu.with_memory_space_constraint(array, pltpu.HBM)


SMEM, VMEM, HBM = (
    pl.BlockSpec(memory_space=pltpu.SMEM),
    pl.BlockSpec(memory_space=pltpu.VMEM),
    pl.BlockSpec(memory_space=pltpu.HBM),
)


def route(owners, passage_rows, index_states, shards):
    return pl.pallas_call(
        route_kernel,
        in_specs=[VMEM, VMEM, HBM],
        out_specs=[VMEM] * 3,
        out_shape=(
            jax.ShapeDtypeStruct((shards, 1, 128), i32),
            jax.ShapeDtypeStruct((Q * K, 128), i32),
            pltpu.VMEM(index_states.shape, index_states.dtype),
        ),
        scratch_shapes=[pltpu.SemaphoreType.DMA],
        compiler_params=pltpu.CompilerParams(vmem_limit_bytes=16 << 20),
        name="route",
    )(far(owners), far(passage_rows), far(index_states))


def fetch(rows_in, index_states):
    shards, width = rows_in.shape[0], index_states.shape[1]
    return pl.pallas_call(
        fetch_kernel,
        out_shape=jax.ShapeDtypeStruct((shards, CAP, width), bf16),
        compiler_params=pltpu.CompilerParams(vmem_limit_bytes=32 << 20),
        name="fetch",
    )(rows_in, pltpu.with_memory_space_constraint(index_states, pltpu.VMEM))


def near(array):
    return pltpu.with_memory_space_constraint(array, pltpu.VMEM)


def turn(w_up):
    width, hidden = w_up.shape
    return pl.pallas_call(
        turn_kernel,
        in_specs=[HBM],
        out_specs=[VMEM] * 2,
        scratch_shapes=[pltpu.VMEM((width, hidden), bf16), pltpu.SemaphoreType.DMA((hidden // WIDE,))],
        out_shape=(
            pltpu.VMEM((WIDE, width), bf16),
            jax.ShapeDtypeStruct((hidden - WIDE, width), bf16),
        ),
        compiler_params=pltpu.CompilerParams(vmem_limit_bytes=24 << 20),
        cost_estimate=pl.CostEstimate(flops=0, bytes_accessed=16 << 20, transcendentals=0),
        name="turn",
    )(far(w_up))


def forward(place, got, slot, questions, reader, first, rest, w_down):
    hidden, width = w_down.shape
    rows = Q * K
    return pl.pallas_call(
        forward_kernel,
        in_specs=[SMEM] + [VMEM] * 5 + [HBM] * 2,
        out_specs=[VMEM] * 7,
        scratch_shapes=[
            pltpu.VMEM((hidden, rows), bf16),
            pltpu.VMEM((hidden - WIDE, width), bf16),
            pltpu.SemaphoreType.DMA((2, hidden // WIDE)),
        ],
        out_shape=(
            jax.ShapeDtypeStruct((Q, K), f32),
            jax.ShapeDtypeStruct((rows, width), bf16),
            jax.ShapeDtypeStruct((rows, width), bf16),
            jax.ShapeDtypeStruct((hidden, rows), f32),
            jax.ShapeDtypeStruct((hidden // NC, rows), bf16),
            jax.ShapeDtypeStruct((hidden // NC + 2 * width, rows), bf16),
            pltpu.VMEM((hidden, width), bf16),
        ),
        compiler_params=pltpu.CompilerParams(vmem_limit_bytes=24 << 20),
        cost_estimate=pl.CostEstimate(
            flops=4 * rows * width * hidden, bytes_accessed=16 << 20, transcendentals=rows * hidden
        ),
        name="forward",
    )(place, got, slot, questions, reader, near(first), far(rest), far(w_down))


def backward(place, grad_emb, slope, w_down):
    hidden, width = w_down.shape
    rows = Q * K
    return pl.pallas_call(
        backward_kernel,
        in_specs=[SMEM] + [VMEM] * 3,
        out_specs=[VMEM] * 2,
        scratch_shapes=[pltpu.VMEM((hidden, rows), bf16)],
        out_shape=(jax.ShapeDtypeStruct((hidden // NC, rows), bf16),) * 2,
        compiler_params=pltpu.CompilerParams(vmem_limit_bytes=24 << 20),
        cost_estimate=pl.CostEstimate(
            flops=2 * rows * width * hidden, bytes_accessed=8 << 20, transcendentals=0
        ),
        name="backward",
    )(place, grad_emb, slope, near(w_down))


def gradient(place, mine, came, right, pack, right_at, x_first, name):
    rows, width = right.shape
    piece = (4, NZ, HALF_R, HALF_C)
    return pl.pallas_call(
        functools.partial(gradient_kernel, x_first, right_at),
        in_specs=[SMEM] + [VMEM] * 4,
        out_specs=[VMEM] * 4,
        scratch_shapes=[pltpu.VMEM((2, 2 * NY * OWN, width), f32)],
        out_shape=(jax.ShapeDtypeStruct(piece, f32),) * 2 + (jax.ShapeDtypeStruct(piece, bf16),) * 2,
        compiler_params=pltpu.CompilerParams(vmem_limit_bytes=24 << 20),
        cost_estimate=pl.CostEstimate(
            flops=4 * rows * width * mine.shape[0], bytes_accessed=8 << 20, transcendentals=0
        ),
        name=name,
    )(place, mine, came, right, pack)


def halves(array):
    half = array.shape[0] // 2
    return array[:half], array[half:]


def meet(keep, send, step):
    came = swap(send, step)
    keep_own, keep_next = halves(keep)
    came_own, came_next = halves(came)
    return (
        keep_own.astype(f32) + came_own.astype(f32),
        (keep_next.astype(f32) + came_next.astype(f32)).astype(bf16),
    )


def total(keep, send, step):
    return keep.astype(f32) + swap(send, step).astype(f32)


def apart(array):
    half = array.shape[0] // 2
    return array[half:], array[:half]


def after(array, other):
    return lax.optimization_barrier((array, other))[0]


def sum_planes(down, up):
    plans = (("x1", "x2", "y1", "y2"), ("y1", "y2", "x1", "x2"))
    both = list(zip((down, up), plans))
    first = [(swap(chain[2], plan[0]), swap(chain[3], plan[0])) for chain, plan in both]
    sends = [(came.astype(f32) + chain[0]).astype(bf16) for (chain, _), (came, _) in zip(both, first)]
    second = [swap(send, plan[1]) for send, (_, plan) in zip(sends, both)]
    keeps = [
        apart(chain[1] + after(came, sends[1]).astype(f32)) for (chain, _), (_, came) in zip(both, first)
    ]
    keeps = [lax.optimization_barrier(keep) for keep in keeps]
    parts = [apart(came) for came in second]
    sends = [(part[0].astype(f32) + keep[0]).astype(bf16) for part, keep in zip(parts, keeps)]
    third = [swap(send, plan[2]) for send, (_, plan) in zip(sends, both)]
    sums = []
    for at, (_, plan) in enumerate(both):
        keep = after(third[at], sends[1]).astype(f32) + (keeps[at][1] + parts[at][1].astype(f32))
        sums.append(swap(keep[1:].astype(bf16), plan[3]).astype(f32) + keep[:1])
    return sums


def on_device(index_states, questions, reader, owners, passage_rows, w_up, w_down):
    shards = lax.axis_size("shard")
    width = questions.shape[1]
    shard, x = lax.axis_index("shard"), lax.axis_index("rep")
    z, y, c = shard >> 3, (shard >> 1) & 3, shard & 1
    place = jnp.stack([z, y, c, x]).astype(i32)

    send_rows, slot, index_near = route(owners.reshape(Q, K), passage_rows, index_states, shards)
    send_rows, place = lax.optimization_barrier((send_rows, place))
    rows_in = lax.all_to_all(send_rows, "shard", split_axis=0, concat_axis=0, tiled=True)
    states_out = fetch(rows_in, index_near)
    got = lax.all_to_all(states_out, "shard", split_axis=0, concat_axis=0, tiled=True)
    derivative, states, grad_emb, slope, hidden, pack, down = forward(
        place, got.reshape(shards * CAP, width), slot, questions, reader, *turn(w_up), w_down
    )
    pack = swap(pack, "c")
    grad_pre, other = backward(place, grad_emb, slope, down)
    other = swap(other, "c")
    units = hidden.shape[0]
    down = gradient(place, hidden, pack, grad_emb, pack, units, True, "gradient_down")
    down, other = lax.optimization_barrier((down, other))
    up = gradient(place, grad_pre, other, states, pack, units + width, False, "gradient_up")
    both = jnp.concatenate(sum_planes(down, up))
    both = both.reshape(2, NZ, HALF_R, HALF_C).swapaxes(0, 1)
    keep, send = halves(both)
    send = send.astype(bf16)
    for step in ("z1", "z2"):
        keep, send = meet(keep, send, step)
    mine = total(keep, send, "z3")[0].astype(bf16)

    label = label4(x, c)
    came = swap(mine, "x2")
    first = (label & 1) == 0
    mine = jnp.concatenate([jnp.where(first, mine, came), jnp.where(first, came, mine)], 1)
    came = swap(mine, "x1")
    first = (label >> 1) == 0
    mine = jnp.concatenate([jnp.where(first, mine, came), jnp.where(first, came, mine)], 2)
    return derivative, mine[1].astype(f32), mine[0].astype(f32)


def solution(mesh):
    placed = (
        P("shard", None),
        P(("shard", "rep"), None),
        P(("shard", "rep"), None),
        P(("shard", "rep"), None, None),
        P(("shard", "rep"), None),
        P(),
        P(),
    )
    return jax.shard_map(
        on_device,
        mesh=mesh,
        in_specs=placed,
        out_specs=(P(("shard", "rep"), None), P("shard", None), P("shard", None)),
        check_vma=False,
    )
```

```python
import functools
import itertools

import jax
import jax.numpy as jnp
from jax import lax
from jax.experimental import pallas as pl
from jax.experimental.pallas import tpu as pltpu
from jax.sharding import PartitionSpec as P

K = 32
Q = 8
CAP = 8
NZ, NY, NC, NX = 8, 4, 2, 4
OWN = 48
CHUNK = NY * NC * OWN
HALF_R, HALF_C = 24, 384
WIDE = 2 * CHUNK

normalizer_heat = 0.1
loss_scale = 64.0
epsilon = 1e-06
gelu_coeff = 0.7978845608028654
cubic = 0.044715

bf16, f32, i32 = jnp.bfloat16, jnp.float32, jnp.int32
AXES = ("shard", "rep")


def gray(v):
    return v ^ (v >> 1)


def low_bit(v):
    return gray(v) & 1


def high_bit(v):
    return v >> 1


def label4(v, core):
    low, high = low_bit(v), high_bit(v)
    return (low * (1 - core) + high * core) * 2 + (high * (1 - core) + low * core)


def place4(label, core):
    first, second = label >> 1, label & 1
    low, high = first * (1 - core) + second * core, second * (1 - core) + first * core
    return high * 2 + (low ^ high)


def label8(v, core):
    v = (v - core) & 7
    top = v >> 2
    return (((v & 1) ^ top) << 2) | ((((v >> 1) & 1) ^ top) << 1) | top


def partner(step):
    def meet(z, y, c, x):
        if step == "c":
            return (z, y, 1 - c, x)
        axis, turn = step[0], int(step[1]) - 1
        if axis == "z":
            mine = label8(z, c)
            other = [v for v in range(NZ) if label8(v, c) == mine ^ (4 >> turn)][0]
            return (other, y, c, x)
        at = x if axis == "x" else y
        mine = label4(at, c)
        other = [v for v in range(4) if label4(v, c) == mine ^ (2 >> turn)][0]
        return (z, y, c, other) if axis == "x" else (z, other, c, x)

    pairs = []
    for at, place in enumerate(itertools.product(range(NZ), range(NY), range(NC), range(NX))):
        z, y, c, x = meet(*place)
        pairs.append((at, ((z * NY + y) * NC + c) * NX + x))
    return pairs


def swap(array, step):
    return lax.ppermute(array, AXES, partner(step))


def column(values):
    count, width = values.shape
    spread = jnp.broadcast_to(values[:, None, :], (count, width, width))
    mask = lax.broadcasted_iota(i32, spread.shape, 1) == lax.broadcasted_iota(i32, spread.shape, 2)
    return jnp.sum(jnp.where(mask, spread, 0.0).reshape(count * width, width), -1, keepdims=True)


def uncolumn(values, width):
    spread = jnp.broadcast_to(values, (values.shape[0], width)).reshape(-1, width, width)
    mask = lax.broadcasted_iota(i32, spread.shape, 1) == lax.broadcasted_iota(i32, spread.shape, 2)
    return jnp.sum(jnp.where(mask, spread, 0.0), 1)


def dot(left, right, dims):
    return lax.dot_general(left, right, ((dims[0], dims[1]), ((), ())), preferred_element_type=f32)


def route_kernel(owner_ref, row_ref, index_hbm, send_ref, slot_ref, index_ref, sem):
    load = pltpu.make_async_copy(index_hbm.at[pl.ds(0, index_ref.shape[0]), :], index_ref, sem)
    load.start()
    rows = Q * K
    shards = send_ref.shape[0]
    owner = column(owner_ref[...].astype(f32))
    row = column(row_ref[...].astype(f32))
    lanes = lax.broadcasted_iota(i32, (rows, shards), 1).astype(f32)
    onehot = (lanes == owner).astype(f32)
    earlier = (
        lax.broadcasted_iota(i32, (rows, rows), 1) < lax.broadcasted_iota(i32, (rows, rows), 0)
    ).astype(bf16)
    hot = onehot.astype(bf16)
    prior = dot(earlier, hot, ((1,), (0,)))
    rank = jnp.sum(prior * onehot, -1, keepdims=True)
    high = jnp.floor(row * (1.0 / 32.0))
    low = row - 32.0 * high
    at = lax.broadcasted_iota(i32, (rows, 128), 1).astype(f32) == rank
    send_high = dot(hot, jnp.where(at, high, 0.0).astype(bf16), ((0,), (0,)))
    send_low = dot(hot, jnp.where(at, low, 0.0).astype(bf16), ((0,), (0,)))
    send_ref[:, 0, :] = (32.0 * send_high + send_low).astype(i32)
    slot_ref[...] = jnp.broadcast_to(owner * CAP + rank, slot_ref.shape).astype(i32)
    load.wait()


def fetch_kernel(rows_ref, index_ref, index_hbm, out_ref, rest_ref, sem):
    half = index_ref.shape[0]
    load = pltpu.make_async_copy(index_hbm.at[pl.ds(half, half), :], rest_ref, sem)
    load.start()
    shards, cap, width = out_ref.shape
    want = rows_ref[...].astype(f32)
    spread = jnp.broadcast_to(want, (shards, cap, want.shape[2]))
    mask = lax.broadcasted_iota(i32, spread.shape, 1) == lax.broadcasted_iota(i32, spread.shape, 2)
    at = jnp.sum(jnp.where(mask, spread, 0.0).reshape(shards * cap, -1), -1, keepdims=True)
    lanes = lax.broadcasted_iota(i32, (shards * cap, half), 1).astype(f32)
    here = (lanes == at).astype(f32).astype(bf16)
    there = (lanes + half == at).astype(f32).astype(bf16)
    got = dot(here, index_ref[...], ((1,), (0,)))
    load.wait()
    got = got + dot(there, rest_ref[...], ((1,), (0,)))
    out_ref[...] = got.reshape(shards, cap, width).astype(bf16)


def turn_kernel(up_hbm, first_ref, rest_ref, up_ref, sems):
    parts = sems.shape[0]
    copies = []
    for t in range(parts):
        cut = pl.ds(t * WIDE, WIDE)
        copies.append(pltpu.make_async_copy(up_hbm.at[:, cut], up_ref.at[:, cut], sems.at[t]))
        copies[t].start()
    for t in range(parts):
        cut = slice(t * WIDE, (t + 1) * WIDE)
        copies[t].wait()
        if t:
            rest_ref[(t - 1) * WIDE : t * WIDE, :] = up_ref[:, cut].T
        else:
            first_ref[...] = up_ref[:, cut].T


def share_units(units_ref, core, mine_ref, other_ref, t):
    for block in range(2 * t * NY, 2 * (t + 1) * NY):
        for own, out_ref in ((core, mine_ref), (1 - core, other_ref)):
            start = pl.multiple_of(block * NC * OWN + own * OWN, 16)
            out_ref[block * OWN : (block + 1) * OWN, :] = units_ref[pl.ds(start, OWN), :]


def forward_kernel(
    place_ref, got_ref, slot_ref, question_ref, reader_ref, first_ref, rest_hbm, down_hbm,
    derivative_ref, states_ref, grad_emb_ref, slope_ref, mine_ref, pack_ref, down_ref,
    hidden_ref, rest_ref, sems,
):
    width = question_ref.shape[1]
    parts = hidden_ref.shape[0] // WIDE
    ups, downs = [], []
    for t in range(parts):
        cut = pl.ds(t * WIDE, WIDE)
        if t < parts - 1:
            ups.append(pltpu.make_async_copy(rest_hbm.at[cut, :], rest_ref.at[cut, :], sems.at[0, t]))
        downs.append(pltpu.make_async_copy(down_hbm.at[cut, :], down_ref.at[cut, :], sems.at[1, t]))
    copies = ups + downs
    copies[0].start()
    copies[1].start()
    lanes = lax.broadcasted_iota(i32, (Q * K, got_ref.shape[0]), 1)
    onehot = (lanes == slot_ref[:, :1]).astype(f32).astype(bf16)
    states = dot(onehot, got_ref[...], ((1,), (0,))).astype(bf16)
    states_ref[...] = states
    for t in range(parts):
        cut = slice(t * WIDE, (t + 1) * WIDE)
        for copy in copies[2 * t + 2 : 2 * t + 4]:
            copy.start()
        if t:
            ups[t - 1].wait()
        wide_up = rest_ref[(t - 1) * WIDE : t * WIDE, :] if t else first_ref[...]
        pre = dot(wide_up, states, ((1,), (1,)))
        square = pre * pre
        tangent = jnp.tanh(pre * (gelu_coeff + (gelu_coeff * cubic) * square))
        gate = 0.5 + 0.5 * tangent
        hidden_ref[cut, :] = (pre * gate).astype(bf16)
        slope_ref[cut, :] = gate + pre * (1.0 - tangent * tangent) * (
            0.5 * gelu_coeff + (1.5 * gelu_coeff * cubic) * square
        )
        share_units(hidden_ref, place_ref[2], mine_ref, pack_ref, t)
    for copy in downs:
        copy.wait()
    embedded = states.astype(f32) + dot(hidden_ref[...], down_ref[...], ((0,), (0,)))

    norms = jnp.sqrt(jnp.sum(embedded * embedded, -1, keepdims=True) + epsilon)
    scale = 1.0 / norms
    unit = embedded * scale
    wide = question_ref[...].astype(f32)
    q_hat = (wide / jnp.sqrt(jnp.sum(wide * wide, -1, keepdims=True) + epsilon)).astype(bf16)
    query = jnp.broadcast_to(q_hat.astype(f32)[:, None, :], (Q, K, width)).reshape(Q * K, width)
    cosine = jnp.sum(unit * query, -1, keepdims=True)

    def share(scores):
        raised = jnp.exp(scores).reshape(Q, K, 1)
        return (raised / jnp.sum(raised, 1, keepdims=True)).reshape(Q * K, 1)

    derivative = loss_scale * (share(cosine / normalizer_heat) - share(column(reader_ref[...])))
    derivative_ref[...] = uncolumn(derivative, K)
    grad_emb = ((derivative / normalizer_heat) * scale * (query - cosine * unit)).astype(bf16)
    grad_emb_ref[...] = grad_emb
    units = mine_ref.shape[0]
    for block, array in enumerate((grad_emb, states)):
        for part in range(width // (Q * K)):
            start = units + block * width + part * Q * K
            pack_ref[start : start + Q * K, :] = array[:, part * Q * K : (part + 1) * Q * K]


def backward_kernel(place_ref, grad_emb_ref, slope_ref, down_ref, mine_ref, other_ref, grad_pre_ref):
    grad_emb = grad_emb_ref[...]
    for t in range(down_ref.shape[0] // WIDE):
        cut = slice(t * WIDE, (t + 1) * WIDE)
        grad_hidden = dot(down_ref[cut, :], grad_emb, ((1,), (1,)))
        grad_pre_ref[cut, :] = (grad_hidden * slope_ref[cut, :]).astype(bf16)
        share_units(grad_pre_ref, place_ref[2], mine_ref, other_ref, t)


def gradient_kernel(
    x_first, right_at, place_ref, mine_ref, came_ref, right_ref, pack_ref,
    next_keep_ref, keep_ref, next_send_ref, send_ref, value_ref,
):
    z, y, core, x = place_ref[0], place_ref[1], place_ref[2], place_ref[3]
    mine_x, mine_y, mine_z = label4(x, core), label4(y, core), label8(z, core)
    right = right_ref[...]
    rows, width = right.shape
    right_came = jnp.concatenate(
        [pack_ref[right_at + part * rows : right_at + (part + 1) * rows, :] for part in range(width // rows)], 1
    )
    outs = (keep_ref, next_keep_ref, send_ref, next_send_ref)
    per = 2 * NY * OWN
    spots = []
    for at in range(NX * NY):
        at_x, at_y = (at >> 2, at & 3) if x_first else (at & 3, at >> 2)
        piece, j = at_x ^ mine_x, place4(at_y ^ mine_y, core)
        spots.append((j * OWN + (piece & 1) * HALF_R, pl.multiple_of((piece >> 1) * HALF_C, 128)))
    for t in range(NZ // 2):
        cut = slice(t * per, (t + 1) * per)
        value_ref[t % 2] = dot(mine_ref[cut, :], right, ((1,), (0,))) + dot(
            came_ref[cut, :], right_came, ((1,), (0,))
        )
        for half in range(2):
            at_z = label8(2 * t + half, core) ^ mine_z
            for at, (row, column) in enumerate(spots):
                row = pl.multiple_of(half * NY * OWN + row, 8)
                out_ref = outs[at >> 2]
                out_ref[at & 3, at_z] = value_ref[
                    t % 2, pl.ds(row, HALF_R), pl.ds(column, HALF_C)
                ].astype(out_ref.dtype)


def far(array):
    return pltpu.with_memory_space_constraint(array, pltpu.HBM)


SMEM, VMEM, HBM = (
    pl.BlockSpec(memory_space=pltpu.SMEM),
    pl.BlockSpec(memory_space=pltpu.VMEM),
    pl.BlockSpec(memory_space=pltpu.HBM),
)


def route(owners, passage_rows, index_states, shards):
    return pl.pallas_call(
        route_kernel,
        in_specs=[VMEM, VMEM, HBM],
        out_specs=[VMEM] * 3,
        out_shape=(
            jax.ShapeDtypeStruct((shards, 1, 128), i32),
            jax.ShapeDtypeStruct((Q * K, 128), i32),
            pltpu.VMEM((index_states.shape[0] // 2, index_states.shape[1]), index_states.dtype),
        ),
        scratch_shapes=[pltpu.SemaphoreType.DMA],
        compiler_params=pltpu.CompilerParams(vmem_limit_bytes=16 << 20),
        name="route",
    )(far(owners), far(passage_rows), far(index_states))


def fetch(rows_in, first_half, index_states):
    shards, (half, width) = rows_in.shape[0], first_half.shape
    return pl.pallas_call(
        fetch_kernel,
        in_specs=[VMEM, VMEM, HBM],
        out_specs=VMEM,
        scratch_shapes=[pltpu.VMEM((half, width), bf16), pltpu.SemaphoreType.DMA],
        out_shape=jax.ShapeDtypeStruct((shards, CAP, width), bf16),
        compiler_params=pltpu.CompilerParams(vmem_limit_bytes=32 << 20),
        name="fetch",
    )(rows_in, near(first_half), far(index_states))


def near(array):
    return pltpu.with_memory_space_constraint(array, pltpu.VMEM)


def turn(w_up):
    width, hidden = w_up.shape
    return pl.pallas_call(
        turn_kernel,
        in_specs=[HBM],
        out_specs=[VMEM] * 2,
        scratch_shapes=[pltpu.VMEM((width, hidden), bf16), pltpu.SemaphoreType.DMA((hidden // WIDE,))],
        out_shape=(
            pltpu.VMEM((WIDE, width), bf16),
            jax.ShapeDtypeStruct((hidden - WIDE, width), bf16),
        ),
        compiler_params=pltpu.CompilerParams(vmem_limit_bytes=24 << 20),
        cost_estimate=pl.CostEstimate(flops=0, bytes_accessed=16 << 20, transcendentals=0),
        name="turn",
    )(far(w_up))


def forward(place, got, slot, questions, reader, first, rest, w_down):
    hidden, width = w_down.shape
    rows = Q * K
    return pl.pallas_call(
        forward_kernel,
        in_specs=[SMEM] + [VMEM] * 5 + [HBM] * 2,
        out_specs=[VMEM] * 7,
        scratch_shapes=[
            pltpu.VMEM((hidden, rows), bf16),
            pltpu.VMEM((hidden - WIDE, width), bf16),
            pltpu.SemaphoreType.DMA((2, hidden // WIDE)),
        ],
        out_shape=(
            jax.ShapeDtypeStruct((Q, K), f32),
            jax.ShapeDtypeStruct((rows, width), bf16),
            jax.ShapeDtypeStruct((rows, width), bf16),
            jax.ShapeDtypeStruct((hidden, rows), f32),
            jax.ShapeDtypeStruct((hidden // NC, rows), bf16),
            jax.ShapeDtypeStruct((hidden // NC + 2 * width, rows), bf16),
            pltpu.VMEM((hidden, width), bf16),
        ),
        compiler_params=pltpu.CompilerParams(vmem_limit_bytes=24 << 20),
        cost_estimate=pl.CostEstimate(
            flops=4 * rows * width * hidden, bytes_accessed=16 << 20, transcendentals=rows * hidden
        ),
        name="forward",
    )(place, got, slot, questions, reader, near(first), far(rest), far(w_down))


def backward(place, grad_emb, slope, w_down):
    hidden, width = w_down.shape
    rows = Q * K
    return pl.pallas_call(
        backward_kernel,
        in_specs=[SMEM] + [VMEM] * 3,
        out_specs=[VMEM] * 2,
        scratch_shapes=[pltpu.VMEM((hidden, rows), bf16)],
        out_shape=(jax.ShapeDtypeStruct((hidden // NC, rows), bf16),) * 2,
        compiler_params=pltpu.CompilerParams(vmem_limit_bytes=24 << 20),
        cost_estimate=pl.CostEstimate(
            flops=2 * rows * width * hidden, bytes_accessed=8 << 20, transcendentals=0
        ),
        name="backward",
    )(place, grad_emb, slope, near(w_down))


def gradient(place, mine, came, right, pack, right_at, x_first, name):
    rows, width = right.shape
    piece = (4, NZ, HALF_R, HALF_C)
    return pl.pallas_call(
        functools.partial(gradient_kernel, x_first, right_at),
        in_specs=[SMEM] + [VMEM] * 4,
        out_specs=[VMEM] * 4,
        scratch_shapes=[pltpu.VMEM((2, 2 * NY * OWN, width), f32)],
        out_shape=(jax.ShapeDtypeStruct(piece, f32),) * 2 + (jax.ShapeDtypeStruct(piece, bf16),) * 2,
        compiler_params=pltpu.CompilerParams(vmem_limit_bytes=24 << 20),
        cost_estimate=pl.CostEstimate(
            flops=4 * rows * width * mine.shape[0], bytes_accessed=8 << 20, transcendentals=0
        ),
        name=name,
    )(place, mine, came, right, pack)


def halves(array):
    half = array.shape[0] // 2
    return array[:half], array[half:]


def meet(keep, send, step):
    came = swap(send, step)
    keep_own, keep_next = halves(keep)
    came_own, came_next = halves(came)
    return (
        keep_own.astype(f32) + came_own.astype(f32),
        (keep_next.astype(f32) + came_next.astype(f32)).astype(bf16),
    )


def total(keep, send, step):
    return keep.astype(f32) + swap(send, step).astype(f32)


def apart(array):
    half = array.shape[0] // 2
    return array[half:], array[:half]


def after(array, other):
    return lax.optimization_barrier((array, other))[0]


def sum_planes(down, up):
    plans = (("x1", "x2", "y1", "y2"), ("y1", "y2", "x1", "x2"))
    both = list(zip((down, up), plans))
    first = [(swap(chain[2], plan[0]), swap(chain[3], plan[0])) for chain, plan in both]
    sends = [(came.astype(f32) + chain[0]).astype(bf16) for (chain, _), (came, _) in zip(both, first)]
    second = [swap(send, plan[1]) for send, (_, plan) in zip(sends, both)]
    keeps = [
        apart(chain[1] + after(came, sends[1]).astype(f32)) for (chain, _), (_, came) in zip(both, first)
    ]
    keeps = [lax.optimization_barrier(keep) for keep in keeps]
    parts = [apart(came) for came in second]
    sends = [(part[0].astype(f32) + keep[0]).astype(bf16) for part, keep in zip(parts, keeps)]
    third = [swap(send, plan[2]) for send, (_, plan) in zip(sends, both)]
    sums = []
    for at, (_, plan) in enumerate(both):
        keep = after(third[at], sends[1]).astype(f32) + (keeps[at][1] + parts[at][1].astype(f32))
        sums.append(swap(keep[1:].astype(bf16), plan[3]).astype(f32) + keep[:1])
    return sums


def on_device(index_states, questions, reader, owners, passage_rows, w_up, w_down):
    shards = lax.axis_size("shard")
    width = questions.shape[1]
    shard, x = lax.axis_index("shard"), lax.axis_index("rep")
    z, y, c = shard >> 3, (shard >> 1) & 3, shard & 1
    place = jnp.stack([z, y, c, x]).astype(i32)

    send_rows, slot, index_near = route(owners.reshape(Q, K), passage_rows, index_states, shards)
    send_rows, place = lax.optimization_barrier((send_rows, place))
    rows_in = lax.all_to_all(send_rows, "shard", split_axis=0, concat_axis=0, tiled=True)
    states_out = fetch(rows_in, index_near, index_states)
    got = lax.all_to_all(states_out, "shard", split_axis=0, concat_axis=0, tiled=True)
    derivative, states, grad_emb, slope, hidden, pack, down = forward(
        place, got.reshape(shards * CAP, width), slot, questions, reader, *turn(w_up), w_down
    )
    pack = swap(pack, "c")
    grad_pre, other = backward(place, grad_emb, slope, down)
    other = swap(other, "c")
    units = hidden.shape[0]
    down = gradient(place, hidden, pack, grad_emb, pack, units, True, "gradient_down")
    down, other = lax.optimization_barrier((down, other))
    up = gradient(place, grad_pre, other, states, pack, units + width, False, "gradient_up")
    both = jnp.concatenate(sum_planes(down, up))
    both = both.reshape(2, NZ, HALF_R, HALF_C).swapaxes(0, 1)
    keep, send = halves(both)
    send = send.astype(bf16)
    for step in ("z1", "z2"):
        keep, send = meet(keep, send, step)
    mine = total(keep, send, "z3")[0].astype(bf16)

    label = label4(x, c)
    came = swap(mine, "x2")
    first = (label & 1) == 0
    mine = jnp.concatenate([jnp.where(first, mine, came), jnp.where(first, came, mine)], 1)
    came = swap(mine, "x1")
    first = (label >> 1) == 0
    mine = jnp.concatenate([jnp.where(first, mine, came), jnp.where(first, came, mine)], 2)
    return derivative, mine[1].astype(f32), mine[0].astype(f32)


def solution(mesh):
    placed = (
        P("shard", None),
        P(("shard", "rep"), None),
        P(("shard", "rep"), None),
        P(("shard", "rep"), None, None),
        P(("shard", "rep"), None),
        P(),
        P(),
    )
    return jax.shard_map(
        on_device,
        mesh=mesh,
        in_specs=placed,
        out_specs=(P(("shard", "rep"), None), P("shard", None), P("shard", None)),
        check_vma=False,
    )
```
